32 devices in a mesh: req: 8 (over z, y), seq: 4 (over x, core).
Axes of the slice: x: 2, y: 2, z: 4, core: 2. Of those that a mesh axis runs over, the one named last changes fastest.
Arguments:
- tokens: bfloat16 [8, 2048, 2560], P('req', 'seq'), may hold values from -6 to 6
- mix_weight: bfloat16 [2560, 2816], P(('req', 'seq')), may hold values from -0.125 to 0.125
- step_weight: bfloat16 [2560, 40], P(('req', 'seq')), may hold values from -0.125 to 0.125
- conv_weight: float32 [4, 2816], replicated, may hold values from -3 to 3
- conv_bias: float32 [2816], replicated, may hold values from -3 to 3
- step_bias: float32 [40], replicated, may hold values from -5 to -3
- decay_rate: float32 [40], replicated, may hold values from 0.0009765625 to 1
- skip_gain: float32 [40], replicated, may hold values from 0.5 to 2
- norm_gain: float32 [2560], replicated, may hold values from 0.1 to 1.9
- prompt_len: int32 [8], replicated, may hold values from 512 to 2048, as said below
- prompt_start: int32 [8], replicated, may hold values from 0 to 1536, as said below
- deal: int32 [8], replicated, may hold values from 0 to 7, as said below
Outputs:
- result: bfloat16 [8, 2048, 2560], P('req', 'seq')
- final_state: float32 [8, 40, 64, 128], P('req', 'seq')
The draws below stay inside these ranges and needn't reach their ends.
Inputs may be any that keep to these rules, and one draw needn't show every extreme that they name: `prompt_len`: one prompt has exactly 2048 positions and one exactly a quarter of 2048. prompt_start plus prompt_len is at most 2048 for every request. `deal`: a permutation of the requests; some slot s holds request (s + 4) modulo 8.
All inputs are finite; a program needn't handle non-finite values.
Results may differ from the reference program's by a relative error of at most 0.0035.
Values may be sent and summed in bfloat16 or wider, within the bound.
No kernel may reach another device: no remote copies, remote signals or barrier semaphores. Data moves between devices by JAX's collectives and lax.ppermute only.
A program may use at most 128 MiB of HBM per device.

```python
import math
import jax
import jax.numpy as jnp
from jax import lax

D = 2560
HEADS = 40
P_SIZE = 64
NSTATE = 128
CONV = 4
GROUP = 256
E = 2560
CONVCH = 2816
REQS = 8
MAXLEN = 2048


def joint_prompt(key):
    inner_key = jax.random.fold_in(key, 11)
    keys = jax.random.split(inner_key, 4)
    places = jnp.arange(REQS, dtype=jnp.int32)
    lengths = jax.random.randint(keys[0], (REQS,), MAXLEN // 4, MAXLEN + 1)
    longest = jax.random.randint(keys[1], (), 0, REQS)
    shortest = (longest + 1 + jax.random.randint(keys[2], (), 0, REQS - 1)) % REQS
    lengths = jnp.where(places == longest, MAXLEN, lengths)
    lengths = jnp.where(places == shortest, MAXLEN // 4, lengths)
    offsets = jax.random.randint(keys[3], (REQS,), 0, MAXLEN - lengths + 1)
    offsets = jnp.where(places == shortest, MAXLEN - MAXLEN // 4, offsets)
    return (lengths.astype(jnp.int32), offsets.astype(jnp.int32))


def draw_prompt_len(key, part):
    return joint_prompt(key)[0]


def draw_prompt_start(key, part):
    return joint_prompt(key)[1]


def draw_deal(key, part):
    inner_key = jax.random.fold_in(key, 23)
    keys = jax.random.split(inner_key, 2)
    places = jnp.arange(REQS, dtype=jnp.int32)
    order = jax.random.permutation(keys[0], REQS).astype(jnp.int32)
    chosen = jax.random.randint(keys[1], (), 0, REQS).astype(jnp.int32)
    target = (chosen + REQS // 2) % REQS
    holder = jnp.sum(jnp.where(order == target, places, 0))
    current = jnp.sum(jnp.where(places == chosen, order, 0))
    swapped = jnp.where(places == holder, current, order)
    swapped = jnp.where(places == chosen, target, swapped)
    return swapped.astype(jnp.int32)


def levels(rng, extent, cuts, smallest, largest):
    gain, own = 1.0, jax.random.fold_in(rng, 6)
    for position, blocks in cuts:
        draws = jnp.exp(jax.random.uniform(jax.random.fold_in(own, position), (blocks,), jnp.float32, smallest / len(cuts), largest / len(cuts)))
        gain = gain * jnp.repeat(draws, extent[position] // blocks).reshape([-1 if axis == position else 1 for axis in range(len(extent))])
    return gain


def centred(stream_key, extent, deviation, limit, shards=(), kind=jnp.bfloat16):
    values = deviation * jax.random.normal(stream_key, extent, jnp.float32)
    if shards:
        values = values * levels(stream_key, extent, shards, -0.22, 0.18)
    return jnp.clip(values, -limit, limit).astype(kind)


def setup_inputs(seed: int = 0) -> dict:
    seeds = jax.random.split(jax.random.key(seed), 13)
    return {
        "tokens": centred(seeds[0], (REQS, MAXLEN, D), 1.0, 6.0, ((0, 8), (1, 4))),
        "mix_weight": centred(seeds[1], (D, CONVCH), D ** -0.5, 0.125, ((0, 32),)),
        "step_weight": centred(seeds[2], (D, HEADS), D ** -0.5, 0.125, ((0, 32),)),
        "conv_weight": centred(seeds[3], (CONV, CONVCH), 0.5, 3.0, (), jnp.float32),
        "conv_bias": centred(seeds[4], (CONVCH,), 0.5, 3.0, (), jnp.float32),
        "step_bias": jnp.clip(jax.random.uniform(seeds[5], (HEADS,), jnp.float32, -5.0, -3.0), -5.0, -3.0),
        "decay_rate": jnp.clip(jnp.exp(jax.random.uniform(seeds[6], (HEADS,), jnp.float32, math.log(0.0009765625), math.log(1.0))), 0.0009765625, 1.0),
        "skip_gain": jnp.clip(jax.random.uniform(seeds[7], (HEADS,), jnp.float32, 0.5, 2.0), 0.5, 2.0),
        "norm_gain": jnp.clip(1.0 + 0.18 * jax.random.normal(seeds[8], (E,), jnp.float32), 0.1, 1.9),
        "prompt_len": draw_prompt_len(jax.random.fold_in(seeds[12], 71), 0),
        "prompt_start": draw_prompt_start(jax.random.fold_in(seeds[12], 71), 0),
        "deal": draw_deal(jax.random.fold_in(seeds[12], 71), 0),
    }


EPS = 1e-05

def group_step(state, block, decay_rate):
    part_in, part_b, part_c, part_step = block
    log_decay = -part_step * decay_rate[None, :]
    cum_decay = jnp.cumsum(log_decay, axis=0)
    count = part_in.shape[0]
    places = jnp.arange(count, dtype=jnp.int32)
    causal = places[:, None] >= places[None, :]
    spread = cum_decay[:, None, :] - cum_decay[None, :, :]
    spread = jnp.where(causal[:, :, None], spread, -1e+30)
    scores = jnp.dot(part_c, part_b.T, preferred_element_type=jnp.float32)
    mixing = (jnp.exp(spread) * scores[:, :, None] * part_step[None, :, :]).astype(jnp.bfloat16)
    inner_out = jnp.einsum('qkh,khp->qhp', mixing.astype(jnp.float32), part_in.astype(jnp.float32))
    carried = jnp.einsum('qn,hpn->qhp', part_c.astype(jnp.float32), state, precision=lax.Precision.HIGHEST)
    carried = carried * jnp.exp(cum_decay)[:, :, None]
    to_end = jnp.exp(cum_decay[-1][None, :] - cum_decay) * part_step
    scaled = (to_end[:, :, None] * part_in.astype(jnp.float32)).astype(jnp.bfloat16)
    local = jnp.einsum('khp,kn->hpn', scaled.astype(jnp.float32), part_b.astype(jnp.float32))
    new_state = jnp.exp(cum_decay[-1])[:, None, None] * state + local
    return (new_state, inner_out + carried)

def one_row(tokens_row, length, start, mix_weight, step_weight, conv_weight, conv_bias, step_bias, decay_rate, skip_gain, norm_gain):
    total = tokens_row.shape[0]
    place = jnp.arange(total, dtype=jnp.int32)
    valid = ((place >= start) & (place < start + length)).astype(jnp.float32)
    mixed = jnp.dot(tokens_row, mix_weight, preferred_element_type=jnp.float32)
    mixed = (mixed * valid[:, None]).astype(jnp.bfloat16)
    raw_step = jnp.dot(tokens_row, step_weight, preferred_element_type=jnp.float32)
    padded = jnp.concatenate([jnp.zeros((CONV - 1, CONVCH), jnp.bfloat16), mixed], axis=0)
    conv_sum = jnp.zeros((total, CONVCH), jnp.float32) + conv_bias[None, :]
    for offset in range(CONV):
        conv_sum = conv_sum + conv_weight[offset][None, :] * padded[offset:offset + total].astype(jnp.float32)
    convolved = jax.nn.silu(conv_sum).astype(jnp.bfloat16)
    inputs = convolved[:, :E].reshape(total, HEADS, P_SIZE)
    mixed_b = convolved[:, E:E + NSTATE]
    mixed_c = convolved[:, E + NSTATE:]
    step_size = jax.nn.softplus(raw_step + step_bias[None, :]) * valid[:, None]
    blocks = total // GROUP
    pieces = (inputs.reshape(blocks, GROUP, HEADS, P_SIZE), mixed_b.reshape(blocks, GROUP, NSTATE), mixed_c.reshape(blocks, GROUP, NSTATE), step_size.reshape(blocks, GROUP, HEADS))

    def advance(state, block):
        return group_step(state, block, decay_rate)
    final_state, outputs = lax.scan(advance, jnp.zeros((HEADS, P_SIZE, NSTATE), jnp.float32), pieces)
    outputs = outputs.reshape(total, HEADS, P_SIZE) + skip_gain[None, :, None] * inputs.astype(jnp.float32)
    flat = outputs.reshape(total, E)
    factor = lax.rsqrt(lax.optimization_barrier(jnp.mean(flat * flat, axis=1, keepdims=True)) + EPS)
    result = (flat * factor * norm_gain[None, :] * valid[:, None]).astype(jnp.bfloat16)
    return (result, final_state)

def reference(tokens, mix_weight, step_weight, conv_weight, conv_bias, step_bias, decay_rate, skip_gain, norm_gain, prompt_len, prompt_start, deal):
    slot_len = prompt_len[deal]
    slot_start = prompt_start[deal]

    def run(item):
        row, length, start = item
        return one_row(row, length, start, mix_weight, step_weight, conv_weight, conv_bias, step_bias, decay_rate, skip_gain, norm_gain)
    result, states = lax.map(run, (tokens, slot_len, slot_start))
    final_state = jnp.zeros_like(states).at[deal].set(states)
    return (result, final_state)
```

```python
import functools

import jax
import jax.numpy as jnp
from jax import lax
from jax.experimental import pallas as pl
from jax.experimental.pallas import tpu as pltpu
from jax.sharding import PartitionSpec as P

GROUP = 256
EPS = 1e-05
LOG2E = 1.4426950408889634
LANES = 128
HALO = 16
F32 = jnp.float32
BF16 = jnp.bfloat16
AXES = ("req", "seq")


def dot(a, b):
    return jnp.dot(a, b, preferred_element_type=F32)


def params(vmem_mib, side=False):
    return pltpu.CompilerParams(
        dimension_semantics=("arbitrary",), vmem_limit_bytes=vmem_mib * 1024 * 1024
    )


def valid_rows(first, rows, start, end):
    place = first + lax.broadcasted_iota(jnp.int32, (rows, LANES), 0)
    return jnp.where((place >= start) & (place < end), 1.0, 0.0).astype(F32)


def place_weights(ints, low, high, whole, sems):
    half = low.shape[0] // 160
    copies = []
    for p in range(2 * half):
        source = low if p < half else high
        row = pl.multiple_of(ints[8 + p] * 160, 160)
        copies.append(
            pltpu.make_async_copy(
                source.at[pl.ds((p % half) * 160, 160), :],
                whole.at[pl.ds(row, 160), :],
                sems.at[p],
            )
        )
    for copy in copies:
        copy.start()
    for copy in copies:
        copy.wait()


def fetch_tokens(ints, step, own, other, tokens):
    mine = (step // 2) == ints[3]

    @pl.when(mine)
    def _():
        tokens[...] = own[...]

    @pl.when(jnp.logical_not(mine))
    def _():
        tokens[...] = other[...]


def convolve(ints, step, acc_of, halo_of, spans, taps, padded):
    start, end, first = ints[0], ints[1], ints[2]

    @pl.when(step == 0)
    def _():
        edge = halo_of()
        ok = valid_rows(first - HALO, HALO, start, end)
        for at, lane in enumerate(spans):
            rounded = (edge[:, lane * LANES : (lane + 1) * LANES] * ok).astype(BF16).astype(F32)
            padded[at, 0:8, :] = rounded[HALO - 8 :, :]

    acc = acc_of()
    ok = valid_rows(first + step * GROUP, GROUP, start, end)
    out = []
    for at, lane in enumerate(spans):
        rounded = (acc[:, lane * LANES : (lane + 1) * LANES] * ok).astype(BF16).astype(F32)
        padded[at, 8 : 8 + GROUP, :] = rounded
        total = taps[4:5, at * LANES : (at + 1) * LANES]
        for k in range(4):
            total = total + taps[k : k + 1, at * LANES : (at + 1) * LANES] * padded[
                at, 5 + k : 5 + k + GROUP, :
            ]
        half = 0.5 * total
        out.append((half + half * jnp.tanh(half)).astype(BF16))
        padded[at, 0:8, :] = padded[at, GROUP : GROUP + 8, :]
    return acc, ok, out


def first_kernel(
    ints, own, other, halo, low, high, taps, rates,
    bc_out, x_out, cq_out, kq_out, kt_out, ca_out, tot_out,
    whole, tokens, padded, before, sems,
):
    step = pl.program_id(0)

    @pl.when(step == 0)
    def _():
        place_weights(ints, low, high, whole, sems)
        before[...] = jnp.zeros_like(before)

    fetch_tokens(ints, step, own, other, tokens)
    acc, ok, out = convolve(
        ints,
        step,
        lambda: dot(tokens[...], whole[...]),
        lambda: dot(halo[...], whole[...]),
        (0, 2, 3),
        taps,
        padded,
    )
    bc_out[...] = out[0]
    x_out[:, 0:LANES] = out[1]
    x_out[:, LANES : 2 * LANES] = out[2]
    raw = acc[:, LANES : 2 * LANES] + rates[0:1, :]
    size = (jnp.maximum(raw, 0.0) + jnp.log1p(jnp.exp(-jnp.abs(raw)))) * ok
    decay = size * rates[1:2, :]
    high_part = decay.astype(BF16)
    rest = decay - high_part.astype(F32)
    mid_part = rest.astype(BF16)
    low_part = (rest - mid_part.astype(F32)).astype(BF16)
    row = lax.broadcasted_iota(jnp.int32, (GROUP, GROUP), 0)
    col = lax.broadcasted_iota(jnp.int32, (GROUP, GROUP), 1)
    below = jnp.where(row >= col, 1.0, 0.0).astype(BF16)
    cum = dot(below, high_part) + dot(below, mid_part) + dot(below, low_part)
    from_key = jnp.log2(size) - cum
    cq_out[...] = cum
    kq_out[...] = from_key
    kt_out[0] = from_key.T[0:32, :]
    ca_out[...] = cum + before[0:1, :]
    before[...] = before[...] + jnp.broadcast_to(cum[GROUP - 1 : GROUP, :], before.shape)
    tot_out[...] = before[...]


def column(a, head):
    return jnp.broadcast_to(a[:, head : head + 1], (a.shape[0], LANES))


def split(a):
    upper = a.astype(BF16)
    return upper, (a - upper.astype(F32)).astype(BF16)


def scan_kernel(
    heads, extra, ints, own, other, halo, low, high, taps, x_ref, b_ref, c_ref, cq_ref, kq_ref,
    kt_ref, tot_ref, skip_ref, y_out, s_out, whole, tokens, padded, state, sems,
):
    step = pl.program_id(0)
    pairs = len(heads)

    @pl.when(step == 0)
    def _():
        place_weights(ints, low, high, whole, sems)
        state[...] = jnp.zeros_like(state)

    fetch_tokens(ints, step, own, other, tokens)
    _, _, out = convolve(
        ints,
        step,
        lambda: dot(tokens[...], whole[...]),
        lambda: dot(halo[...], whole[...]),
        tuple(range(pairs - extra)),
        taps,
        padded,
    )
    xs = [x_ref[:, i * LANES : (i + 1) * LANES] for i in range(extra)] + out
    b, c = b_ref[...], c_ref[...]
    scores = lax.dot_general(c, b, (((1,), (1,)), ((), ())), preferred_element_type=F32)
    half = GROUP // 2
    row = lax.broadcasted_iota(jnp.int32, (half, half), 0)
    col = lax.broadcasted_iota(jnp.int32, (half, half), 1)
    causal = row >= col
    left = lax.broadcasted_iota(jnp.int32, (GROUP, LANES), 1) < LANES // 2
    cq, kq, kt = cq_ref[...], kq_ref[...], kt_ref[0]
    upper, lower = split(state[...])
    carried = dot(jnp.concatenate([c, c], axis=1), jnp.concatenate([upper, lower], axis=0))
    zero = jnp.zeros((GROUP, LANES), BF16)
    scaled, ends = [], []
    for i, head in enumerate(heads):
        x = xs[i]
        top, bottom, spread = [], [], []
        for h in (head, head + 1):
            q = column(cq, h)
            spread.append(q)
            k0 = jnp.broadcast_to(kt[h : h + 1, 0:half], (half, half))
            k1 = jnp.broadcast_to(kt[h : h + 1, half:], (half, half))
            m00 = jnp.where(causal, jnp.exp2(q[0:half] + k0) * scores[0:half, 0:half], 0.0)
            m10 = jnp.exp2(q[half:] + k0) * scores[half:, 0:half]
            m11 = jnp.where(causal, jnp.exp2(q[half:] + k1) * scores[half:, half:], 0.0)
            top.append(m00.astype(BF16))
            bottom.append(m10.astype(BF16))
            bottom.append(m11.astype(BF16))
        x0, x1 = jnp.where(left, x, zero), jnp.where(left, zero, x)
        y_top = dot(jnp.concatenate(top, axis=1), jnp.concatenate([x0[0:half], x1[0:half]], axis=0))
        y_bottom = dot(jnp.concatenate(bottom, axis=1), jnp.concatenate([x0, x1], axis=0))
        q = jnp.where(left, spread[0], spread[1])
        lanes = slice(i * LANES, (i + 1) * LANES)
        xf = x.astype(F32)
        rest = jnp.exp2(q) * carried[:, lanes] + skip_ref[0:1, lanes] * xf
        y_out[0:half, lanes] = y_top + rest[0:half]
        y_out[half:, lanes] = y_bottom + rest[half:]
        k = jnp.where(left, column(kq, head), column(kq, head + 1))
        end = q[GROUP - 1 : GROUP, :]
        scaled.append((jnp.exp2(k + end) * xf).astype(BF16))
        ends.append(jnp.exp2(end))
    local = lax.dot_general(
        b, jnp.concatenate(scaled, axis=1), (((0,), (0,)), ((), ())), preferred_element_type=F32
    )
    new = jnp.concatenate(ends, axis=1) * state[...] + local
    state[...] = new

    @pl.when(step == pl.num_programs(0) - 1)
    def _():
        s_out[0:LANES, :] = new
        whole_row = lax.broadcasted_iota(jnp.int32, (8, LANES), 1) < LANES // 2
        for i, head in enumerate(heads):
            t = tot_ref[...]
            s_out[LANES : LANES + 8, i * LANES : (i + 1) * LANES] = jnp.where(
                whole_row, column(t, head), column(t, head + 1)
            )


def join_kernel(heads, halves, ints, y_ref, c_ref, ca_ref, s_ref, r_ref, send_out, keep_out, fin_out):
    step = pl.program_id(0)
    later = ints[4] > 0
    left = lax.broadcasted_iota(jnp.int32, (GROUP, LANES), 1) < LANES // 2
    c, ca = c_ref[...], ca_ref[...]
    entering = r_ref[0:LANES, :] * jnp.where(later, 1.0, 0.0)
    upper, lower = split(entering)
    carried = dot(jnp.concatenate([c, c], axis=1), jnp.concatenate([upper, lower], axis=0))
    ys = []
    for i, head in enumerate(heads):
        lanes = slice(i * LANES, (i + 1) * LANES)
        q = jnp.where(left, column(ca, head), column(ca, head + 1))
        ys.append(y_ref[:, lanes] + jnp.exp2(q) * carried[:, lanes])

    @pl.when(step < 2)
    def _():
        for i in range(len(heads)):
            send_out[:, i * LANES : (i + 1) * LANES] = ys[i]

    @pl.when(step >= 2)
    def _():
        for i in range(len(heads)):
            keep_out[:, i * LANES : (i + 1) * LANES] = ys[i]

    @pl.when(step == 0)
    def _():
        for i, (early, late) in enumerate(halves):
            a = slice(early * LANES, (early + 1) * LANES)
            b = slice(late * LANES, (late + 1) * LANES)
            at_first = jnp.exp2(r_ref[LANES : LANES + 1, a]) * s_ref[0:LANES, a] + r_ref[0:LANES, a]
            at_last = jnp.exp2(s_ref[LANES : LANES + 1, b]) * r_ref[0:LANES, b] + s_ref[0:LANES, b]
            both = jnp.where(later, at_last, at_first)
            fin_out[i * LANES : (i + 1) * LANES, :] = both.T.astype(fin_out.dtype)


def norm_kernel(places, ints, gain_ref, ka_ref, kb_ref, ra_ref, rb_ref, out_ref):
    step = pl.program_id(0)
    core = ints[3]
    rows = out_ref.shape[0]
    first = ints[2] + core * (2 * GROUP) + step * rows
    ok = valid_rows(first, rows, ints[0], ints[1])
    blocks = []
    for who, refs in ((core, (ka_ref, kb_ref)), (1 - core, (ra_ref, rb_ref))):
        for ref, wheres in zip(refs, places, strict=True):
            for i, where in enumerate(wheres):
                at = pl.multiple_of((where + 5 * who) * LANES, LANES)
                blocks.append((at, ref, i))
    total = jnp.zeros((rows, LANES), F32)
    for _, ref, i in blocks:
        v = ref[:, i * LANES : (i + 1) * LANES]
        total = total + v * v
    mean = jnp.sum(total, axis=1, keepdims=True) * (1.0 / out_ref.shape[1])
    factor = lax.rsqrt(mean + EPS) * ok
    for at, ref, i in blocks:
        v = ref[:, i * LANES : (i + 1) * LANES]
        out_ref[:, pl.ds(at, LANES)] = (v * factor * gain_ref[0:1, pl.ds(at, LANES)]).astype(BF16)


def swapped(x, masks):
    count = lax.axis_size("req") * lax.axis_size("seq")
    return lax.ppermute(x, AXES, [(i, i ^ masks[i % 2]) for i in range(count)])


def spec(shape, index):
    return pl.BlockSpec(shape, index)


def fixed(shape):
    return pl.BlockSpec(shape, lambda i, ints: (0,) * len(shape))


def by_step(shape):
    return pl.BlockSpec(shape, lambda i, ints: (i,) + (0,) * (len(shape) - 1))


ANY = pl.BlockSpec(memory_space=pl.ANY)


def on_device(
    tokens, mix_weight, step_weight, conv_weight, conv_bias, step_bias, decay_rate, skip_gain,
    norm_gain, prompt_len, prompt_start, deal,
):
    seq_index = lax.axis_index("seq")
    req_index = lax.axis_index("req")
    core, along = seq_index % 2, seq_index // 2
    rows = tokens[0]
    span, depth = rows.shape
    inner = norm_gain.shape[0]
    heads = decay_rate.shape[0]
    head_dim = inner // heads
    nstate = (mix_weight.shape[1] - inner) // 2
    share = heads // 4
    quarter = inner // 4
    slots = jnp.arange(deal.shape[0], dtype=jnp.int32)
    request = jnp.sum(jnp.where(slots == req_index, deal, 0))
    length = jnp.sum(jnp.where(slots == request, prompt_len, 0))
    start = jnp.sum(jnp.where(slots == request, prompt_start, 0))
    chip = req_index * 2 + along

    def mine_of(a, b, who):
        bc = lax.dynamic_slice_in_dim(a, inner + nstate * who, nstate, 1)
        early = lax.dynamic_slice_in_dim(a, quarter * who, quarter, 1)
        late = lax.dynamic_slice_in_dim(a, 2 * quarter + quarter * who, quarter, 1)
        parts = [bc]
        if b is not None:
            parts += [steps_of(b, who)]
        for lo, hi in ((0, 1), (1, 3), (3, 5)):
            parts += [early[:, lo * LANES : hi * LANES], late[:, lo * LANES : hi * LANES]]
        return jnp.concatenate(parts, axis=1)

    def steps_of(b, who):
        one = lax.dynamic_slice_in_dim(b, share * who, share, 1)
        two = lax.dynamic_slice_in_dim(b, 2 * share + share * who, share, 1)
        return jnp.concatenate(
            [one, two, jnp.zeros((b.shape[0], LANES - 2 * share), b.dtype)], axis=1
        )

    kept = mine_of(mix_weight, step_weight, core)
    given = mine_of(mix_weight, step_weight, 1 - core)
    got = swapped(given, (1, 1))
    weights = jnp.where(
        core == 0, jnp.concatenate([kept, got], axis=0), jnp.concatenate([got, kept], axis=0)
    )
    other = swapped(rows, (1, 1))
    last_rows = jnp.where(core == 1, rows[span - HALO :], other[span - HALO :])
    count = lax.axis_size("req") * lax.axis_size("seq")
    halo = lax.ppermute(
        last_rows, AXES, [(i, i + 2) for i in range(count) if (i // 2) % 2 == 0]
    )

    masks = ((16, 16), (8, 8), (2, 4), (4, 2))
    order = []
    for p in range(16):
        rel = [0, 0]
        for s, mask in enumerate(masks):
            if (p >> s) & 1:
                rel = [rel[0] ^ (mask[0] // 2), rel[1] ^ (mask[1] // 2)]
        order.append(jnp.bitwise_xor(chip, jnp.where(core == 0, rel[0], rel[1])))

    def gathered(block):
        for mask in masks[:-1]:
            block = jnp.concatenate([block, swapped(block, mask)], axis=0)
        return block, swapped(block, masks[-1])

    width = weights.shape[1] // 3
    chunks = [gathered(weights[:, i * width : (i + 1) * width]) for i in range(3)]

    taps = mine_of(
        jnp.concatenate([conv_weight, conv_bias[None], jnp.zeros_like(conv_weight[:3])], axis=0),
        None,
        core,
    )
    rates = jnp.concatenate(
        [
            steps_of(step_bias[None], core),
            steps_of(decay_rate[None] * (-LOG2E), core),
            jnp.zeros((6, LANES), F32),
        ],
        axis=0,
    )
    skip_all = mine_of(
        jnp.concatenate([jnp.repeat(skip_gain, head_dim), jnp.zeros((2 * nstate,), F32)])[None],
        None,
        core,
    )
    skip = jnp.broadcast_to(skip_all[:, LANES:], (8, inner // 2))
    ints = jnp.stack(
        [start, start + length, along * 2 * span, core, along]
        + [jnp.zeros_like(core)] * 3
        + order
    ).astype(jnp.int32)

    chip_rows = 2 * span
    steps = chip_rows // GROUP
    per = span // GROUP

    def clamp(v):
        return jnp.clip(v, 0, per - 1)

    own_spec = pl.BlockSpec((GROUP, depth), lambda i, ints: (clamp(i - per * ints[3]), 0))
    other_spec = pl.BlockSpec(
        (GROUP, depth), lambda i, ints: (clamp(i - per * (1 - ints[3])), 0)
    )
    halo_spec = fixed((HALO, depth))

    def scratch(spans):
        return [
            pltpu.VMEM((depth, width), BF16),
            pltpu.VMEM((GROUP, depth), BF16),
            pltpu.VMEM((spans, GROUP + 8, LANES), F32),
        ]

    bc, x0, cq, kq, kt, ca, tot = pl.pallas_call(
        first_kernel,
        grid_spec=pltpu.PrefetchScalarGridSpec(
            num_scalar_prefetch=1,
            grid=(steps,),
            in_specs=[
                own_spec, other_spec, halo_spec, ANY, ANY, fixed((8, 3 * LANES)), fixed((8, LANES)),
            ],
            out_specs=[
                by_step((GROUP, LANES)),
                by_step((GROUP, 2 * LANES)),
                by_step((GROUP, LANES)),
                by_step((GROUP, LANES)),
                by_step((1, 32, GROUP)),
                by_step((GROUP, LANES)),
                fixed((8, LANES)),
            ],
            scratch_shapes=scratch(3)
            + [pltpu.VMEM((8, LANES), F32), pltpu.SemaphoreType.DMA((16,))],
        ),
        out_shape=[
            jax.ShapeDtypeStruct((chip_rows, LANES), BF16),
            jax.ShapeDtypeStruct((chip_rows, 2 * LANES), BF16),
            jax.ShapeDtypeStruct((chip_rows, LANES), F32),
            jax.ShapeDtypeStruct((chip_rows, LANES), F32),
            jax.ShapeDtypeStruct((steps, 32, GROUP), F32),
            jax.ShapeDtypeStruct((chip_rows, LANES), F32),
            jax.ShapeDtypeStruct((8, LANES), F32),
        ],
        compiler_params=params(40),
        cost_estimate=pl.CostEstimate(
            flops=2 * chip_rows * depth * width, bytes_accessed=9000000, transcendentals=500000
        ),
        name="first",
    )(ints, rows, other, halo, *chunks[0], taps[:, : 3 * LANES], rates)

    bc_other = swapped(bc, (1, 1))
    b = jnp.where(core == 0, bc, bc_other)
    c = jnp.where(core == 0, bc_other, bc)

    def pair_heads(lo, hi):
        return [2 * i for i in range(lo, hi)] + [share + 2 * i for i in range(lo, hi)]

    batches = (
        (pair_heads(0, 1) + pair_heads(1, 3), 2, ((0, 1), (2, 4), (3, 5)), 3 * LANES, 0),
        (pair_heads(3, 5), 0, ((0, 2), (1, 3)), 7 * LANES, 6 * LANES),
    )

    def scanned(batch, chunk):
        firsts, extra, _, tap_at, skip_at = batch
        pairs = len(firsts)
        new = pairs - extra
        return pl.pallas_call(
            functools.partial(scan_kernel, firsts, extra),
            grid_spec=pltpu.PrefetchScalarGridSpec(
                num_scalar_prefetch=1,
                grid=(steps,),
                in_specs=[
                    own_spec, other_spec, halo_spec, ANY, ANY, fixed((8, new * LANES)),
                    by_step((GROUP, 2 * LANES)), by_step((GROUP, LANES)), by_step((GROUP, LANES)),
                    by_step((GROUP, LANES)), by_step((GROUP, LANES)), by_step((1, 32, GROUP)),
                    fixed((8, LANES)), fixed((8, pairs * LANES)),
                ],
                out_specs=[
                    by_step((GROUP, pairs * LANES)),
                    fixed((LANES + 8, pairs * LANES)),
                ],
                scratch_shapes=scratch(new)
                + [pltpu.VMEM((LANES, pairs * LANES), F32), pltpu.SemaphoreType.DMA((16,))],
            ),
            out_shape=[
                jax.ShapeDtypeStruct((chip_rows, pairs * LANES), F32),
                jax.ShapeDtypeStruct((LANES + 8, pairs * LANES), F32),
            ],
            compiler_params=params(48),
            cost_estimate=pl.CostEstimate(
                flops=2 * chip_rows * depth * width + pairs * 600000000,
                bytes_accessed=12000000,
                transcendentals=pairs * 400000,
            ),
            name="scan",
        )(
            ints, rows, other, halo, *chunk, taps[:, tap_at : tap_at + new * LANES],
            x0, b, c, cq, kq, kt, tot, skip[:, skip_at : skip_at + pairs * LANES],
        )

    def turned(i, ints):
        return (i + 2 * (1 - ints[3])) % 4, 0

    def joined(batch, y, s, r):
        firsts, _, halves, _, _ = batch
        pairs = len(firsts)
        half_rows = chip_rows // 2
        return pl.pallas_call(
            functools.partial(join_kernel, firsts, halves),
            grid_spec=pltpu.PrefetchScalarGridSpec(
                num_scalar_prefetch=1,
                grid=(steps,),
                in_specs=[
                    pl.BlockSpec((GROUP, pairs * LANES), turned),
                    pl.BlockSpec((GROUP, LANES), turned),
                    pl.BlockSpec((GROUP, LANES), turned),
                    fixed((LANES + 8, pairs * LANES)),
                    fixed((LANES + 8, pairs * LANES)),
                ],
                out_specs=[
                    pl.BlockSpec((GROUP, pairs * LANES), lambda i, ints: (jnp.minimum(i, 1), 0)),
                    pl.BlockSpec((GROUP, pairs * LANES), lambda i, ints: (jnp.maximum(i - 2, 0), 0)),
                    fixed((len(halves) * LANES, nstate)),
                ],
            ),
            out_shape=[
                jax.ShapeDtypeStruct((half_rows, pairs * LANES), F32),
                jax.ShapeDtypeStruct((half_rows, pairs * LANES), F32),
                jax.ShapeDtypeStruct((len(halves) * LANES, nstate), BF16),
            ],
            compiler_params=params(32),
            cost_estimate=pl.CostEstimate(
                flops=4 * chip_rows * LANES * pairs * LANES,
                bytes_accessed=chip_rows * pairs * LANES * 8,
                transcendentals=chip_rows * pairs * LANES,
            ),
            name="join",
        )(ints, y, c, ca, s, r)

    wanted = jnp.sum(jnp.where(deal == req_index, slots, 0))
    partner_wanted = jnp.sum(jnp.where(deal == (req_index ^ 1), slots, 0))

    def delivered(block):
        one = swapped(block, (16, 16))
        pair = jnp.stack([block, one])
        two = swapped(pair, (8, 8))
        cand = jnp.concatenate([pair, two], axis=0)

        def pick(row):
            rel = row ^ req_index
            at = (rel >> 2) + 2 * ((rel >> 1) & 1)
            return lax.dynamic_index_in_dim(cand, at, 0, False), rel & 1

        sent, _ = pick(partner_wanted)
        three = swapped(sent, (4, 4))
        here, odd = pick(wanted)
        return jnp.where(odd == 1, three, here).astype(F32)

    kept_y, got_y, finals = [], [], []
    for batch, chunk in zip(batches, chunks[1:], strict=True):
        y, s = scanned(batch, chunk)
        r = swapped(s, (2, 2))
        send, keep, fin = joined(batch, y, s, r)
        got_y.append(swapped(send, (1, 1)))
        kept_y.append(keep)
        finals.append(delivered(fin))

    final_state = jnp.concatenate(finals, axis=0).reshape(1, share, head_dim, nstate)
    places = (
        [0, 10, 1, 2, 11, 12],
        [3, 4, 13, 14],
    )
    result = pl.pallas_call(
        functools.partial(norm_kernel, places),
        grid_spec=pltpu.PrefetchScalarGridSpec(
            num_scalar_prefetch=1,
            grid=(span // GROUP,),
            in_specs=[
                fixed((1, inner)),
                by_step((GROUP, 6 * LANES)),
                by_step((GROUP, 4 * LANES)),
                by_step((GROUP, 6 * LANES)),
                by_step((GROUP, 4 * LANES)),
            ],
            out_specs=by_step((GROUP, inner)),
        ),
        out_shape=jax.ShapeDtypeStruct((span, inner), BF16),
        compiler_params=params(32),
        cost_estimate=pl.CostEstimate(
            flops=6 * span * inner, bytes_accessed=6 * span * inner, transcendentals=span
        ),
        name="norm",
    )(ints, norm_gain[None], *kept_y, *got_y)
    return (result[None], final_state)


def passed_along(block, axis, distance):
    devices = range(lax.axis_size(axis))
    route = [(i - distance, i) for i in devices if i - distance in devices]
    return lax.ppermute(block, axis, route)


def carried_in(part, axis, combine, identity):
    place = lax.axis_index(axis)
    gathered = jax.tree.map(lambda a: lax.all_gather(a, axis), part)
    state = jax.tree.map(lambda a, e: jnp.zeros_like(a) + jnp.asarray(e, a.dtype), part, identity)

    def one(step, state):
        return combine(
            state, jax.tree.map(lambda a: lax.dynamic_index_in_dim(a, step, 0, False), gathered)
        )

    return lax.fori_loop(0, place, one, state)


def broadcast(x, axis, root):
    mine = lax.axis_index(axis) == root
    return lax.psum(jnp.where(mine, x, jnp.zeros_like(x)), axis)


def on_device_general(
    tokens,
    mix_weight,
    step_weight,
    conv_weight,
    conv_bias,
    step_bias,
    decay_rate,
    skip_gain,
    norm_gain,
    prompt_len,
    prompt_start,
    deal,
):
    seq_count = lax.axis_size("seq")
    seq_index = lax.axis_index("seq")
    req_index = lax.axis_index("req")
    rows = tokens[0]
    span = rows.shape[0]
    total_reqs = deal.shape[0]
    slots = jnp.arange(total_reqs, dtype=jnp.int32)
    request = jnp.sum(jnp.where(slots == req_index, deal, 0))
    length = jnp.sum(jnp.where(slots == request, prompt_len, 0))
    start = jnp.sum(jnp.where(slots == request, prompt_start, 0))
    place = seq_index * span + jnp.arange(span, dtype=jnp.int32)
    valid = ((place >= start) & (place < start + length)).astype(jnp.float32)
    whole_mix, whole_step = (
        lax.all_gather(mix_weight, ("req", "seq"), axis=0, tiled=True),
        lax.all_gather(step_weight, ("req", "seq"), axis=0, tiled=True),
    )
    mixed = jnp.dot(rows, whole_mix, preferred_element_type=jnp.float32)
    raw_step = jnp.dot(rows, whole_step, preferred_element_type=jnp.float32)
    mixed = (mixed * valid[:, None]).astype(jnp.bfloat16)
    taps = conv_weight.shape[0]
    edge = passed_along(mixed[span - (taps - 1) :], "seq", 1)
    padded = jnp.concatenate([edge, mixed], axis=0)
    conv_sum = jnp.zeros(mixed.shape, jnp.float32) + conv_bias[None, :]
    for offset in range(taps):
        conv_sum = conv_sum + conv_weight[offset][None, :] * padded[offset : offset + span].astype(
            jnp.float32
        )
    convolved = jax.nn.silu(conv_sum).astype(jnp.bfloat16)
    heads = decay_rate.shape[0]
    inner = norm_gain.shape[0]
    head_dim = inner // heads
    nstate = (mixed.shape[1] - inner) // 2
    blocks = span // GROUP
    inputs = convolved[:, :inner].reshape(span, heads, head_dim)
    mixed_b = convolved[:, inner : inner + nstate]
    mixed_c = convolved[:, inner + nstate :]
    step_size = jax.nn.softplus(raw_step + step_bias[None, :]) * valid[:, None]
    pieces = (
        inputs.reshape(blocks, GROUP, heads, head_dim),
        mixed_b.reshape(blocks, GROUP, nstate),
        mixed_c.reshape(blocks, GROUP, nstate),
        step_size.reshape(blocks, GROUP, heads),
    )

    def local_group(block):
        part_in, part_b, part_c, part_step = block
        cum_decay = jnp.cumsum(-part_step * decay_rate[None, :], axis=0)
        places = jnp.arange(GROUP, dtype=jnp.int32)
        causal = places[:, None] >= places[None, :]
        spread = cum_decay[:, None, :] - cum_decay[None, :, :]
        spread = jnp.where(causal[:, :, None], spread, -1e30)
        scores = jnp.einsum("qn,kn->qk", part_c, part_b, preferred_element_type=jnp.float32)
        mixing = (jnp.exp(spread) * scores[:, :, None] * part_step[None, :, :]).astype(jnp.bfloat16)
        inner_out = jnp.einsum("qkh,khp->qhp", mixing, part_in, preferred_element_type=jnp.float32)
        to_end = jnp.exp(cum_decay[-1][None, :] - cum_decay) * part_step
        scaled = (to_end[:, :, None] * part_in.astype(jnp.float32)).astype(jnp.bfloat16)
        local = jnp.einsum("khp,kn->hpn", scaled, part_b, preferred_element_type=jnp.float32)
        return (inner_out, cum_decay, local)

    inner_out, cum_decay, group_state = lax.map(local_group, pieces)
    totals = cum_decay[:, -1, :]

    def advance(carry, item):
        group_total, group_local = item
        return (jnp.exp(group_total)[:, None, None] * carry + group_local, carry)

    dev_state, entry_zero = lax.scan(
        advance, jnp.zeros((heads, head_dim, nstate), jnp.float32), (totals, group_state)
    )
    before = jnp.cumsum(totals, axis=0) - totals
    dev_decay = jnp.exp(jnp.sum(totals, axis=0))

    def chain(earlier, later):
        return (earlier[0] * later[0], later[0][:, None, None] * earlier[1] + later[1])

    incoming_decay, incoming = carried_in(
        (dev_decay, dev_state), "seq", chain, (jnp.ones_like(dev_decay), jnp.zeros_like(dev_state))
    )
    entry = entry_zero + jnp.exp(before)[:, :, None, None] * incoming[None]
    carried = jnp.einsum(
        "cqn,chpn->cqhp", pieces[2].astype(jnp.float32), entry, precision=lax.Precision.HIGHEST
    )
    carried = carried * jnp.exp(cum_decay)[:, :, :, None]
    outputs = (inner_out + carried).reshape(span, heads, head_dim) + skip_gain[
        None, :, None
    ] * inputs.astype(jnp.float32)
    flat = outputs.reshape(span, inner)
    factor = lax.rsqrt(jnp.mean(flat * flat, axis=1, keepdims=True) + EPS)
    result = (flat * factor * norm_gain[None, :] * valid[:, None]).astype(jnp.bfloat16)[None]
    share = heads // seq_count
    leaving = dev_decay[:, None, None] * incoming + dev_state
    last_state = broadcast(leaving, "seq", seq_count - 1)
    own_state = lax.dynamic_slice_in_dim(last_state, seq_index * share, share, 0)[None]
    wanted = jnp.sum(jnp.where(deal == req_index, slots, 0))
    piece = lax.all_gather(own_state, "req", axis=0, tiled=True)
    count = piece.shape[0]
    chosen = jnp.arange(count, dtype=jnp.int32) == wanted
    final_state = jnp.zeros_like(own_state) + jnp.sum(
        jnp.where(chosen[:, None, None, None], piece, 0.0), axis=0, keepdims=True
    )
    return (result, final_state)


def solution(mesh):
    fits = mesh.shape["req"] == 8 and mesh.shape["seq"] == 4
    return jax.shard_map(
        on_device if fits else on_device_general,
        mesh=mesh,
        in_specs=(
            P("req", "seq", None),
            P(("req", "seq"), None),
            P(("req", "seq"), None),
        )
        + (P(),) * 9,
        out_specs=(P("req", "seq", None), P("req", "seq", None, None)),
        check_vma=False,
    )
```

```python
import functools

import jax
import jax.numpy as jnp
from jax import lax
from jax.experimental import pallas as pl
from jax.experimental.pallas import tpu as pltpu
from jax.sharding import PartitionSpec as P

GROUP = 256
EPS = 1e-05
LOG2E = 1.4426950408889634
LANES = 128
HALO = 16
F32 = jnp.float32
BF16 = jnp.bfloat16
AXES = ("req", "seq")
FLIPS = {"a": 16, "b": 8, "y": 4, "x": 2}
ROUTES = (("axyb", "abxy"), ("abyx", "axby"), ("ayxb", "abyx"), ("aybx", "abxy"))
PAIRS = ((0,), (1, 2, 3), (4, 5, 6, 7), (8, 9))
VMEM = pl.BlockSpec(memory_space=pltpu.VMEM)
SMEM = pl.BlockSpec(memory_space=pltpu.SMEM)


def dot(a, b):
    return jnp.dot(a, b, preferred_element_type=F32)


def params(vmem_mib):
    return pltpu.CompilerParams(vmem_limit_bytes=vmem_mib * 1024 * 1024)


def first_head(pair, share):
    return (pair % 2) * share + 2 * (pair // 2)


def lanes(i):
    return slice(i * LANES, (i + 1) * LANES)


def valid_rows(first, rows, start, end):
    place = first + lax.broadcasted_iota(jnp.int32, (rows, LANES), 0)
    return jnp.where((place >= start) & (place < end), 1.0, 0.0).astype(F32)


def column(a, head):
    return jnp.broadcast_to(a[:, head : head + 1], (a.shape[0], LANES))


def split(a):
    upper = a.astype(BF16)
    return upper, (a - upper.astype(F32)).astype(BF16)


def project(chunk, ints, own, other, low, high, whole, padded, raw):
    block = low.shape[0] // 8
    for p in range(16):
        source = low if p < 8 else high
        row = pl.multiple_of(ints[8 + 16 * chunk + p] * block, block)
        whole[pl.ds(row, block), :] = source[(p % 8) * block : (p % 8 + 1) * block, :]
    start, end, first, core = ints[0], ints[1], ints[2], ints[3]
    span = other.shape[0]
    spans = [i for i in range(low.shape[1] // LANES) if raw is None or i != 1]
    mine = dot(own[...], whole[...])
    theirs = dot(other[...], whole[...])
    at_mine = pl.multiple_of(core * span, span)
    at_theirs = pl.multiple_of((1 - core) * span, span)
    ok_edge = valid_rows(first - 8, 8, start, end)
    ok_mine = valid_rows(first + at_mine, span, start, end)
    ok_theirs = valid_rows(first + at_theirs, span, start, end)

    def rounded(a, ok):
        return (a * ok).astype(BF16).astype(F32)

    for at, lane in enumerate(spans):
        edge = mine[0:HALO, lanes(lane)][HALO - 8 :]
        padded[at, 0:8, :] = rounded(edge, ok_edge)
        padded[at, pl.ds(8 + at_mine, span), :] = rounded(mine[HALO:, lanes(lane)], ok_mine)
        padded[at, pl.ds(8 + at_theirs, span), :] = rounded(theirs[:, lanes(lane)], ok_theirs)
    if raw is not None:
        raw[pl.ds(at_mine, span), :] = mine[HALO:, lanes(1)]
        raw[pl.ds(at_theirs, span), :] = theirs[:, lanes(1)]


def convolved(at, group, taps, padded):
    total = taps[4:5, lanes(at)]
    for k in range(4):
        rows = padded[at, group * GROUP + 5 + k : (group + 1) * GROUP + 5 + k, :]
        total = total + taps[k : k + 1, lanes(at)] * rows
    half = 0.5 * total
    return (half + half * jnp.tanh(half)).astype(BF16)


def first_kernel(
    ints, own, other, low, high, taps, rates,
    bc_out, x_out, cq_out, kq_out, kt_out, ca_out, tot_out,
    whole, padded, raw,
):
    project(0, ints, own, other, low, high, whole, padded, raw)
    row = lax.broadcasted_iota(jnp.int32, (GROUP, GROUP), 0)
    col = lax.broadcasted_iota(jnp.int32, (GROUP, GROUP), 1)
    below = jnp.where(row >= col, 1.0, 0.0).astype(BF16)
    before = jnp.zeros((1, LANES), F32)
    for group in range(bc_out.shape[0] // GROUP):
        rows = slice(group * GROUP, (group + 1) * GROUP)
        bc_out[rows, :] = convolved(0, group, taps, padded)
        for at in range(1, padded.shape[0]):
            x_out[rows, lanes(at - 1)] = convolved(at, group, taps, padded)
        ok = valid_rows(ints[2] + group * GROUP, GROUP, ints[0], ints[1])
        step = raw[rows, :] + rates[0:1, :]
        size = (jnp.maximum(step, 0.0) + jnp.log1p(jnp.exp(-jnp.abs(step)))) * ok
        decay = size * rates[1:2, :]
        high_part, rest = split(decay)
        rest = decay - high_part.astype(F32)
        mid_part, low_part = split(rest)
        cum = dot(below, high_part) + dot(below, mid_part) + dot(below, low_part)
        from_key = jnp.log2(size) - cum
        cq_out[rows, :] = cum
        kq_out[rows, :] = from_key
        kt_out[group] = from_key.T[0:32, :]
        ca_out[rows, :] = cum + before
        before = before + cum[GROUP - 1 : GROUP, :]
    tot_out[...] = jnp.broadcast_to(before, tot_out.shape)


def scan_kernel(
    chunk, heads, extra, ints, own, other, low, high, taps, x_ref, b_ref, c_ref, cq_ref, kq_ref,
    kt_ref, tot_ref, skip_ref, y_out, s_out, send_out, whole, padded, carry,
):
    project(chunk, ints, own, other, low, high, whole, padded, None)
    pairs = len(heads)
    half = GROUP // 2
    row = lax.broadcasted_iota(jnp.int32, (half, half), 0)
    col = lax.broadcasted_iota(jnp.int32, (half, half), 1)
    causal = row >= col
    left = lax.broadcasted_iota(jnp.int32, (GROUP, LANES), 1) < LANES // 2
    zero = jnp.zeros((GROUP, LANES), BF16)
    for group in range(y_out.shape[0] // GROUP):
        rows = slice(group * GROUP, (group + 1) * GROUP)
        b, c = b_ref[rows, :], c_ref[rows, :]
        scores = lax.dot_general(c, b, (((1,), (1,)), ((), ())), preferred_element_type=F32)
        cq, kq, kt = cq_ref[rows, :], kq_ref[rows, :], kt_ref[group]
        carried = None
        if group:
            upper, lower = split(carry[...])
            carried = dot(jnp.concatenate([c, c], axis=1), jnp.concatenate([upper, lower], axis=0))
        scaled, ends = [], []
        for i, head in enumerate(heads):
            if i < extra:
                x = x_ref[rows, lanes(i)]
            else:
                x = convolved(i - extra, group, taps, padded)
            top, bottom, spread = [], [], []
            for h in (head, head + 1):
                q = column(cq, h)
                spread.append(q)
                k0 = jnp.broadcast_to(kt[h : h + 1, 0:half], (half, half))
                k1 = jnp.broadcast_to(kt[h : h + 1, half:], (half, half))
                m00 = jnp.where(causal, jnp.exp2(q[0:half] + k0) * scores[0:half, 0:half], 0.0)
                m10 = jnp.exp2(q[half:] + k0) * scores[half:, 0:half]
                m11 = jnp.where(causal, jnp.exp2(q[half:] + k1) * scores[half:, half:], 0.0)
                top.append(m00.astype(BF16))
                bottom.append(m10.astype(BF16))
                bottom.append(m11.astype(BF16))
            x0, x1 = jnp.where(left, x, zero), jnp.where(left, zero, x)
            y_top = dot(
                jnp.concatenate(top, axis=1), jnp.concatenate([x0[0:half], x1[0:half]], axis=0)
            )
            y_bottom = dot(jnp.concatenate(bottom, axis=1), jnp.concatenate([x0, x1], axis=0))
            q = jnp.where(left, spread[0], spread[1])
            xf = x.astype(F32)
            rest = skip_ref[0:1, lanes(i)] * xf
            if group:
                rest = rest + jnp.exp2(q) * carried[:, lanes(i)]
            y_out[group * GROUP : group * GROUP + half, lanes(i)] = y_top + rest[0:half]
            y_out[group * GROUP + half : (group + 1) * GROUP, lanes(i)] = y_bottom + rest[half:]
            k = jnp.where(left, column(kq, head), column(kq, head + 1))
            end = q[GROUP - 1 : GROUP, :]
            scaled.append((jnp.exp2(k + end) * xf).astype(BF16))
            ends.append(jnp.exp2(end))
        local = lax.dot_general(
            b, jnp.concatenate(scaled, axis=1), (((0,), (0,)), ((), ())), preferred_element_type=F32
        )
        if group:
            local = jnp.concatenate(ends, axis=1) * carry[...] + local
        carry[...] = local
    s_out[...] = carry[...]
    send_out[0:LANES, :] = carry[...].astype(BF16)
    side = lax.broadcasted_iota(jnp.int32, (8, LANES), 1) < LANES // 2
    for i, head in enumerate(heads):
        total = jnp.where(side, column(tot_ref[...], head), column(tot_ref[...], head + 1))
        one, rest = split(total)
        two, three = split(total - one.astype(F32))
        place = lax.broadcasted_iota(jnp.int32, (8, LANES), 0)
        parts = jnp.where(place == 0, one.astype(F32), two.astype(F32))
        parts = jnp.where(place >= 2, three.astype(F32), parts)
        parts = jnp.where(place >= 3, 0.0, parts)
        send_out[LANES:, lanes(i)] = jnp.concatenate([parts, jnp.zeros_like(parts)], axis=0).astype(
            BF16
        )


def join_kernel(heads, sizes, halves, ints, c_ref, ca_ref, tot_ref, r_ref, *refs):
    count = len(sizes)
    y_refs, s_refs = refs[:count], refs[count : 2 * count]
    send_out, keep_out, fin_out = refs[2 * count :]
    later = ints[4] > 0
    core = ints[3]
    where = [(j, k) for j, size in enumerate(sizes) for k in range(size)]
    span = send_out.shape[0]
    left = lax.broadcasted_iota(jnp.int32, (span, LANES), 1) < LANES // 2
    received = r_ref[0:LANES, :].astype(F32)
    entering = (received * jnp.where(later, 1.0, 0.0)).astype(BF16)
    for out, at in ((send_out, (1 - core) * span), (keep_out, core * span)):
        rows = pl.ds(pl.multiple_of(at, span), span)
        c, ca = c_ref[rows, :], ca_ref[rows, :]
        carried = dot(c, entering)
        for i, head in enumerate(heads):
            j, k = where[i]
            q = jnp.where(left, column(ca, head), column(ca, head + 1))
            out[:, lanes(i)] = y_refs[j][rows, lanes(k)] + jnp.exp2(q) * carried[:, lanes(i)]
    side = lax.broadcasted_iota(jnp.int32, (8, LANES), 1) < LANES // 2
    for i, (early, late) in enumerate(halves):

        def own_state(p):
            j, k = where[p]
            return s_refs[j][:, lanes(k)]

        parts = r_ref[LANES:, lanes(early)].astype(F32)
        their_total = parts[0:1] + parts[1:2] + parts[2:3]
        tot = tot_ref[...]
        my_total = jnp.where(side, column(tot, heads[late]), column(tot, heads[late] + 1))[0:1]
        at_first = jnp.exp2(their_total) * own_state(early) + received[:, lanes(early)]
        at_last = jnp.exp2(my_total) * received[:, lanes(late)] + own_state(late)
        both = jnp.where(later, at_last, at_first)
        fin_out[i * LANES : (i + 1) * LANES, :] = both.T.astype(fin_out.dtype)


def norm_kernel(places, ints, gain_ref, ka_ref, kb_ref, ra_ref, rb_ref, out_ref):
    step = pl.program_id(0)
    core = ints[3]
    rows = out_ref.shape[0]
    first = ints[2] + (core * pl.num_programs(0) + step) * rows
    ok = valid_rows(first, rows, ints[0], ints[1])
    blocks = []
    for who, refs in ((core, (ka_ref, kb_ref)), (1 - core, (ra_ref, rb_ref))):
        for ref, wheres in zip(refs, places, strict=True):
            for i, where in enumerate(wheres):
                at = pl.multiple_of((where + 5 * who) * LANES, LANES)
                blocks.append((at, ref, i))
    total = jnp.zeros((rows, LANES), F32)
    for _, ref, i in blocks:
        v = ref[:, lanes(i)]
        total = total + v * v
    mean = jnp.sum(total, axis=1, keepdims=True) * (1.0 / out_ref.shape[1])
    factor = lax.rsqrt(mean + EPS) * ok
    for at, ref, i in blocks:
        v = ref[:, lanes(i)]
        out_ref[:, pl.ds(at, LANES)] = (v * factor * gain_ref[0:1, pl.ds(at, LANES)]).astype(BF16)


def swapped(x, masks):
    count = lax.axis_size("req") * lax.axis_size("seq")
    return lax.ppermute(x, AXES, [(i, i ^ masks[i % 2]) for i in range(count)])


def on_device(
    tokens, mix_weight, step_weight, conv_weight, conv_bias, step_bias, decay_rate, skip_gain,
    norm_gain, prompt_len, prompt_start, deal,
):
    seq_index = lax.axis_index("seq")
    req_index = lax.axis_index("req")
    core, along = seq_index % 2, seq_index // 2
    rows = tokens[0]
    span, depth = rows.shape
    inner = norm_gain.shape[0]
    heads = decay_rate.shape[0]
    head_dim = inner // heads
    nstate = (mix_weight.shape[1] - inner) // 2
    share = heads // 4
    quarter = inner // 4
    chip = req_index * 2 + along

    def mine_of(a, b, who):
        bc = lax.dynamic_slice_in_dim(a, inner + nstate * who, nstate, 1)
        early = lax.dynamic_slice_in_dim(a, quarter * who, quarter, 1)
        late = lax.dynamic_slice_in_dim(a, 2 * quarter + quarter * who, quarter, 1)
        parts = [bc]
        if b is not None:
            parts += [steps_of(b, who)]
        for i in range(quarter // LANES):
            parts += [early[:, lanes(i)], late[:, lanes(i)]]
        return jnp.concatenate(parts, axis=1)

    def steps_of(b, who):
        one = lax.dynamic_slice_in_dim(b, share * who, share, 1)
        two = lax.dynamic_slice_in_dim(b, 2 * share + share * who, share, 1)
        return jnp.concatenate(
            [one, two, jnp.zeros((b.shape[0], LANES - 2 * share), b.dtype)], axis=1
        )

    kept = mine_of(mix_weight, step_weight, core)
    given = mine_of(mix_weight, step_weight, 1 - core)
    got = swapped(given, (1, 1))
    weights = jnp.where(
        core == 0, jnp.concatenate([kept, got], axis=0), jnp.concatenate([got, kept], axis=0)
    )

    order = []

    def gathered(block, routes):
        masks = [(FLIPS[one], FLIPS[two]) for one, two in zip(*routes, strict=True)]
        for p in range(2 ** len(masks)):
            one, two = (
                sum(mask[who] // 2 for s, mask in enumerate(masks) if (p >> s) & 1)
                for who in range(2)
            )
            order.append(jnp.bitwise_xor(chip, jnp.where(core == 0, one, two)))
        for mask in masks[:-1]:
            block = jnp.concatenate([block, swapped(block, mask)], axis=0)
        return block, swapped(block, masks[-1])

    chunks, at = [], 0
    for i, routes in enumerate(ROUTES):
        width = (len(PAIRS[i]) + (2 if i == 0 else 0)) * LANES
        chunks.append(gathered(weights[:, at : at + width], routes))
        at += width

    other = swapped(rows, (1, 1))
    last_rows = jnp.where(core == 1, rows[span - HALO :], other[span - HALO :])
    count = lax.axis_size("req") * lax.axis_size("seq")
    halo = lax.ppermute(
        last_rows, AXES, [(i, i + 2) for i in range(count) if (i // 2) % 2 == 0]
    )
    own = jnp.concatenate([halo, rows], axis=0)

    slots = jnp.arange(deal.shape[0], dtype=jnp.int32)
    request = jnp.sum(jnp.where(slots == req_index, deal, 0))
    length = jnp.sum(jnp.where(slots == request, prompt_len, 0))
    start = jnp.sum(jnp.where(slots == request, prompt_start, 0))
    taps = mine_of(
        jnp.concatenate([conv_weight, conv_bias[None], jnp.zeros_like(conv_weight[:3])], axis=0),
        None,
        core,
    )
    rates = jnp.concatenate(
        [
            steps_of(step_bias[None], core),
            steps_of(decay_rate[None] * (-LOG2E), core),
            jnp.zeros((6, LANES), F32),
        ],
        axis=0,
    )
    skip_all = mine_of(
        jnp.concatenate([jnp.repeat(skip_gain, head_dim), jnp.zeros((2 * nstate,), F32)])[None],
        None,
        core,
    )
    skip = jnp.broadcast_to(skip_all[:, LANES:], (8, inner // 2))
    ints = jnp.stack(
        [start, start + length, along * 2 * span, core, along]
        + [jnp.zeros_like(core)] * 3
        + order
    ).astype(jnp.int32)

    chip_rows = 2 * span
    groups = chip_rows // GROUP

    def scratch(width, spans):
        return [
            pltpu.VMEM((depth, width), BF16),
            pltpu.VMEM((spans, chip_rows + 8, LANES), F32),
        ]

    width = chunks[0][0].shape[1]
    extra = len(PAIRS[0])
    bc, x0, cq, kq, kt, ca, tot = pl.pallas_call(
        first_kernel,
        in_specs=[SMEM] + [VMEM] * 6,
        out_specs=[VMEM] * 7,
        scratch_shapes=scratch(width, 1 + extra) + [pltpu.VMEM((chip_rows, LANES), F32)],
        out_shape=[
            jax.ShapeDtypeStruct((chip_rows, LANES), BF16),
            jax.ShapeDtypeStruct((chip_rows, extra * LANES), BF16),
            jax.ShapeDtypeStruct((chip_rows, LANES), F32),
            jax.ShapeDtypeStruct((chip_rows, LANES), F32),
            jax.ShapeDtypeStruct((groups, 32, GROUP), F32),
            jax.ShapeDtypeStruct((chip_rows, LANES), F32),
            jax.ShapeDtypeStruct((8, LANES), F32),
        ],
        compiler_params=params(24),
        cost_estimate=pl.CostEstimate(
            flops=2 * chip_rows * depth * width, bytes_accessed=9000000, transcendentals=500000
        ),
        name="first",
    )(ints, own, other, *chunks[0], taps[:, : (1 + extra) * LANES], rates)

    bc_other = swapped(bc, (1, 1))
    b = jnp.where(core == 0, bc, bc_other)
    c = jnp.where(core == 0, bc_other, bc)

    def scanned(index):
        chunk = chunks[index]
        more = extra if index == 1 else 0
        held = (PAIRS[0] if more else ()) + PAIRS[index]
        pairs = len(held)
        new = pairs - more
        firsts = [first_head(p, share) for p in held]
        tap_at, skip_at = (1 + PAIRS[index][0]) * LANES, held[0] * LANES
        width = chunk[0].shape[1]
        return pl.pallas_call(
            functools.partial(scan_kernel, index, firsts, more),
            in_specs=[SMEM] + [VMEM] * 13,
            out_specs=[VMEM] * 3,
            scratch_shapes=scratch(width, new) + [pltpu.VMEM((LANES, pairs * LANES), F32)],
            out_shape=[
                jax.ShapeDtypeStruct((chip_rows, pairs * LANES), F32),
                jax.ShapeDtypeStruct((LANES, pairs * LANES), F32),
                jax.ShapeDtypeStruct((LANES + 16, pairs * LANES), BF16),
            ],
            compiler_params=params(28),
            cost_estimate=pl.CostEstimate(
                flops=2 * chip_rows * depth * width + pairs * 600000000,
                bytes_accessed=12000000,
                transcendentals=pairs * 400000,
            ),
            name="scan",
        )(
            ints, own, other, *chunk, taps[:, tap_at : tap_at + new * LANES],
            x0, b, c, cq, kq, kt, tot, skip[:, skip_at : skip_at + pairs * LANES],
        )

    def joined(held, ys, ss, r):
        pairs = len(held)
        halves = [(i, i + 1) for i in range(0, pairs, 2)]
        sizes = [y.shape[1] // LANES for y in ys]
        return pl.pallas_call(
            functools.partial(join_kernel, [first_head(p, share) for p in held], sizes, halves),
            in_specs=[SMEM] + [VMEM] * (4 + 2 * len(ys)),
            out_specs=[VMEM] * 3,
            out_shape=[
                jax.ShapeDtypeStruct((span, pairs * LANES), F32),
                jax.ShapeDtypeStruct((span, pairs * LANES), F32),
                jax.ShapeDtypeStruct((len(halves) * LANES, nstate), BF16),
            ],
            compiler_params=params(28),
            cost_estimate=pl.CostEstimate(
                flops=4 * chip_rows * LANES * pairs * LANES,
                bytes_accessed=chip_rows * pairs * LANES * 8,
                transcendentals=chip_rows * pairs * LANES,
            ),
            name="join",
        )(ints, c, ca, tot, r, *ys, *ss)

    wanted = jnp.sum(jnp.where(deal == req_index, slots, 0))
    partner_wanted = jnp.sum(jnp.where(deal == (req_index ^ 1), slots, 0))

    def delivered(block):
        one = swapped(block, (16, 16))
        pair = jnp.stack([block, one])
        two = swapped(pair, (8, 8))

        def pick(row):
            rel = row ^ req_index
            far, near = (rel >> 2) & 1, (rel >> 1) & 1
            return jnp.where(
                near == 1,
                jnp.where(far == 1, two[1], two[0]),
                jnp.where(far == 1, one, block),
            )

        three = swapped(pick(partner_wanted), (4, 4))
        odd = (wanted ^ req_index) & 1
        return jnp.where(odd == 1, three, pick(wanted)).astype(F32)

    y1, s1, t1 = scanned(1)
    y2, s2, t2 = scanned(2)
    r12 = swapped(jnp.concatenate([t1, t2], axis=1), (2, 2))
    first_pairs = PAIRS[0] + PAIRS[1] + PAIRS[2]
    send_a, keep_a, fin_a = joined(first_pairs, (y1, y2), (s1, s2), r12)
    got_a = swapped(send_a, (1, 1))
    final_a = delivered(fin_a)
    y3, s3, t3 = scanned(3)
    r3 = swapped(t3, (2, 2))
    send_b, keep_b, fin_b = joined(PAIRS[3], (y3,), (s3,), r3)
    got_b = swapped(send_b, (1, 1))
    final_b = delivered(fin_b)

    final_state = jnp.concatenate([final_a, final_b], axis=0).reshape(1, share, head_dim, nstate)
    places = [
        [(p % 2) * (2 * quarter // LANES) + p // 2 for p in held]
        for held in (first_pairs, PAIRS[3])
    ]
    block = span // 4
    result = pl.pallas_call(
        functools.partial(norm_kernel, places),
        grid_spec=pltpu.PrefetchScalarGridSpec(
            num_scalar_prefetch=1,
            grid=(span // block,),
            in_specs=[pl.BlockSpec((1, inner), lambda i, ints: (0, 0))]
            + [
                pl.BlockSpec((block, a.shape[1]), lambda i, ints: (i, 0))
                for a in (keep_a, keep_b, got_a, got_b)
            ],
            out_specs=pl.BlockSpec((block, inner), lambda i, ints: (i, 0)),
        ),
        out_shape=jax.ShapeDtypeStruct((span, inner), BF16),
        compiler_params=params(24),
        cost_estimate=pl.CostEstimate(
            flops=6 * span * inner, bytes_accessed=6 * span * inner, transcendentals=span
        ),
        name="norm",
    )(ints, norm_gain[None], keep_a, keep_b, got_a, got_b)
    return (result[None], final_state)


def passed_along(block, axis, distance):
    devices = range(lax.axis_size(axis))
    route = [(i - distance, i) for i in devices if i - distance in devices]
    return lax.ppermute(block, axis, route)


def carried_in(part, axis, combine, identity):
    place = lax.axis_index(axis)
    gathered = jax.tree.map(lambda a: lax.all_gather(a, axis), part)
    state = jax.tree.map(lambda a, e: jnp.zeros_like(a) + jnp.asarray(e, a.dtype), part, identity)

    def one(step, state):
        return combine(
            state, jax.tree.map(lambda a: lax.dynamic_index_in_dim(a, step, 0, False), gathered)
        )

    return lax.fori_loop(0, place, one, state)


def broadcast(x, axis, root):
    mine = lax.axis_index(axis) == root
    return lax.psum(jnp.where(mine, x, jnp.zeros_like(x)), axis)


def on_device_general(
    tokens,
    mix_weight,
    step_weight,
    conv_weight,
    conv_bias,
    step_bias,
    decay_rate,
    skip_gain,
    norm_gain,
    prompt_len,
    prompt_start,
    deal,
):
    seq_count = lax.axis_size("seq")
    seq_index = lax.axis_index("seq")
    req_index = lax.axis_index("req")
    rows = tokens[0]
    span = rows.shape[0]
    total_reqs = deal.shape[0]
    slots = jnp.arange(total_reqs, dtype=jnp.int32)
    request = jnp.sum(jnp.where(slots == req_index, deal, 0))
    length = jnp.sum(jnp.where(slots == request, prompt_len, 0))
    start = jnp.sum(jnp.where(slots == request, prompt_start, 0))
    place = seq_index * span + jnp.arange(span, dtype=jnp.int32)
    valid = ((place >= start) & (place < start + length)).astype(jnp.float32)
    whole_mix, whole_step = (
        lax.all_gather(mix_weight, ("req", "seq"), axis=0, tiled=True),
        lax.all_gather(step_weight, ("req", "seq"), axis=0, tiled=True),
    )
    mixed = jnp.dot(rows, whole_mix, preferred_element_type=jnp.float32)
    raw_step = jnp.dot(rows, whole_step, preferred_element_type=jnp.float32)
    mixed = (mixed * valid[:, None]).astype(jnp.bfloat16)
    taps = conv_weight.shape[0]
    edge = passed_along(mixed[span - (taps - 1) :], "seq", 1)
    padded = jnp.concatenate([edge, mixed], axis=0)
    conv_sum = jnp.zeros(mixed.shape, jnp.float32) + conv_bias[None, :]
    for offset in range(taps):
        conv_sum = conv_sum + conv_weight[offset][None, :] * padded[offset : offset + span].astype(
            jnp.float32
        )
    convolved = jax.nn.silu(conv_sum).astype(jnp.bfloat16)
    heads = decay_rate.shape[0]
    inner = norm_gain.shape[0]
    head_dim = inner // heads
    nstate = (mixed.shape[1] - inner) // 2
    blocks = span // GROUP
    inputs = convolved[:, :inner].reshape(span, heads, head_dim)
    mixed_b = convolved[:, inner : inner + nstate]
    mixed_c = convolved[:, inner + nstate :]
    step_size = jax.nn.softplus(raw_step + step_bias[None, :]) * valid[:, None]
    pieces = (
        inputs.reshape(blocks, GROUP, heads, head_dim),
        mixed_b.reshape(blocks, GROUP, nstate),
        mixed_c.reshape(blocks, GROUP, nstate),
        step_size.reshape(blocks, GROUP, heads),
    )

    def local_group(block):
        part_in, part_b, part_c, part_step = block
        cum_decay = jnp.cumsum(-part_step * decay_rate[None, :], axis=0)
        places = jnp.arange(GROUP, dtype=jnp.int32)
        causal = places[:, None] >= places[None, :]
        spread = cum_decay[:, None, :] - cum_decay[None, :, :]
        spread = jnp.where(causal[:, :, None], spread, -1e30)
        scores = jnp.einsum("qn,kn->qk", part_c, part_b, preferred_element_type=jnp.float32)
        mixing = (jnp.exp(spread) * scores[:, :, None] * part_step[None, :, :]).astype(jnp.bfloat16)
        inner_out = jnp.einsum("qkh,khp->qhp", mixing, part_in, preferred_element_type=jnp.float32)
        to_end = jnp.exp(cum_decay[-1][None, :] - cum_decay) * part_step
        scaled = (to_end[:, :, None] * part_in.astype(jnp.float32)).astype(jnp.bfloat16)
        local = jnp.einsum("khp,kn->hpn", scaled, part_b, preferred_element_type=jnp.float32)
        return (inner_out, cum_decay, local)

    inner_out, cum_decay, group_state = lax.map(local_group, pieces)
    totals = cum_decay[:, -1, :]

    def advance(carry, item):
        group_total, group_local = item
        return (jnp.exp(group_total)[:, None, None] * carry + group_local, carry)

    dev_state, entry_zero = lax.scan(
        advance, jnp.zeros((heads, head_dim, nstate), jnp.float32), (totals, group_state)
    )
    before = jnp.cumsum(totals, axis=0) - totals
    dev_decay = jnp.exp(jnp.sum(totals, axis=0))

    def chain(earlier, later):
        return (earlier[0] * later[0], later[0][:, None, None] * earlier[1] + later[1])

    incoming_decay, incoming = carried_in(
        (dev_decay, dev_state), "seq", chain, (jnp.ones_like(dev_decay), jnp.zeros_like(dev_state))
    )
    entry = entry_zero + jnp.exp(before)[:, :, None, None] * incoming[None]
    carried = jnp.einsum(
        "cqn,chpn->cqhp", pieces[2].astype(jnp.float32), entry, precision=lax.Precision.HIGHEST
    )
    carried = carried * jnp.exp(cum_decay)[:, :, :, None]
    outputs = (inner_out + carried).reshape(span, heads, head_dim) + skip_gain[
        None, :, None
    ] * inputs.astype(jnp.float32)
    flat = outputs.reshape(span, inner)
    factor = lax.rsqrt(jnp.mean(flat * flat, axis=1, keepdims=True) + EPS)
    result = (flat * factor * norm_gain[None, :] * valid[:, None]).astype(jnp.bfloat16)[None]
    share = heads // seq_count
    leaving = dev_decay[:, None, None] * incoming + dev_state
    last_state = broadcast(leaving, "seq", seq_count - 1)
    own_state = lax.dynamic_slice_in_dim(last_state, seq_index * share, share, 0)[None]
    wanted = jnp.sum(jnp.where(deal == req_index, slots, 0))
    piece = lax.all_gather(own_state, "req", axis=0, tiled=True)
    count = piece.shape[0]
    chosen = jnp.arange(count, dtype=jnp.int32) == wanted
    final_state = jnp.zeros_like(own_state) + jnp.sum(
        jnp.where(chosen[:, None, None, None], piece, 0.0), axis=0, keepdims=True
    )
    return (result, final_state)


def solution(mesh):
    fits = mesh.shape["req"] == 8 and mesh.shape["seq"] == 4
    return jax.shard_map(
        on_device if fits else on_device_general,
        mesh=mesh,
        in_specs=(
            P("req", "seq", None),
            P(("req", "seq"), None),
            P(("req", "seq"), None),
        )
        + (P(),) * 9,
        out_specs=(P("req", "seq", None), P("req", "seq", None, None)),
        check_vma=False,
    )
```

```python
import functools

import jax
import jax.numpy as jnp
from jax import lax
from jax.experimental import pallas as pl
from jax.experimental.pallas import tpu as pltpu
from jax.sharding import PartitionSpec as P

GROUP = 256
EPS = 1e-05
LOG2E = 1.4426950408889634
LANES = 128
HALO = 16
F32 = jnp.float32
BF16 = jnp.bfloat16
AXES = ("req", "seq")
FLIPS = {"a": 16, "b": 8, "y": 4, "x": 2}
ROUTES = (("axyb", "abxy"), ("abyx", "axby"), ("ayxb", "abyx"), ("aybx", "abxy"))
PAIRS = ((0,), (1, 2, 3), (4, 5, 6, 7), (8, 9))
SCHEDULE = (
    "0.0", "1.0", "tokens", "0.1", "2.0", "1.1", "0.2", "halo", "settings", "3.0",
    "2.1", "1.2", "0.3", "own", "3.1", "2.2", "1.3", "3.2", "2.3", "K0",
    "3.3", "K1", "K2", "xA", "K3", "xB", "JA", "fA0", "JB", "fB0",
    "fA1", "fB1", "fA2", "fB2", "norm", "fA3", "fB3",
)
VMEM = pl.BlockSpec(memory_space=pltpu.VMEM)
SMEM = pl.BlockSpec(memory_space=pltpu.SMEM)


def dot(a, b):
    return jnp.dot(a, b, preferred_element_type=F32)


def params(vmem_mib):
    return pltpu.CompilerParams(vmem_limit_bytes=vmem_mib * 1024 * 1024)


def first_head(pair, share):
    return (pair % 2) * share + 2 * (pair // 2)


def lanes(i):
    return slice(i * LANES, (i + 1) * LANES)


def valid_rows(first, rows, start, end):
    place = first + lax.broadcasted_iota(jnp.int32, (rows, LANES), 0)
    return jnp.where((place >= start) & (place < end), 1.0, 0.0).astype(F32)


def column(a, head):
    return jnp.broadcast_to(a[:, head : head + 1], (a.shape[0], LANES))


def split(a):
    upper = a.astype(BF16)
    return upper, (a - upper.astype(F32)).astype(BF16)


def project(chunk, ints, own, other, low, high, whole, padded, raw):
    block = low.shape[0] // 8
    start, end, first, core = ints[0], ints[1], ints[2], ints[3]
    for p in range(16):
        one, two = (
            sum(FLIPS[step] // 2 for i, step in enumerate(route) if (p >> i) & 1)
            for route in ROUTES[chunk]
        )
        chip = jnp.bitwise_xor(ints[5], jnp.where(core == 0, one, two))
        source = low if p < 8 else high
        row = pl.multiple_of(chip * block, block)
        whole[pl.ds(row, block), :] = source[(p % 8) * block : (p % 8 + 1) * block, :]
    span = other.shape[0]
    spans = [i for i in range(low.shape[1] // LANES) if raw is None or i != 1]
    mine = dot(own[...], whole[...])
    theirs = dot(other[...], whole[...])
    at_mine = pl.multiple_of(core * span, span)
    at_theirs = pl.multiple_of((1 - core) * span, span)
    ok_edge = valid_rows(first - 8, 8, start, end)
    ok_mine = valid_rows(first + at_mine, span, start, end)
    ok_theirs = valid_rows(first + at_theirs, span, start, end)

    def rounded(a, ok):
        return (a * ok).astype(BF16).astype(F32)

    for at, lane in enumerate(spans):
        edge = mine[0:HALO, lanes(lane)][HALO - 8 :]
        padded[at, 0:8, :] = rounded(edge, ok_edge)
        padded[at, pl.ds(8 + at_mine, span), :] = rounded(mine[HALO:, lanes(lane)], ok_mine)
        padded[at, pl.ds(8 + at_theirs, span), :] = rounded(theirs[:, lanes(lane)], ok_theirs)
    if raw is not None:
        raw[pl.ds(at_mine, span), :] = mine[HALO:, lanes(1)]
        raw[pl.ds(at_theirs, span), :] = theirs[:, lanes(1)]


def convolved(at, group, taps, padded):
    total = taps[4:5, lanes(at)]
    for k in range(4):
        rows = padded[at, group * GROUP + 5 + k : (group + 1) * GROUP + 5 + k, :]
        total = total + taps[k : k + 1, lanes(at)] * rows
    half = 0.5 * total
    return (half + half * jnp.tanh(half)).astype(BF16)


def first_kernel(
    ints, own, other, low, high, taps, rates,
    bc_out, x_out, cq_out, kq_out, kt_out, ca_out, tot_out,
    whole, padded, raw,
):
    project(0, ints, own, other, low, high, whole, padded, raw)
    row = lax.broadcasted_iota(jnp.int32, (GROUP, GROUP), 0)
    col = lax.broadcasted_iota(jnp.int32, (GROUP, GROUP), 1)
    below = jnp.where(row >= col, 1.0, 0.0).astype(BF16)
    before = jnp.zeros((1, LANES), F32)
    for group in range(bc_out.shape[0] // GROUP):
        rows = slice(group * GROUP, (group + 1) * GROUP)
        bc_out[rows, :] = convolved(0, group, taps, padded)
        for at in range(1, padded.shape[0]):
            x_out[rows, lanes(at - 1)] = convolved(at, group, taps, padded)
        ok = valid_rows(ints[2] + group * GROUP, GROUP, ints[0], ints[1])
        step = raw[rows, :] + rates[0:1, :]
        size = (jnp.maximum(step, 0.0) + jnp.log1p(jnp.exp(-jnp.abs(step)))) * ok
        decay = size * rates[1:2, :]
        high_part, rest = split(decay)
        rest = decay - high_part.astype(F32)
        mid_part, low_part = split(rest)
        cum = dot(below, high_part) + dot(below, mid_part) + dot(below, low_part)
        from_key = jnp.log2(size) - cum
        cq_out[rows, :] = cum
        kq_out[rows, :] = from_key
        kt_out[group] = from_key.T[0:32, :]
        ca_out[rows, :] = cum + before
        before = before + cum[GROUP - 1 : GROUP, :]
    tot_out[...] = jnp.broadcast_to(before, tot_out.shape)


def scan_kernel(
    chunk, heads, extra, ints, own, other, low, high, taps, x_ref, b_ref, c_ref, cq_ref, kq_ref,
    kt_ref, tot_ref, skip_ref, y_out, s_out, send_out, whole, padded, carry,
):
    project(chunk, ints, own, other, low, high, whole, padded, None)
    pairs = len(heads)
    half = GROUP // 2
    row = lax.broadcasted_iota(jnp.int32, (half, half), 0)
    col = lax.broadcasted_iota(jnp.int32, (half, half), 1)
    causal = row >= col
    left = lax.broadcasted_iota(jnp.int32, (GROUP, LANES), 1) < LANES // 2
    zero = jnp.zeros((GROUP, LANES), BF16)
    for group in range(y_out.shape[0] // GROUP):
        rows = slice(group * GROUP, (group + 1) * GROUP)
        b, c = b_ref[rows, :], c_ref[rows, :]
        scores = lax.dot_general(c, b, (((1,), (1,)), ((), ())), preferred_element_type=F32)
        cq, kq, kt = cq_ref[rows, :], kq_ref[rows, :], kt_ref[group]
        carried = None
        if group:
            upper, lower = split(carry[...])
            carried = dot(jnp.concatenate([c, c], axis=1), jnp.concatenate([upper, lower], axis=0))
        scaled, ends = [], []
        for i, head in enumerate(heads):
            if i < extra:
                x = x_ref[rows, lanes(i)]
            else:
                x = convolved(i - extra, group, taps, padded)
            top, bottom, spread = [], [], []
            for h in (head, head + 1):
                q = column(cq, h)
                spread.append(q)
                k0 = jnp.broadcast_to(kt[h : h + 1, 0:half], (half, half))
                k1 = jnp.broadcast_to(kt[h : h + 1, half:], (half, half))
                m00 = jnp.where(causal, jnp.exp2(q[0:half] + k0) * scores[0:half, 0:half], 0.0)
                m10 = jnp.exp2(q[half:] + k0) * scores[half:, 0:half]
                m11 = jnp.where(causal, jnp.exp2(q[half:] + k1) * scores[half:, half:], 0.0)
                top.append(m00.astype(BF16))
                bottom.append(m10.astype(BF16))
                bottom.append(m11.astype(BF16))
            x0, x1 = jnp.where(left, x, zero), jnp.where(left, zero, x)
            y_top = dot(
                jnp.concatenate(top, axis=1), jnp.concatenate([x0[0:half], x1[0:half]], axis=0)
            )
            y_bottom = dot(jnp.concatenate(bottom, axis=1), jnp.concatenate([x0, x1], axis=0))
            q = jnp.where(left, spread[0], spread[1])
            xf = x.astype(F32)
            rest = skip_ref[2:3, lanes(i)] * xf
            if group:
                rest = rest + jnp.exp2(q) * carried[:, lanes(i)]
            y_out[group * GROUP : group * GROUP + half, lanes(i)] = y_top + rest[0:half]
            y_out[group * GROUP + half : (group + 1) * GROUP, lanes(i)] = y_bottom + rest[half:]
            k = jnp.where(left, column(kq, head), column(kq, head + 1))
            end = q[GROUP - 1 : GROUP, :]
            scaled.append((jnp.exp2(k + end) * xf).astype(BF16))
            ends.append(jnp.exp2(end))
        local = lax.dot_general(
            b, jnp.concatenate(scaled, axis=1), (((0,), (0,)), ((), ())), preferred_element_type=F32
        )
        if group:
            local = jnp.concatenate(ends, axis=1) * carry[...] + local
        carry[...] = local
    s_out[...] = carry[...]
    send_out[0:LANES, :] = carry[...].astype(BF16)
    side = lax.broadcasted_iota(jnp.int32, (8, LANES), 1) < LANES // 2
    for i, head in enumerate(heads):
        total = jnp.where(side, column(tot_ref[...], head), column(tot_ref[...], head + 1))
        one, rest = split(total)
        two, three = split(total - one.astype(F32))
        place = lax.broadcasted_iota(jnp.int32, (8, LANES), 0)
        parts = jnp.where(place == 0, one.astype(F32), two.astype(F32))
        parts = jnp.where(place >= 2, three.astype(F32), parts)
        parts = jnp.where(place >= 3, 0.0, parts)
        send_out[LANES:, lanes(i)] = jnp.concatenate([parts, jnp.zeros_like(parts)], axis=0).astype(
            BF16
        )


def join_kernel(heads, sizes, halves, ints, c_ref, ca_ref, tot_ref, r_ref, *refs):
    count = len(sizes)
    y_refs, s_refs = refs[:count], refs[count : 2 * count]
    send_out, keep_out, fin_out = refs[2 * count :]
    later = ints[4] > 0
    core = ints[3]
    where = [(j, k) for j, size in enumerate(sizes) for k in range(size)]
    span = send_out.shape[0]
    received = r_ref[0:LANES, :].astype(F32)
    entering = (received * jnp.where(later, 1.0, 0.0)).astype(BF16)
    from_head = lax.broadcasted_iota(jnp.int32, (2 * LANES, LANES), 0) % LANES
    second = lax.broadcasted_iota(jnp.int32, (2 * LANES, LANES), 1) // (LANES // 2)
    spread = jnp.concatenate(
        [jnp.where(from_head == head + second, 1.0, 0.0).astype(BF16) for head in heads], axis=1
    )
    for out, at in ((send_out, (1 - core) * span), (keep_out, core * span)):
        rows = pl.ds(pl.multiple_of(at, span), span)
        decay = jnp.exp2(ca_ref[rows, :])
        decay = dot(jnp.concatenate(split(decay), axis=1), spread)
        carried = dot(c_ref[rows, :], entering)
        for i in range(len(heads)):
            j, k = where[i]
            out[:, lanes(i)] = (
                y_refs[j][rows, lanes(k)] + decay[:, lanes(i)] * carried[:, lanes(i)]
            )
    side = lax.broadcasted_iota(jnp.int32, (8, LANES), 1) < LANES // 2
    tot = tot_ref[...]
    for i, (early, late) in enumerate(halves):

        def own_state(p):
            j, k = where[p]
            return s_refs[j][:, lanes(k)]

        parts = r_ref[LANES:, lanes(early)].astype(F32)
        their_total = parts[0:1] + parts[1:2] + parts[2:3]
        my_total = jnp.where(side, column(tot, heads[late]), column(tot, heads[late] + 1))[0:1]
        at_first = jnp.exp2(their_total) * own_state(early) + received[:, lanes(early)]
        at_last = jnp.exp2(my_total) * received[:, lanes(late)] + own_state(late)
        both = jnp.where(later, at_last, at_first)
        fin_out[i * LANES : (i + 1) * LANES, :] = both.T.astype(fin_out.dtype)


def norm_kernel(places, ints, gain_ref, ka_ref, kb_ref, ra_ref, rb_ref, out_ref):
    step = pl.program_id(0)
    core = ints[3]
    rows = out_ref.shape[0]
    first = ints[2] + (core * pl.num_programs(0) + step) * rows
    ok = valid_rows(first, rows, ints[0], ints[1])
    blocks = []
    for who, refs in ((core, (ka_ref, kb_ref)), (1 - core, (ra_ref, rb_ref))):
        for ref, wheres in zip(refs, places, strict=True):
            for i, where in enumerate(wheres):
                at = pl.multiple_of((where + 5 * who) * LANES, LANES)
                blocks.append((at, ref, i))
    total = jnp.zeros((rows, LANES), F32)
    for _, ref, i in blocks:
        v = ref[:, lanes(i)]
        total = total + v * v
    mean = jnp.sum(total, axis=1, keepdims=True) * (1.0 / out_ref.shape[1])
    factor = lax.rsqrt(mean + EPS) * ok
    for at, ref, i in blocks:
        v = ref[:, lanes(i)]
        out_ref[:, pl.ds(at, LANES)] = (v * factor * gain_ref[0:1, pl.ds(at, LANES)]).astype(BF16)


def head_of(lane, core, share):
    return jnp.where(lane < 2 * share, lane + core * share + (lane // share) * share, -1)


def chosen_heads(core, heads):
    row = lax.broadcasted_iota(jnp.int32, (heads, LANES), 0)
    lane = lax.broadcasted_iota(jnp.int32, (heads, LANES), 1)
    return jnp.where(row == head_of(lane, core, heads // 4), 1.0, 0.0)


def columns_of(source, core, inner):
    first = inner // 4 // LANES
    blocks = [inner // LANES + core]
    for i in range(first):
        blocks += [first * core + i, 2 * first + first * core + i]
    return [source[:, pl.ds(pl.multiple_of(at * LANES, LANES), LANES)] for at in blocks]


def sort_kernel(inner, ints, mix, step, kept_out, given_out):
    for out, core in ((kept_out, ints[3]), (given_out, 1 - ints[3])):
        parts = columns_of(mix, core, inner)
        out[:, lanes(0)] = parts[0]
        out[:, lanes(1)] = dot(step[...], chosen_heads(core, step.shape[1]).astype(BF16)).astype(BF16)
        for i, part in enumerate(parts[1:]):
            out[:, lanes(2 + i)] = part


def stack_kernel(ints, kept, got, *outs):
    rows = kept.shape[0]
    core = ints[3]
    at = 0
    for out in outs:
        width = out.shape[1]
        out[pl.ds(pl.multiple_of(core * rows, rows), rows), :] = kept[:, at : at + width]
        out[pl.ds(pl.multiple_of((1 - core) * rows, rows), rows), :] = got[:, at : at + width]
        at += width


def settings_kernel(inner, ints, conv, bias, per_head, taps_out, rates_out, skip_out):
    core = ints[3]
    for i, (tap, more) in enumerate(
        zip(columns_of(conv, core, inner), columns_of(bias, core, inner), strict=True)
    ):
        taps_out[0:4, lanes(i)] = tap
        taps_out[4:5, lanes(i)] = more
        taps_out[5:8, lanes(i)] = jnp.zeros((3, LANES), F32)
    heads = per_head.shape[1]
    exact = functools.partial(
        jnp.dot, precision=lax.Precision.HIGHEST, preferred_element_type=F32
    )
    own = exact(per_head[...], chosen_heads(core, heads))
    rates_out[...] = own
    row = lax.broadcasted_iota(jnp.int32, (LANES, inner // 2), 0)
    lane = lax.broadcasted_iota(jnp.int32, (LANES, inner // 2), 1)
    pair, second = lane // LANES, (lane % LANES) // (LANES // 2)
    mine = (pair % 2) * (heads // 4) + 2 * (pair // 2) + second
    skip_out[...] = exact(own, jnp.where(row == mine, 1.0, 0.0))


def swapped(x, masks):
    count = lax.axis_size("req") * lax.axis_size("seq")
    return lax.ppermute(x, AXES, [(i, i ^ masks[i % 2]) for i in range(count)])


def on_device(
    tokens, mix_weight, step_weight, conv_weight, conv_bias, step_bias, decay_rate, skip_gain,
    norm_gain, prompt_len, prompt_start, deal,
):
    seq_index = lax.axis_index("seq")
    req_index = lax.axis_index("req")
    core, along = seq_index % 2, seq_index // 2
    rows = tokens[0]
    span, depth = rows.shape
    inner = norm_gain.shape[0]
    heads = decay_rate.shape[0]
    head_dim = inner // heads
    nstate = (mix_weight.shape[1] - inner) // 2
    share = heads // 4
    quarter = inner // 4
    slots = jnp.arange(deal.shape[0], dtype=jnp.int32)
    request = jnp.sum(jnp.where(slots == req_index, deal, 0))
    length = jnp.sum(jnp.where(slots == request, prompt_len, 0))
    start = jnp.sum(jnp.where(slots == request, prompt_start, 0))
    wanted = jnp.sum(jnp.where(deal == req_index, slots, 0))
    partner_wanted = jnp.sum(jnp.where(deal == (req_index ^ 1), slots, 0))
    chip = req_index * 2 + along
    place = jnp.stack([along * 2 * span, core, along, chip])
    early_ints = jnp.concatenate([jnp.zeros((2,), jnp.int32), place])
    state = {}

    def after(*values):
        if "token" not in state:
            return values if len(values) > 1 else values[0]
        *out, state["token"] = lax.optimization_barrier((*values, state["token"]))
        return tuple(out) if len(out) > 1 else out[0]

    widths = [(len(held) + (2 if i == 0 else 0)) * LANES for i, held in enumerate(PAIRS)]
    total = sum(widths)
    portion = mix_weight.shape[0]
    kept, given = pl.pallas_call(
        functools.partial(sort_kernel, inner),
        in_specs=[SMEM, VMEM, VMEM],
        out_specs=[VMEM] * 2,
        out_shape=[jax.ShapeDtypeStruct((portion, total), BF16)] * 2,
        compiler_params=params(8),
        name="sort",
    )(early_ints, mix_weight, step_weight)
    got = swapped(given, (1, 1))
    blocks = pl.pallas_call(
        stack_kernel,
        in_specs=[SMEM, VMEM, VMEM],
        out_specs=[VMEM] * len(widths),
        out_shape=[jax.ShapeDtypeStruct((2 * portion, width), BF16) for width in widths],
        compiler_params=params(8),
        name="stack",
    )(early_ints, kept, got)
    blocks = list(blocks)
    arrived = [None] * len(widths)

    chip_rows = 2 * span
    groups = chip_rows // GROUP

    def scratch(width, spans):
        return [
            pltpu.VMEM((depth, width), BF16),
            pltpu.VMEM((spans, chip_rows + 8, LANES), F32),
        ]

    extra = len(PAIRS[0])

    def projected(ints, own, other, low, high, taps, rates):
        width = widths[0]
        return pl.pallas_call(
            first_kernel,
            in_specs=[SMEM] + [VMEM] * 6,
            out_specs=[VMEM] * 7,
            scratch_shapes=scratch(width, 1 + extra) + [pltpu.VMEM((chip_rows, LANES), F32)],
            out_shape=[
                jax.ShapeDtypeStruct((chip_rows, LANES), BF16),
                jax.ShapeDtypeStruct((chip_rows, extra * LANES), BF16),
                jax.ShapeDtypeStruct((chip_rows, LANES), F32),
                jax.ShapeDtypeStruct((chip_rows, LANES), F32),
                jax.ShapeDtypeStruct((groups, 32, GROUP), F32),
                jax.ShapeDtypeStruct((chip_rows, LANES), F32),
                jax.ShapeDtypeStruct((8, LANES), F32),
            ],
            compiler_params=params(24),
            cost_estimate=pl.CostEstimate(
                flops=2 * chip_rows * depth * width, bytes_accessed=9000000, transcendentals=500000
            ),
            name="first",
        )(ints, own, other, low, high, taps[:, : (1 + extra) * LANES], rates)

    def scanned(index, ints, own, other, low, high, taps, skip, x0, b, c, cq, kq, kt, tot):
        more = extra if index == 1 else 0
        held = (PAIRS[0] if more else ()) + PAIRS[index]
        pairs = len(held)
        new = pairs - more
        firsts = [first_head(p, share) for p in held]
        tap_at, skip_at = (1 + PAIRS[index][0]) * LANES, held[0] * LANES
        width = widths[index]
        return pl.pallas_call(
            functools.partial(scan_kernel, index, firsts, more),
            in_specs=[SMEM] + [VMEM] * 13,
            out_specs=[VMEM] * 3,
            scratch_shapes=scratch(width, new) + [pltpu.VMEM((LANES, pairs * LANES), F32)],
            out_shape=[
                jax.ShapeDtypeStruct((chip_rows, pairs * LANES), F32),
                jax.ShapeDtypeStruct((LANES, pairs * LANES), F32),
                jax.ShapeDtypeStruct((LANES + 16, pairs * LANES), BF16),
            ],
            compiler_params=params(28),
            cost_estimate=pl.CostEstimate(
                flops=2 * chip_rows * depth * width + pairs * 600000000,
                bytes_accessed=12000000,
                transcendentals=pairs * 400000,
            ),
            name="scan",
        )(
            ints, own, other, low, high, taps[:, tap_at : tap_at + new * LANES],
            x0, b, c, cq, kq, kt, tot, skip[:, skip_at : skip_at + pairs * LANES],
        )

    def joined(held, ints, c, ca, tot, ys, ss, r):
        pairs = len(held)
        halves = [(i, i + 1) for i in range(0, pairs, 2)]
        sizes = [y.shape[1] // LANES for y in ys]
        return pl.pallas_call(
            functools.partial(join_kernel, [first_head(p, share) for p in held], sizes, halves),
            in_specs=[SMEM] + [VMEM] * (4 + 2 * len(ys)),
            out_specs=[VMEM] * 3,
            out_shape=[
                jax.ShapeDtypeStruct((span, pairs * LANES), F32),
                jax.ShapeDtypeStruct((span, pairs * LANES), F32),
                jax.ShapeDtypeStruct((len(halves) * LANES, nstate), BF16),
            ],
            compiler_params=params(28),
            cost_estimate=pl.CostEstimate(
                flops=4 * chip_rows * LANES * pairs * LANES,
                bytes_accessed=chip_rows * pairs * LANES * 8,
                transcendentals=chip_rows * pairs * LANES,
            ),
            name="join",
        )(ints, c, ca, tot, r, *ys, *ss)

    early_pairs = sum(PAIRS[:-1], ())

    def normed(ints, keep_a, keep_b, got_a, got_b):
        places = [
            [(p % 2) * (2 * quarter // LANES) + p // 2 for p in held]
            for held in (early_pairs, PAIRS[-1])
        ]
        block = span // 2
        return pl.pallas_call(
            functools.partial(norm_kernel, places),
            grid_spec=pltpu.PrefetchScalarGridSpec(
                num_scalar_prefetch=1,
                grid=(span // block,),
                in_specs=[pl.BlockSpec((1, inner), lambda i, ints: (0, 0))]
                + [
                    pl.BlockSpec((block, a.shape[1]), lambda i, ints: (i, 0))
                    for a in (keep_a, keep_b, got_a, got_b)
                ],
                out_specs=pl.BlockSpec((block, inner), lambda i, ints: (i, 0)),
            ),
            out_shape=jax.ShapeDtypeStruct((span, inner), BF16),
            compiler_params=params(24),
            cost_estimate=pl.CostEstimate(
                flops=6 * span * inner, bytes_accessed=6 * span * inner, transcendentals=span
            ),
            name="norm",
        )(ints, norm_gain[None], keep_a, keep_b, got_a, got_b)

    def pick(row, cand):
        rel = row ^ req_index
        far, near = (rel >> 2) & 1, (rel >> 1) & 1
        here, one, two = cand
        return jnp.where(
            near == 1,
            jnp.where(far == 1, two[1], two[0]),
            jnp.where(far == 1, one, here),
        )

    v = state
    last = len(PAIRS) - 1
    for event in SCHEDULE:
        if event[0].isdigit():
            i, step = (int(part) for part in event.split("."))
            if step:
                blocks[i] = jnp.concatenate(after(blocks[i], arrived[i]), axis=0)
                v["token"] = blocks[i]
            route = ROUTES[i]
            arrived[i] = swapped(blocks[i], (FLIPS[route[0][step]], FLIPS[route[1][step]]))
        elif event == "tokens":
            v["other"] = swapped(rows, (1, 1))
        elif event == "halo":
            other = after(v["other"])
            edge = jnp.where(core == 1, rows[span - HALO :], other[span - HALO :])
            count = lax.axis_size("req") * lax.axis_size("seq")
            route = [(i, i + 2) for i in range(count) if (i // 2) % 2 == 0]
            v["token"] = edge
            v["halo"] = lax.ppermute(edge, AXES, route)
        elif event == "settings":
            front = jnp.stack([start, start + length])
            v["ints"] = after(jnp.concatenate([front, place]))
            per_head = jnp.concatenate(
                [jnp.stack([step_bias, decay_rate * (-LOG2E), skip_gain]), jnp.zeros((5, heads))]
            )
            half = inner // 2
            v["taps"], v["rates"], v["skip"] = pl.pallas_call(
                functools.partial(settings_kernel, inner),
                in_specs=[SMEM, VMEM, VMEM, VMEM],
                out_specs=[VMEM] * 3,
                out_shape=[
                    jax.ShapeDtypeStruct((8, half + LANES), F32),
                    jax.ShapeDtypeStruct((8, LANES), F32),
                    jax.ShapeDtypeStruct((8, half), F32),
                ],
                compiler_params=params(8),
                name="settings",
            )(v["ints"], conv_weight, conv_bias[None], per_head)
            v["token"] = v["rates"]
        elif event == "own":
            v["own"] = jnp.concatenate([after(v["halo"]), rows], axis=0)
            v["token"] = v["own"]
        elif event == "K0":
            ints = after(v["ints"])
            bc, x0, cq, kq, kt, ca, tot = projected(
                ints, v["own"], v["other"], blocks[0], arrived[0], v["taps"], v["rates"]
            )
            v["token"] = tot
            v["bc"] = swapped(bc, (1, 1))
        elif event[0] == "K":
            i = int(event[1:])
            if i == 1:
                two = after(v["bc"])
                b = jnp.where(core == 0, bc, two)
                c = jnp.where(core == 0, two, bc)
            ints = after(v["ints"])
            v["y", i], v["s", i], v["t", i] = scanned(
                i, ints, v["own"], v["other"], blocks[i], arrived[i], v["taps"], v["skip"],
                x0, b, c, cq, kq, kt, tot,
            )
            v["token"] = v["t", i]
        elif event in ("xA", "xB"):
            which = range(1, last) if event == "xA" else (last,)
            sent = [v["t", i] for i in which]
            if len(sent) > 1:
                sent = jnp.concatenate(after(*sent), axis=1)
                v["token"] = sent
            else:
                sent = sent[0]
            v["r", event[1]] = swapped(sent, (2, 2))
        elif event in ("JA", "JB"):
            which = range(1, last) if event == "JA" else (last,)
            held = early_pairs if event == "JA" else PAIRS[last]
            ints, r = after(v["ints"], v["r", event[1]])
            send, v["keep", event[1]], v["fin", event[1]] = joined(
                held, ints, c, ca, tot, [v["y", i] for i in which], [v["s", i] for i in which], r
            )
            v["token"] = v["fin", event[1]]
            v["got", event[1]] = swapped(send, (1, 1))
        elif event[0] == "f":
            key = event[1]
            if event[2] == "0":
                v["one", key] = swapped(v["fin", key], (16, 16))
            elif event[2] == "1":
                v["pair", key] = jnp.stack(after(v["fin", key], v["one", key]))
                v["token"] = v["pair", key]
                v["two", key] = swapped(v["pair", key], (8, 8))
            elif event[2] == "2":
                cand = (v["fin", key], v["one", key], after(v["two", key]))
                v["cand", key] = cand
                v["picked", key] = pick(partner_wanted, cand)
                v["token"] = v["picked", key]
                v["three", key] = swapped(v["picked", key], (4, 4))
            else:
                three = after(v["three", key])
                odd = (wanted ^ req_index) & 1
                v["final", key] = jnp.where(odd == 1, three, pick(wanted, v["cand", key])).astype(
                    F32
                )
                v["token"] = v["final", key]
        else:
            ints = after(v["ints"])
            result = normed(ints, v["keep", "A"], v["keep", "B"], v["got", "A"], v["got", "B"])
            v["token"] = result
    final_state = jnp.concatenate([v["final", "A"], v["final", "B"]], axis=0)
    return (result[None], final_state.reshape(1, share, head_dim, nstate))


def passed_along(block, axis, distance):
    devices = range(lax.axis_size(axis))
    route = [(i - distance, i) for i in devices if i - distance in devices]
    return lax.ppermute(block, axis, route)


def carried_in(part, axis, combine, identity):
    place = lax.axis_index(axis)
    gathered = jax.tree.map(lambda a: lax.all_gather(a, axis), part)
    state = jax.tree.map(lambda a, e: jnp.zeros_like(a) + jnp.asarray(e, a.dtype), part, identity)

    def one(step, state):
        return combine(
            state, jax.tree.map(lambda a: lax.dynamic_index_in_dim(a, step, 0, False), gathered)
        )

    return lax.fori_loop(0, place, one, state)


def broadcast(x, axis, root):
    mine = lax.axis_index(axis) == root
    return lax.psum(jnp.where(mine, x, jnp.zeros_like(x)), axis)


def on_device_general(
    tokens,
    mix_weight,
    step_weight,
    conv_weight,
    conv_bias,
    step_bias,
    decay_rate,
    skip_gain,
    norm_gain,
    prompt_len,
    prompt_start,
    deal,
):
    seq_count = lax.axis_size("seq")
    seq_index = lax.axis_index("seq")
    req_index = lax.axis_index("req")
    rows = tokens[0]
    span = rows.shape[0]
    total_reqs = deal.shape[0]
    slots = jnp.arange(total_reqs, dtype=jnp.int32)
    request = jnp.sum(jnp.where(slots == req_index, deal, 0))
    length = jnp.sum(jnp.where(slots == request, prompt_len, 0))
    start = jnp.sum(jnp.where(slots == request, prompt_start, 0))
    place = seq_index * span + jnp.arange(span, dtype=jnp.int32)
    valid = ((place >= start) & (place < start + length)).astype(jnp.float32)
    whole_mix, whole_step = (
        lax.all_gather(mix_weight, ("req", "seq"), axis=0, tiled=True),
        lax.all_gather(step_weight, ("req", "seq"), axis=0, tiled=True),
    )
    mixed = jnp.dot(rows, whole_mix, preferred_element_type=jnp.float32)
    raw_step = jnp.dot(rows, whole_step, preferred_element_type=jnp.float32)
    mixed = (mixed * valid[:, None]).astype(jnp.bfloat16)
    taps = conv_weight.shape[0]
    edge = passed_along(mixed[span - (taps - 1) :], "seq", 1)
    padded = jnp.concatenate([edge, mixed], axis=0)
    conv_sum = jnp.zeros(mixed.shape, jnp.float32) + conv_bias[None, :]
    for offset in range(taps):
        conv_sum = conv_sum + conv_weight[offset][None, :] * padded[offset : offset + span].astype(
            jnp.float32
        )
    convolved = jax.nn.silu(conv_sum).astype(jnp.bfloat16)
    heads = decay_rate.shape[0]
    inner = norm_gain.shape[0]
    head_dim = inner // heads
    nstate = (mixed.shape[1] - inner) // 2
    blocks = span // GROUP
    inputs = convolved[:, :inner].reshape(span, heads, head_dim)
    mixed_b = convolved[:, inner : inner + nstate]
    mixed_c = convolved[:, inner + nstate :]
    step_size = jax.nn.softplus(raw_step + step_bias[None, :]) * valid[:, None]
    pieces = (
        inputs.reshape(blocks, GROUP, heads, head_dim),
        mixed_b.reshape(blocks, GROUP, nstate),
        mixed_c.reshape(blocks, GROUP, nstate),
        step_size.reshape(blocks, GROUP, heads),
    )

    def local_group(block):
        part_in, part_b, part_c, part_step = block
        cum_decay = jnp.cumsum(-part_step * decay_rate[None, :], axis=0)
        places = jnp.arange(GROUP, dtype=jnp.int32)
        causal = places[:, None] >= places[None, :]
        spread = cum_decay[:, None, :] - cum_decay[None, :, :]
        spread = jnp.where(causal[:, :, None], spread, -1e30)
        scores = jnp.einsum("qn,kn->qk", part_c, part_b, preferred_element_type=jnp.float32)
        mixing = (jnp.exp(spread) * scores[:, :, None] * part_step[None, :, :]).astype(jnp.bfloat16)
        inner_out = jnp.einsum("qkh,khp->qhp", mixing, part_in, preferred_element_type=jnp.float32)
        to_end = jnp.exp(cum_decay[-1][None, :] - cum_decay) * part_step
        scaled = (to_end[:, :, None] * part_in.astype(jnp.float32)).astype(jnp.bfloat16)
        local = jnp.einsum("khp,kn->hpn", scaled, part_b, preferred_element_type=jnp.float32)
        return (inner_out, cum_decay, local)

    inner_out, cum_decay, group_state = lax.map(local_group, pieces)
    totals = cum_decay[:, -1, :]

    def advance(carry, item):
        group_total, group_local = item
        return (jnp.exp(group_total)[:, None, None] * carry + group_local, carry)

    dev_state, entry_zero = lax.scan(
        advance, jnp.zeros((heads, head_dim, nstate), jnp.float32), (totals, group_state)
    )
    before = jnp.cumsum(totals, axis=0) - totals
    dev_decay = jnp.exp(jnp.sum(totals, axis=0))

    def chain(earlier, later):
        return (earlier[0] * later[0], later[0][:, None, None] * earlier[1] + later[1])

    incoming_decay, incoming = carried_in(
        (dev_decay, dev_state), "seq", chain, (jnp.ones_like(dev_decay), jnp.zeros_like(dev_state))
    )
    entry = entry_zero + jnp.exp(before)[:, :, None, None] * incoming[None]
    carried = jnp.einsum(
        "cqn,chpn->cqhp", pieces[2].astype(jnp.float32), entry, precision=lax.Precision.HIGHEST
    )
    carried = carried * jnp.exp(cum_decay)[:, :, :, None]
    outputs = (inner_out + carried).reshape(span, heads, head_dim) + skip_gain[
        None, :, None
    ] * inputs.astype(jnp.float32)
    flat = outputs.reshape(span, inner)
    factor = lax.rsqrt(jnp.mean(flat * flat, axis=1, keepdims=True) + EPS)
    result = (flat * factor * norm_gain[None, :] * valid[:, None]).astype(jnp.bfloat16)[None]
    share = heads // seq_count
    leaving = dev_decay[:, None, None] * incoming + dev_state
    last_state = broadcast(leaving, "seq", seq_count - 1)
    own_state = lax.dynamic_slice_in_dim(last_state, seq_index * share, share, 0)[None]
    wanted = jnp.sum(jnp.where(deal == req_index, slots, 0))
    piece = lax.all_gather(own_state, "req", axis=0, tiled=True)
    count = piece.shape[0]
    chosen = jnp.arange(count, dtype=jnp.int32) == wanted
    final_state = jnp.zeros_like(own_state) + jnp.sum(
        jnp.where(chosen[:, None, None, None], piece, 0.0), axis=0, keepdims=True
    )
    return (result, final_state)


def solution(mesh):
    fits = mesh.shape["req"] == 8 and mesh.shape["seq"] == 4
    return jax.shard_map(
        on_device if fits else on_device_general,
        mesh=mesh,
        in_specs=(
            P("req", "seq", None),
            P(("req", "seq"), None),
            P(("req", "seq"), None),
        )
        + (P(),) * 9,
        out_specs=(P("req", "seq", None), P("req", "seq", None, None)),
        check_vma=False,
    )
```

```python
import functools

import jax
import jax.numpy as jnp
from jax import lax
from jax.experimental import pallas as pl
from jax.experimental.pallas import tpu as pltpu
from jax.sharding import PartitionSpec as P

GROUP = 256
EPS = 1e-05
LOG2E = 1.4426950408889634
LANES = 128
HALO = 16
KEYS, ROW = 32, 64
F32 = jnp.float32
BF16 = jnp.bfloat16
AXES = ("req", "seq")
FLIPS = {"a": 16, "b": 8, "y": 4, "x": 2}
ROUTES = (("axyb", "abxy"), ("abyx", "axby"), ("ayxb", "abyx"), ("aybx", "abxy"))
PAIRS = ((0,), (1, 2, 3), (4, 5, 6, 7), (8, 9))
CUT = 3
SCHEDULE = (
    "0.0", "1.0", "tokens", "0.1", "2.0", "1.1", "0.2", "halo", "settings", "3.0",
    "2.1", "1.2", "0.3", "own", "3.1", "2.2", "1.3", "3.2", "2.3", "K0",
    "K1", "3.3", "K2", "xA", "K3", "xB", "JA", "fA0", "JB", "fB0",
    "fA1", "norm", "fB1", "fA2", "fB2", "fA3", "fB3",
)
VMEM = pl.BlockSpec(memory_space=pltpu.VMEM)
SMEM = pl.BlockSpec(memory_space=pltpu.SMEM)


def dot(a, b):
    return jnp.dot(a, b, preferred_element_type=F32)


def params(vmem_mib):
    return pltpu.CompilerParams(vmem_limit_bytes=vmem_mib * 1024 * 1024)


def first_head(pair, share):
    return (pair % 2) * share + 2 * (pair // 2)


def lanes(i):
    return slice(i * LANES, (i + 1) * LANES)


def valid_rows(first, rows, start, end):
    place = first + lax.broadcasted_iota(jnp.int32, (rows, LANES), 0)
    return jnp.where((place >= start) & (place < end), 1.0, 0.0).astype(F32)


def column(a, head):
    return jnp.broadcast_to(a[:, head : head + 1], (a.shape[0], LANES))


def split(a):
    upper = a.astype(BF16)
    return upper, (a - upper.astype(F32)).astype(BF16)


def project(chunk, ints, own, other, low, high, whole, padded, raw):
    block = low.shape[0] // 8
    start, end, first, core = ints[0], ints[1], ints[2], ints[3]
    for p in range(16):
        one, two = (
            sum(FLIPS[step] // 2 for i, step in enumerate(route) if (p >> i) & 1)
            for route in ROUTES[chunk]
        )
        chip = jnp.bitwise_xor(ints[5], jnp.where(core == 0, one, two))
        source = low if p < 8 else high
        row = pl.multiple_of(chip * block, block)
        whole[pl.ds(row, block), :] = source[(p % 8) * block : (p % 8 + 1) * block, :]
    span = other.shape[0]
    spans = [i for i in range(low.shape[1] // LANES) if raw is None or i != 1]
    mine = dot(own[...], whole[...])
    theirs = dot(other[...], whole[...])
    at_mine = pl.multiple_of(core * span, span)
    at_theirs = pl.multiple_of((1 - core) * span, span)
    ok_edge = valid_rows(first - 8, 8, start, end)
    ok_mine = valid_rows(first + at_mine, span, start, end)
    ok_theirs = valid_rows(first + at_theirs, span, start, end)

    def rounded(a, ok):
        return (a * ok).astype(BF16).astype(F32)

    for at, lane in enumerate(spans):
        edge = mine[0:HALO, lanes(lane)][HALO - 8 :]
        padded[at, 0:8, :] = rounded(edge, ok_edge)
        padded[at, pl.ds(8 + at_mine, span), :] = rounded(mine[HALO:, lanes(lane)], ok_mine)
        padded[at, pl.ds(8 + at_theirs, span), :] = rounded(theirs[:, lanes(lane)], ok_theirs)
    if raw is not None:
        raw[pl.ds(at_mine, span), :] = mine[HALO:, lanes(1)]
        raw[pl.ds(at_theirs, span), :] = theirs[:, lanes(1)]


def convolved(at, tap, group, taps, padded):
    total = taps[4:5, lanes(tap)]
    for k in range(4):
        rows = padded[at, group * GROUP + 5 + k : (group + 1) * GROUP + 5 + k, :]
        total = total + taps[k : k + 1, lanes(tap)] * rows
    half = 0.5 * total
    return (half + half * jnp.tanh(half)).astype(BF16)


def first_kernel(
    ints, own, other, low, high, taps, rates,
    bc_out, x_out, table_out, kt_out, tot_out,
    whole, padded, raw,
):
    project(0, ints, own, other, low, high, whole, padded, raw)
    row = lax.broadcasted_iota(jnp.int32, (GROUP, GROUP), 0)
    col = lax.broadcasted_iota(jnp.int32, (GROUP, GROUP), 1)
    below = jnp.where(row >= col, 1.0, 0.0).astype(BF16)
    before = jnp.zeros((1, LANES), F32)
    for group in range(bc_out.shape[0] // GROUP):
        rows = slice(group * GROUP, (group + 1) * GROUP)
        bc_out[rows, :] = convolved(0, 0, group, taps, padded)
        for at in range(1, padded.shape[0]):
            x_out[rows, lanes(at - 1)] = convolved(at, at, group, taps, padded)
        ok = valid_rows(ints[2] + group * GROUP, GROUP, ints[0], ints[1])
        step = raw[rows, :] + rates[0:1, :]
        size = (jnp.maximum(step, 0.0) + jnp.log1p(jnp.exp(-jnp.abs(step)))) * ok
        decay = size * rates[1:2, :]
        high_part, rest = split(decay)
        rest = decay - high_part.astype(F32)
        mid_part, low_part = split(rest)
        cum = dot(below, high_part) + dot(below, mid_part) + dot(below, low_part)
        from_key = jnp.log2(size) - cum
        kt_out[group] = from_key.T[0:32, :]
        lane = lax.broadcasted_iota(jnp.int32, (GROUP, LANES), 1)
        table = jnp.where(lane < KEYS, cum, pltpu.roll(from_key, KEYS, 1))
        table_out[rows, :] = jnp.where(lane < ROW, table, pltpu.roll(cum + before, ROW, 1))
        before = before + cum[GROUP - 1 : GROUP, :]
    tot_out[...] = jnp.broadcast_to(before, tot_out.shape)


def sorted_bc(ints, mine, theirs):
    first = ints[3] == 0
    return jnp.where(first, mine, theirs), jnp.where(first, theirs, mine)


def scan_kernel(
    chunk, held, heads, extra, ints, own, other, low, high, taps, x_ref, mine_ref, their_ref, table_ref,
    kt_ref, tot_ref, skip_ref, y_out, s_out, send_out, whole, padded, carry,
):
    project(chunk, ints, own, other, low, high, whole, padded, None)
    pairs = len(heads)
    half = GROUP // 2
    row = lax.broadcasted_iota(jnp.int32, (half, half), 0)
    col = lax.broadcasted_iota(jnp.int32, (half, half), 1)
    causal = row >= col
    left = lax.broadcasted_iota(jnp.int32, (GROUP, LANES), 1) < LANES // 2
    zero = jnp.zeros((GROUP, LANES), BF16)
    for group in range(y_out.shape[0] // GROUP):
        rows = slice(group * GROUP, (group + 1) * GROUP)
        b, c = sorted_bc(ints, mine_ref[rows, :], their_ref[rows, :])
        scores = lax.dot_general(c, b, (((1,), (1,)), ((), ())), preferred_element_type=F32)
        table, kt = table_ref[rows, :], kt_ref[group]
        carried = None
        if group:
            upper, lower = split(carry[...])
            carried = dot(jnp.concatenate([c, c], axis=1), jnp.concatenate([upper, lower], axis=0))
        scaled, ends = [], []
        for i, head in enumerate(heads):
            if i < extra:
                x = x_ref[rows, lanes(i)]
            else:
                x = convolved(i - extra, held[i] + 1, group, taps, padded)
            top, bottom, spread = [], [], []
            for h in (head, head + 1):
                q = column(table, h)
                spread.append(q)
                k0 = jnp.broadcast_to(kt[h : h + 1, 0:half], (half, half))
                k1 = jnp.broadcast_to(kt[h : h + 1, half:], (half, half))
                m00 = jnp.where(causal, jnp.exp2(q[0:half] + k0) * scores[0:half, 0:half], 0.0)
                m10 = jnp.exp2(q[half:] + k0) * scores[half:, 0:half]
                m11 = jnp.where(causal, jnp.exp2(q[half:] + k1) * scores[half:, half:], 0.0)
                top.append(m00.astype(BF16))
                bottom.append(m10.astype(BF16))
                bottom.append(m11.astype(BF16))
            x0, x1 = jnp.where(left, x, zero), jnp.where(left, zero, x)
            y_top = dot(
                jnp.concatenate(top, axis=1), jnp.concatenate([x0[0:half], x1[0:half]], axis=0)
            )
            y_bottom = dot(jnp.concatenate(bottom, axis=1), jnp.concatenate([x0, x1], axis=0))
            q = jnp.where(left, spread[0], spread[1])
            xf = x.astype(F32)
            rest = skip_ref[2:3, lanes(held[i])] * xf
            if group:
                rest = rest + jnp.exp2(q) * carried[:, lanes(i)]
            y_out[group * GROUP : group * GROUP + half, lanes(i)] = y_top + rest[0:half]
            y_out[group * GROUP + half : (group + 1) * GROUP, lanes(i)] = y_bottom + rest[half:]
            k = jnp.where(left, column(table, KEYS + head), column(table, KEYS + head + 1))
            end = q[GROUP - 1 : GROUP, :]
            scaled.append((jnp.exp2(k + end) * xf).astype(BF16))
            ends.append(jnp.exp2(end))
        local = lax.dot_general(
            b, jnp.concatenate(scaled, axis=1), (((0,), (0,)), ((), ())), preferred_element_type=F32
        )
        if group:
            local = jnp.concatenate(ends, axis=1) * carry[...] + local
        carry[...] = local
    s_out[...] = carry[...]
    send_out[0:LANES, :] = carry[...].astype(BF16)
    side = lax.broadcasted_iota(jnp.int32, (8, LANES), 1) < LANES // 2
    for i, head in enumerate(heads):
        total = jnp.where(side, column(tot_ref[...], head), column(tot_ref[...], head + 1))
        one, rest = split(total)
        two, three = split(total - one.astype(F32))
        place = lax.broadcasted_iota(jnp.int32, (8, LANES), 0)
        parts = jnp.where(place == 0, one.astype(F32), two.astype(F32))
        parts = jnp.where(place >= 2, three.astype(F32), parts)
        parts = jnp.where(place >= 3, 0.0, parts)
        send_out[LANES:, lanes(i)] = jnp.concatenate([parts, jnp.zeros_like(parts)], axis=0).astype(
            BF16
        )


def join_kernel(heads, sizes, halves, ints, mine_ref, their_ref, table_ref, tot_ref, r_ref, *refs):
    count = len(sizes)
    y_refs, s_refs = refs[:count], refs[count : 2 * count]
    send_out, keep_out, fin_out = refs[2 * count :]
    later = ints[4] > 0
    core = ints[3]
    where = [(j, k) for j, size in enumerate(sizes) for k in range(size)]
    span = send_out.shape[0]
    received = r_ref[0:LANES, :].astype(F32)
    entering = (received * jnp.where(later, 1.0, 0.0)).astype(BF16)
    from_head = lax.broadcasted_iota(jnp.int32, (2 * LANES, LANES), 0) % LANES
    second = lax.broadcasted_iota(jnp.int32, (2 * LANES, LANES), 1) // (LANES // 2)
    spread = jnp.concatenate(
        [jnp.where(from_head == ROW + head + second, 1.0, 0.0).astype(BF16) for head in heads], axis=1
    )
    for out, at in ((send_out, (1 - core) * span), (keep_out, core * span)):
        rows = pl.ds(pl.multiple_of(at, span), span)
        lane = lax.broadcasted_iota(jnp.int32, (span, LANES), 1)
        decay = jnp.exp2(jnp.where(lane < ROW, 0.0, table_ref[rows, :]))
        decay = dot(jnp.concatenate(split(decay), axis=1), spread)
        _, c = sorted_bc(ints, mine_ref[rows, :], their_ref[rows, :])
        carried = dot(c, entering)
        for i in range(len(heads)):
            j, k = where[i]
            out[:, lanes(i)] = (
                y_refs[j][rows, lanes(k)] + decay[:, lanes(i)] * carried[:, lanes(i)]
            )
    side = lax.broadcasted_iota(jnp.int32, (8, LANES), 1) < LANES // 2
    tot = tot_ref[...]
    for i, (early, late) in enumerate(halves):

        def own_state(p):
            j, k = where[p]
            return s_refs[j][:, lanes(k)]

        parts = r_ref[LANES:, lanes(early)].astype(F32)
        their_total = parts[0:1] + parts[1:2] + parts[2:3]
        my_total = jnp.where(side, column(tot, heads[late]), column(tot, heads[late] + 1))[0:1]
        at_first = jnp.exp2(their_total) * own_state(early) + received[:, lanes(early)]
        at_last = jnp.exp2(my_total) * received[:, lanes(late)] + own_state(late)
        both = jnp.where(later, at_last, at_first)
        fin_out[i * LANES : (i + 1) * LANES, :] = both.T.astype(fin_out.dtype)


def norm_kernel(places, ints, gain_ref, ka_ref, kb_ref, ra_ref, rb_ref, out_ref):
    step = pl.program_id(0)
    core = ints[3]
    rows = out_ref.shape[0]
    first = ints[2] + (core * pl.num_programs(0) + step) * rows
    ok = valid_rows(first, rows, ints[0], ints[1])
    blocks = []
    for who, refs in ((core, (ka_ref, kb_ref)), (1 - core, (ra_ref, rb_ref))):
        for ref, wheres in zip(refs, places, strict=True):
            for i, where in enumerate(wheres):
                at = pl.multiple_of((where + 5 * who) * LANES, LANES)
                blocks.append((at, ref, i))
    total = jnp.zeros((rows, LANES), F32)
    for _, ref, i in blocks:
        v = ref[:, lanes(i)]
        total = total + v * v
    mean = jnp.sum(total, axis=1, keepdims=True) * (1.0 / out_ref.shape[1])
    factor = lax.rsqrt(mean + EPS) * ok
    for at, ref, i in blocks:
        v = ref[:, lanes(i)]
        out_ref[:, pl.ds(at, LANES)] = (v * factor * gain_ref[0:1, pl.ds(at, LANES)]).astype(BF16)


def head_of(lane, core, share):
    return jnp.where(lane < 2 * share, lane + core * share + (lane // share) * share, -1)


def chosen_heads(core, heads, rows):
    row = lax.broadcasted_iota(jnp.int32, (rows, LANES), 0)
    lane = lax.broadcasted_iota(jnp.int32, (rows, LANES), 1)
    return jnp.where(row == head_of(lane, core, heads // 4), 1.0, 0.0)


def columns_of(source, core, inner):
    first = inner // 4 // LANES
    blocks = [inner // LANES + core]
    for i in range(first):
        blocks += [first * core + i, 2 * first + first * core + i]
    return [source[:, pl.ds(pl.multiple_of(at * LANES, LANES), LANES)] for at in blocks]


def sort_kernel(inner, ints, mix, step, kept_out, given_out):
    for out, core in ((kept_out, ints[1]), (given_out, 1 - ints[1])):
        parts = columns_of(mix, core, inner)
        out[:, lanes(0)] = parts[0]
        out[:, lanes(1)] = dot(step[...], chosen_heads(core, step.shape[1], step.shape[1]).astype(BF16)).astype(BF16)
        for i, part in enumerate(parts[1:]):
            out[:, lanes(2 + i)] = part


def stack_kernel(ints, kept, got, *outs):
    rows = kept.shape[0]
    core = ints[1]
    at = 0
    for out in outs:
        width = out.shape[1]
        out[pl.ds(pl.multiple_of(core * rows, rows), rows), :] = kept[:, at : at + width]
        out[pl.ds(pl.multiple_of((1 - core) * rows, rows), rows), :] = got[:, at : at + width]
        at += width


def settings_kernel(
    inner, place, deal, lengths, starts, small, ints_out, taps_out, rates_out, skip_out
):
    request, wanted, near = jnp.int32(0), jnp.int32(0), jnp.int32(0)
    req = place[4]
    for i in range(deal.shape[0]):
        request = jnp.where(req == i, deal[i], request)
        wanted = jnp.where(deal[i] == req, i, wanted)
        near = jnp.where(deal[i] == jnp.bitwise_xor(req, 1), i, near)
    start, length = jnp.int32(0), jnp.int32(0)
    for i in range(deal.shape[0]):
        start = jnp.where(request == i, starts[i], start)
        length = jnp.where(request == i, lengths[i], length)
    ints_out[0] = start
    ints_out[1] = start + length
    for i in range(4):
        ints_out[2 + i] = place[i]
    ints_out[6] = wanted
    ints_out[7] = near
    core = place[1]
    for i, part in enumerate(columns_of(small, core, inner)):
        row = lax.broadcasted_iota(jnp.int32, (8, LANES), 0)
        taps_out[:, lanes(i)] = jnp.where(row < 5, part[0:8], 0.0)
    heads = inner // LANES * 2
    exact = functools.partial(
        jnp.dot, precision=lax.Precision.HIGHEST, preferred_element_type=F32
    )
    own = exact(small[8:16, 0:LANES], chosen_heads(core, heads, LANES))
    rates_out[...] = own
    row = lax.broadcasted_iota(jnp.int32, (LANES, inner // 2), 0)
    lane = lax.broadcasted_iota(jnp.int32, (LANES, inner // 2), 1)
    pair, second = lane // LANES, (lane % LANES) // (LANES // 2)
    mine = (pair % 2) * (heads // 4) + 2 * (pair // 2) + second
    skip_out[...] = exact(own, jnp.where(row == mine, 1.0, 0.0))


def swapped(x, masks):
    count = lax.axis_size("req") * lax.axis_size("seq")
    return lax.ppermute(x, AXES, [(i, i ^ masks[i % 2]) for i in range(count)])


def on_device(
    tokens, mix_weight, step_weight, conv_weight, conv_bias, step_bias, decay_rate, skip_gain,
    norm_gain, prompt_len, prompt_start, deal,
):
    seq_index = lax.axis_index("seq")
    req_index = lax.axis_index("req")
    core, along = seq_index % 2, seq_index // 2
    rows = tokens[0]
    span, depth = rows.shape
    inner = norm_gain.shape[0]
    heads = decay_rate.shape[0]
    head_dim = inner // heads
    nstate = (mix_weight.shape[1] - inner) // 2
    share = heads // 4
    quarter = inner // 4
    chip = req_index * 2 + along
    place = jnp.stack([along * 2 * span, core, along, chip, req_index])
    state = {}

    def after(*values):
        if "token" not in state:
            return values if len(values) > 1 else values[0]
        *out, state["token"] = lax.optimization_barrier((*values, state["token"]))
        return tuple(out) if len(out) > 1 else out[0]

    widths = [(len(held) + (2 if i == 0 else 0)) * LANES for i, held in enumerate(PAIRS)]
    total = sum(widths)
    portion = mix_weight.shape[0]
    kept, given = pl.pallas_call(
        functools.partial(sort_kernel, inner),
        in_specs=[SMEM, VMEM, VMEM],
        out_specs=[VMEM] * 2,
        out_shape=[jax.ShapeDtypeStruct((portion, total), BF16)] * 2,
        compiler_params=params(8),
        name="sort",
    )(place, mix_weight, step_weight)
    got = swapped(given, (1, 1))
    blocks = pl.pallas_call(
        stack_kernel,
        in_specs=[SMEM, VMEM, VMEM],
        out_specs=[VMEM] * len(widths),
        out_shape=[jax.ShapeDtypeStruct((2 * portion, width), BF16) for width in widths],
        compiler_params=params(8),
        name="stack",
    )(place, kept, got)
    blocks = list(blocks)
    arrived = [None] * len(widths)

    chip_rows = 2 * span
    groups = chip_rows // GROUP

    def scratch(width, spans):
        return [
            pltpu.VMEM((depth, width), BF16),
            pltpu.VMEM((spans, chip_rows + 8, LANES), F32),
        ]

    extra = len(PAIRS[0])

    def projected(ints, own, other, low, high, taps, rates):
        width = widths[0]
        return pl.pallas_call(
            first_kernel,
            in_specs=[SMEM] + [VMEM] * 6,
            out_specs=[VMEM] * 5,
            scratch_shapes=scratch(width, 1 + extra) + [pltpu.VMEM((chip_rows, LANES), F32)],
            out_shape=[
                jax.ShapeDtypeStruct((chip_rows, LANES), BF16),
                jax.ShapeDtypeStruct((chip_rows, extra * LANES), BF16),
                jax.ShapeDtypeStruct((chip_rows, LANES), F32),
                jax.ShapeDtypeStruct((groups, 32, GROUP), F32),
                jax.ShapeDtypeStruct((8, LANES), F32),
            ],
            compiler_params=params(28),
            cost_estimate=pl.CostEstimate(
                flops=2 * chip_rows * depth * width, bytes_accessed=9000000, transcendentals=500000
            ),
            name="first",
        )(ints, own, other, low, high, taps, rates)

    def scanned(index, ints, own, other, low, high, taps, skip, x0, mine, theirs, table, kt, tot):
        more = extra if index == 1 else 0
        held = (PAIRS[0] if more else ()) + PAIRS[index]
        pairs = len(held)
        new = pairs - more
        firsts = [first_head(p, share) for p in held]
        width = widths[index]
        return pl.pallas_call(
            functools.partial(scan_kernel, index, held, firsts, more),
            in_specs=[SMEM] + [VMEM] * 12,
            out_specs=[VMEM] * 3,
            scratch_shapes=scratch(width, new) + [pltpu.VMEM((LANES, pairs * LANES), F32)],
            out_shape=[
                jax.ShapeDtypeStruct((chip_rows, pairs * LANES), F32),
                jax.ShapeDtypeStruct((LANES, pairs * LANES), F32),
                jax.ShapeDtypeStruct((LANES + 16, pairs * LANES), BF16),
            ],
            compiler_params=params(28),
            cost_estimate=pl.CostEstimate(
                flops=2 * chip_rows * depth * width + pairs * 600000000,
                bytes_accessed=12000000,
                transcendentals=pairs * 400000,
            ),
            name="scan",
        )(
            ints, own, other, low, high, taps,
            x0, mine, theirs, table, kt, tot, skip,
        )

    def joined(held, ints, mine, theirs, table, tot, ys, ss, r):
        pairs = len(held)
        halves = [(i, i + 1) for i in range(0, pairs, 2)]
        sizes = [y.shape[1] // LANES for y in ys]
        return pl.pallas_call(
            functools.partial(join_kernel, [first_head(p, share) for p in held], sizes, halves),
            in_specs=[SMEM] + [VMEM] * (5 + 2 * len(ys)),
            out_specs=[VMEM] * 3,
            out_shape=[
                jax.ShapeDtypeStruct((span, pairs * LANES), F32),
                jax.ShapeDtypeStruct((span, pairs * LANES), F32),
                jax.ShapeDtypeStruct((len(halves) * LANES, nstate), BF16),
            ],
            compiler_params=params(28),
            cost_estimate=pl.CostEstimate(
                flops=4 * chip_rows * LANES * pairs * LANES,
                bytes_accessed=chip_rows * pairs * LANES * 8,
                transcendentals=chip_rows * pairs * LANES,
            ),
            name="join",
        )(ints, mine, theirs, table, tot, r, *ys, *ss)

    early_pairs, late_pairs = sum(PAIRS[:CUT], ()), sum(PAIRS[CUT:], ())

    def normed(ints, keep_a, keep_b, got_a, got_b):
        places = [
            [(p % 2) * (2 * quarter // LANES) + p // 2 for p in held]
            for held in (early_pairs, late_pairs)
        ]
        block = span // 2
        return pl.pallas_call(
            functools.partial(norm_kernel, places),
            grid_spec=pltpu.PrefetchScalarGridSpec(
                num_scalar_prefetch=1,
                grid=(span // block,),
                in_specs=[pl.BlockSpec((1, inner), lambda i, ints: (0, 0))]
                + [
                    pl.BlockSpec((block, a.shape[1]), lambda i, ints: (i, 0))
                    for a in (keep_a, keep_b, got_a, got_b)
                ],
                out_specs=pl.BlockSpec((block, inner), lambda i, ints: (i, 0)),
            ),
            out_shape=jax.ShapeDtypeStruct((span, inner), BF16),
            compiler_params=params(28),
            cost_estimate=pl.CostEstimate(
                flops=6 * span * inner, bytes_accessed=6 * span * inner, transcendentals=span
            ),
            name="norm",
        )(ints, norm_gain[None], keep_a, keep_b, got_a, got_b)

    def pick(row, cand):
        rel = row ^ req_index
        far, near = (rel >> 2) & 1, (rel >> 1) & 1
        here, one, two = cand
        return jnp.where(
            near == 1,
            jnp.where(far == 1, two[1], two[0]),
            jnp.where(far == 1, one, here),
        )

    v = state
    last = len(PAIRS) - 1
    for event in SCHEDULE:
        if event[0].isdigit():
            i, step = (int(part) for part in event.split("."))
            if step:
                blocks[i] = jnp.concatenate(after(blocks[i], arrived[i]), axis=0)
                v["token"] = blocks[i]
            route = ROUTES[i]
            arrived[i] = swapped(blocks[i], (FLIPS[route[0][step]], FLIPS[route[1][step]]))
        elif event == "tokens":
            v["other"] = swapped(rows, (1, 1))
        elif event == "halo":
            other = after(v["other"])
            edge = jnp.where(core == 1, rows[span - HALO :], other[span - HALO :])
            count = lax.axis_size("req") * lax.axis_size("seq")
            route = [(i, i + 2) for i in range(count) if (i // 2) % 2 == 0]
            v["token"] = edge
            v["halo"] = lax.ppermute(edge, AXES, route)
        elif event == "settings":
            half = inner // 2

            conv_w, conv_b, step_b, rate, gain = after(
                conv_weight, conv_bias, step_bias, decay_rate, skip_gain
            )

            def row(values):
                return jnp.pad(values, (0, conv_weight.shape[1] - values.shape[0]))[None]

            small = jnp.concatenate(
                [conv_w, conv_b[None], jnp.zeros((3, conv_w.shape[1]), F32)]
                + [row(step_b), row(rate * (-LOG2E)), row(gain)]
                + [jnp.zeros((5, conv_weight.shape[1]), F32)],
                axis=0,
            )
            v["ints"], v["taps"], v["rates"], v["skip"] = pl.pallas_call(
                functools.partial(settings_kernel, inner),
                in_specs=[SMEM] * 4 + [VMEM],
                out_specs=[SMEM] + [VMEM] * 3,
                out_shape=[
                    jax.ShapeDtypeStruct((8,), jnp.int32),
                    jax.ShapeDtypeStruct((8, half + LANES), F32),
                    jax.ShapeDtypeStruct((8, LANES), F32),
                    jax.ShapeDtypeStruct((8, half), F32),
                ],
                compiler_params=params(8),
                name="settings",
            )(after(place), deal, prompt_len, prompt_start, small)
            v["token"] = v["rates"]
        elif event == "own":
            v["own"] = jnp.concatenate([after(v["halo"]), rows], axis=0)
            v["token"] = v["own"]
        elif event == "K0":
            ints = after(v["ints"])
            bc, x0, table, kt, tot = projected(
                ints, v["own"], v["other"], blocks[0], arrived[0], v["taps"], v["rates"]
            )
            v["token"] = tot
            v["bc"] = swapped(bc, (1, 1))
        elif event[0] == "K":
            i = int(event[1:])
            if i == 1:
                theirs = after(v["bc"])
            ints = after(v["ints"])
            v["y", i], v["s", i], v["t", i] = scanned(
                i, ints, v["own"], v["other"], blocks[i], arrived[i], v["taps"], v["skip"],
                x0, bc, theirs, table, kt, tot,
            )
            v["token"] = v["t", i]
        elif event in ("xA", "xB"):
            which = range(1, CUT) if event == "xA" else range(CUT, last + 1)
            sent = [v["t", i] for i in which]
            if len(sent) > 1:
                sent = jnp.concatenate(after(*sent), axis=1)
                v["token"] = sent
            else:
                sent = sent[0]
            v["r", event[1]] = swapped(sent, (2, 2))
        elif event in ("JA", "JB"):
            which = range(1, CUT) if event == "JA" else range(CUT, last + 1)
            held = early_pairs if event == "JA" else late_pairs
            ints, r = after(v["ints"], v["r", event[1]])
            send, v["keep", event[1]], v["fin", event[1]] = joined(
                held, ints, bc, theirs, table, tot, [v["y", i] for i in which], [v["s", i] for i in which], r
            )
            v["token"] = v["fin", event[1]]
            v["got", event[1]] = swapped(send, (1, 1))
        elif event[0] == "f":
            key = event[1]
            if event[2] == "0":
                v["one", key] = swapped(v["fin", key], (16, 16))
            elif event[2] == "1":
                v["pair", key] = jnp.stack(after(v["fin", key], v["one", key]))
                v["token"] = v["pair", key]
                v["two", key] = swapped(v["pair", key], (8, 8))
            elif event[2] == "2":
                cand = (v["fin", key], v["one", key], after(v["two", key]))
                v["cand", key] = cand
                v["picked", key] = pick(v["ints"][7], cand)
                v["token"] = v["picked", key]
                v["three", key] = swapped(v["picked", key], (4, 4))
            else:
                three = after(v["three", key])
                odd = (v["ints"][6] ^ req_index) & 1
                v["final", key] = jnp.where(odd == 1, three, pick(v["ints"][6], v["cand", key])).astype(
                    F32
                )
                v["token"] = v["final", key]
        else:
            ints = after(v["ints"])
            result = normed(ints, v["keep", "A"], v["keep", "B"], v["got", "A"], v["got", "B"])
            v["token"] = result
    final_state = jnp.concatenate([v["final", "A"], v["final", "B"]], axis=0)
    return (result[None], final_state.reshape(1, share, head_dim, nstate))


def passed_along(block, axis, distance):
    devices = range(lax.axis_size(axis))
    route = [(i - distance, i) for i in devices if i - distance in devices]
    return lax.ppermute(block, axis, route)


def carried_in(part, axis, combine, identity):
    place = lax.axis_index(axis)
    gathered = jax.tree.map(lambda a: lax.all_gather(a, axis), part)
    state = jax.tree.map(lambda a, e: jnp.zeros_like(a) + jnp.asarray(e, a.dtype), part, identity)

    def one(step, state):
        return combine(
            state, jax.tree.map(lambda a: lax.dynamic_index_in_dim(a, step, 0, False), gathered)
        )

    return lax.fori_loop(0, place, one, state)


def broadcast(x, axis, root):
    mine = lax.axis_index(axis) == root
    return lax.psum(jnp.where(mine, x, jnp.zeros_like(x)), axis)


def on_device_general(
    tokens,
    mix_weight,
    step_weight,
    conv_weight,
    conv_bias,
    step_bias,
    decay_rate,
    skip_gain,
    norm_gain,
    prompt_len,
    prompt_start,
    deal,
):
    seq_count = lax.axis_size("seq")
    seq_index = lax.axis_index("seq")
    req_index = lax.axis_index("req")
    rows = tokens[0]
    span = rows.shape[0]
    total_reqs = deal.shape[0]
    slots = jnp.arange(total_reqs, dtype=jnp.int32)
    request = jnp.sum(jnp.where(slots == req_index, deal, 0))
    length = jnp.sum(jnp.where(slots == request, prompt_len, 0))
    start = jnp.sum(jnp.where(slots == request, prompt_start, 0))
    place = seq_index * span + jnp.arange(span, dtype=jnp.int32)
    valid = ((place >= start) & (place < start + length)).astype(jnp.float32)
    whole_mix, whole_step = (
        lax.all_gather(mix_weight, ("req", "seq"), axis=0, tiled=True),
        lax.all_gather(step_weight, ("req", "seq"), axis=0, tiled=True),
    )
    mixed = jnp.dot(rows, whole_mix, preferred_element_type=jnp.float32)
    raw_step = jnp.dot(rows, whole_step, preferred_element_type=jnp.float32)
    mixed = (mixed * valid[:, None]).astype(jnp.bfloat16)
    taps = conv_weight.shape[0]
    edge = passed_along(mixed[span - (taps - 1) :], "seq", 1)
    padded = jnp.concatenate([edge, mixed], axis=0)
    conv_sum = jnp.zeros(mixed.shape, jnp.float32) + conv_bias[None, :]
    for offset in range(taps):
        conv_sum = conv_sum + conv_weight[offset][None, :] * padded[offset : offset + span].astype(
            jnp.float32
        )
    convolved = jax.nn.silu(conv_sum).astype(jnp.bfloat16)
    heads = decay_rate.shape[0]
    inner = norm_gain.shape[0]
    head_dim = inner // heads
    nstate = (mixed.shape[1] - inner) // 2
    blocks = span // GROUP
    inputs = convolved[:, :inner].reshape(span, heads, head_dim)
    mixed_b = convolved[:, inner : inner + nstate]
    mixed_c = convolved[:, inner + nstate :]
    step_size = jax.nn.softplus(raw_step + step_bias[None, :]) * valid[:, None]
    pieces = (
        inputs.reshape(blocks, GROUP, heads, head_dim),
        mixed_b.reshape(blocks, GROUP, nstate),
        mixed_c.reshape(blocks, GROUP, nstate),
        step_size.reshape(blocks, GROUP, heads),
    )

    def local_group(block):
        part_in, part_b, part_c, part_step = block
        cum_decay = jnp.cumsum(-part_step * decay_rate[None, :], axis=0)
        places = jnp.arange(GROUP, dtype=jnp.int32)
        causal = places[:, None] >= places[None, :]
        spread = cum_decay[:, None, :] - cum_decay[None, :, :]
        spread = jnp.where(causal[:, :, None], spread, -1e30)
        scores = jnp.einsum("qn,kn->qk", part_c, part_b, preferred_element_type=jnp.float32)
        mixing = (jnp.exp(spread) * scores[:, :, None] * part_step[None, :, :]).astype(jnp.bfloat16)
        inner_out = jnp.einsum("qkh,khp->qhp", mixing, part_in, preferred_element_type=jnp.float32)
        to_end = jnp.exp(cum_decay[-1][None, :] - cum_decay) * part_step
        scaled = (to_end[:, :, None] * part_in.astype(jnp.float32)).astype(jnp.bfloat16)
        local = jnp.einsum("khp,kn->hpn", scaled, part_b, preferred_element_type=jnp.float32)
        return (inner_out, cum_decay, local)

    inner_out, cum_decay, group_state = lax.map(local_group, pieces)
    totals = cum_decay[:, -1, :]

    def advance(carry, item):
        group_total, group_local = item
        return (jnp.exp(group_total)[:, None, None] * carry + group_local, carry)

    dev_state, entry_zero = lax.scan(
        advance, jnp.zeros((heads, head_dim, nstate), jnp.float32), (totals, group_state)
    )
    before = jnp.cumsum(totals, axis=0) - totals
    dev_decay = jnp.exp(jnp.sum(totals, axis=0))

    def chain(earlier, later):
        return (earlier[0] * later[0], later[0][:, None, None] * earlier[1] + later[1])

    incoming_decay, incoming = carried_in(
        (dev_decay, dev_state), "seq", chain, (jnp.ones_like(dev_decay), jnp.zeros_like(dev_state))
    )
    entry = entry_zero + jnp.exp(before)[:, :, None, None] * incoming[None]
    carried = jnp.einsum(
        "cqn,chpn->cqhp", pieces[2].astype(jnp.float32), entry, precision=lax.Precision.HIGHEST
    )
    carried = carried * jnp.exp(cum_decay)[:, :, :, None]
    outputs = (inner_out + carried).reshape(span, heads, head_dim) + skip_gain[
        None, :, None
    ] * inputs.astype(jnp.float32)
    flat = outputs.reshape(span, inner)
    factor = lax.rsqrt(jnp.mean(flat * flat, axis=1, keepdims=True) + EPS)
    result = (flat * factor * norm_gain[None, :] * valid[:, None]).astype(jnp.bfloat16)[None]
    share = heads // seq_count
    leaving = dev_decay[:, None, None] * incoming + dev_state
    last_state = broadcast(leaving, "seq", seq_count - 1)
    own_state = lax.dynamic_slice_in_dim(last_state, seq_index * share, share, 0)[None]
    wanted = jnp.sum(jnp.where(deal == req_index, slots, 0))
    piece = lax.all_gather(own_state, "req", axis=0, tiled=True)
    count = piece.shape[0]
    chosen = jnp.arange(count, dtype=jnp.int32) == wanted
    final_state = jnp.zeros_like(own_state) + jnp.sum(
        jnp.where(chosen[:, None, None, None], piece, 0.0), axis=0, keepdims=True
    )
    return (result, final_state)


def solution(mesh):
    fits = mesh.shape["req"] == 8 and mesh.shape["seq"] == 4
    return jax.shard_map(
        on_device if fits else on_device_general,
        mesh=mesh,
        in_specs=(
            P("req", "seq", None),
            P(("req", "seq"), None),
            P(("req", "seq"), None),
        )
        + (P(),) * 9,
        out_specs=(P("req", "seq", None), P("req", "seq", None, None)),
        check_vma=False,
    )
```

```python
import functools

import jax
import jax.numpy as jnp
from jax import lax
from jax.experimental import pallas as pl
from jax.experimental.pallas import tpu as pltpu
from jax.sharding import PartitionSpec as P

GROUP = 256
EPS = 1e-05
LOG2E = 1.4426950408889634
LANES = 128
HALO = 16
KEYS, ROW = 32, 64
F32 = jnp.float32
BF16 = jnp.bfloat16
AXES = ("req", "seq")
FLIPS = {"a": 16, "b": 8, "y": 4, "x": 2}
ROUTES = (("axyb", "abxy"), ("abyx", "axby"), ("ayxb", "abyx"), ("aybx", "abxy"))
PAIRS = ((0,), (1, 2, 3), (4, 5, 6, 7), (8, 9))
CUT = 2
SCHEDULE = (
    "0.0", "1.0", "tokens", "0.1", "2.0", "1.1", "0.2", "halo", "settings", "3.0",
    "2.1", "1.2", "0.3", "own", "3.1", "2.2", "1.3", "3.2", "2.3", "K0",
    "K1", "xA", "3.3", "K2", "JA", "fA0", "K3", "xB", "fA1", "JB",
    "fB0", "fA2", "fB1", "norm", "fA3", "fB2", "fB3",
)
VMEM = pl.BlockSpec(memory_space=pltpu.VMEM)
LIGHT = pl.CostEstimate(flops=1000, bytes_accessed=1000, transcendentals=0)
SMEM = pl.BlockSpec(memory_space=pltpu.SMEM)


def dot(a, b):
    return jnp.dot(a, b, preferred_element_type=F32)


def params(vmem_mib):
    return pltpu.CompilerParams(vmem_limit_bytes=vmem_mib * 1024 * 1024)


def first_head(pair, share):
    return (pair % 2) * share + 2 * (pair // 2)


def lanes(i):
    return slice(i * LANES, (i + 1) * LANES)


def valid_rows(first, rows, start, end):
    place = first + lax.broadcasted_iota(jnp.int32, (rows, LANES), 0)
    return jnp.where((place >= start) & (place < end), 1.0, 0.0).astype(F32)


def column(a, head):
    return jnp.broadcast_to(a[:, head : head + 1], (a.shape[0], LANES))


def split(a):
    upper = a.astype(BF16)
    return upper, (a - upper.astype(F32)).astype(BF16)


def project(chunk, ints, own, other, low, high, whole, padded, raw):
    block = low.shape[0] // 8
    start, end, first, core = ints[0], ints[1], ints[2], ints[3]
    for p in range(16):
        one, two = (
            sum(FLIPS[step] // 2 for i, step in enumerate(route) if (p >> i) & 1)
            for route in ROUTES[chunk]
        )
        chip = jnp.bitwise_xor(ints[5], jnp.where(core == 0, one, two))
        source = low if p < 8 else high
        row = pl.multiple_of(chip * block, block)
        whole[pl.ds(row, block), :] = source[(p % 8) * block : (p % 8 + 1) * block, :]
    span = other.shape[0]
    spans = [i for i in range(low.shape[1] // LANES) if raw is None or i != 1]
    mine = dot(own[...], whole[...])
    theirs = dot(other[...], whole[...])
    at_mine = pl.multiple_of(core * span, span)
    at_theirs = pl.multiple_of((1 - core) * span, span)
    ok_edge = valid_rows(first - 8, 8, start, end)
    ok_mine = valid_rows(first + at_mine, span, start, end)
    ok_theirs = valid_rows(first + at_theirs, span, start, end)

    def rounded(a, ok):
        return (a * ok).astype(BF16).astype(F32)

    for at, lane in enumerate(spans):
        edge = mine[0:HALO, lanes(lane)][HALO - 8 :]
        padded[at, 0:8, :] = rounded(edge, ok_edge)
        padded[at, pl.ds(8 + at_mine, span), :] = rounded(mine[HALO:, lanes(lane)], ok_mine)
        padded[at, pl.ds(8 + at_theirs, span), :] = rounded(theirs[:, lanes(lane)], ok_theirs)
    if raw is not None:
        raw[pl.ds(at_mine, span), :] = mine[HALO:, lanes(1)]
        raw[pl.ds(at_theirs, span), :] = theirs[:, lanes(1)]


def convolved(at, tap, group, taps, padded):
    total = taps[4:5, lanes(tap)]
    for k in range(4):
        rows = padded[at, group * GROUP + 5 + k : (group + 1) * GROUP + 5 + k, :]
        total = total + taps[k : k + 1, lanes(tap)] * rows
    half = 0.5 * total
    return (half + half * jnp.tanh(half)).astype(BF16)


def first_kernel(
    ints, own, other, low, high, taps, rates,
    bc_out, x_out, table_out, kt_out, tot_out,
    whole, padded, raw,
):
    project(0, ints, own, other, low, high, whole, padded, raw)
    row = lax.broadcasted_iota(jnp.int32, (GROUP, GROUP), 0)
    col = lax.broadcasted_iota(jnp.int32, (GROUP, GROUP), 1)
    below = jnp.where(row >= col, 1.0, 0.0).astype(BF16)
    before = jnp.zeros((1, LANES), F32)
    for group in range(bc_out.shape[0] // GROUP):
        rows = slice(group * GROUP, (group + 1) * GROUP)
        bc_out[rows, :] = convolved(0, 0, group, taps, padded)
        for at in range(1, padded.shape[0]):
            x_out[rows, lanes(at - 1)] = convolved(at, at, group, taps, padded)
        ok = valid_rows(ints[2] + group * GROUP, GROUP, ints[0], ints[1])
        step = raw[rows, :] + rates[0:1, :]
        size = (jnp.maximum(step, 0.0) + jnp.log1p(jnp.exp(-jnp.abs(step)))) * ok
        decay = size * rates[1:2, :]
        high_part, rest = split(decay)
        rest = decay - high_part.astype(F32)
        mid_part, low_part = split(rest)
        cum = dot(below, high_part) + dot(below, mid_part) + dot(below, low_part)
        from_key = jnp.log2(size) - cum
        kt_out[group] = from_key.T[0:32, :]
        lane = lax.broadcasted_iota(jnp.int32, (GROUP, LANES), 1)
        table = jnp.where(lane < KEYS, cum, pltpu.roll(from_key, KEYS, 1))
        table_out[rows, :] = jnp.where(lane < ROW, table, pltpu.roll(cum + before, ROW, 1))
        before = before + cum[GROUP - 1 : GROUP, :]
    tot_out[...] = jnp.broadcast_to(before, tot_out.shape)


def sorted_bc(ints, mine, theirs):
    first = ints[3] == 0
    return jnp.where(first, mine, theirs), jnp.where(first, theirs, mine)


def scan_kernel(
    chunk, held, heads, extra, ints, own, other, low, high, taps, x_ref, mine_ref, their_ref, table_ref,
    kt_ref, tot_ref, skip_ref, *refs,
):
    y_out, s_out, send_out, whole, padded, carry = refs[-6:]
    project(chunk, ints, own, other, low, high, whole, padded, None)
    base = 0
    for earlier in refs[:-6]:
        base = earlier.shape[1] // LANES
        send_out[:, 0 : base * LANES] = earlier[...]
    half = GROUP // 2
    row = lax.broadcasted_iota(jnp.int32, (half, half), 0)
    col = lax.broadcasted_iota(jnp.int32, (half, half), 1)
    causal = row >= col
    left = lax.broadcasted_iota(jnp.int32, (GROUP, LANES), 1) < LANES // 2
    zero = jnp.zeros((GROUP, LANES), BF16)
    for group in range(y_out.shape[0] // GROUP):
        rows = slice(group * GROUP, (group + 1) * GROUP)
        b, c = sorted_bc(ints, mine_ref[rows, :], their_ref[rows, :])
        scores = lax.dot_general(c, b, (((1,), (1,)), ((), ())), preferred_element_type=F32)
        table, kt = table_ref[rows, :], kt_ref[group]
        carried = None
        if group:
            upper, lower = split(carry[...])
            carried = dot(jnp.concatenate([c, c], axis=1), jnp.concatenate([upper, lower], axis=0))
        scaled, ends = [], []
        for i, head in enumerate(heads):
            if i < extra:
                x = x_ref[rows, lanes(i)]
            else:
                x = convolved(i - extra, held[i] + 1, group, taps, padded)
            top, bottom, spread = [], [], []
            for h in (head, head + 1):
                q = column(table, h)
                spread.append(q)
                k0 = jnp.broadcast_to(kt[h : h + 1, 0:half], (half, half))
                k1 = jnp.broadcast_to(kt[h : h + 1, half:], (half, half))
                m00 = jnp.where(causal, jnp.exp2(q[0:half] + k0) * scores[0:half, 0:half], 0.0)
                m10 = jnp.exp2(q[half:] + k0) * scores[half:, 0:half]
                m11 = jnp.where(causal, jnp.exp2(q[half:] + k1) * scores[half:, half:], 0.0)
                top.append(m00.astype(BF16))
                bottom.append(m10.astype(BF16))
                bottom.append(m11.astype(BF16))
            x0, x1 = jnp.where(left, x, zero), jnp.where(left, zero, x)
            y_top = dot(
                jnp.concatenate(top, axis=1), jnp.concatenate([x0[0:half], x1[0:half]], axis=0)
            )
            y_bottom = dot(jnp.concatenate(bottom, axis=1), jnp.concatenate([x0, x1], axis=0))
            q = jnp.where(left, spread[0], spread[1])
            xf = x.astype(F32)
            rest = skip_ref[2:3, lanes(held[i])] * xf
            if group:
                rest = rest + jnp.exp2(q) * carried[:, lanes(i)]
            y_out[group * GROUP : group * GROUP + half, lanes(i)] = y_top + rest[0:half]
            y_out[group * GROUP + half : (group + 1) * GROUP, lanes(i)] = y_bottom + rest[half:]
            k = jnp.where(left, column(table, KEYS + head), column(table, KEYS + head + 1))
            end = q[GROUP - 1 : GROUP, :]
            scaled.append((jnp.exp2(k + end) * xf).astype(BF16))
            ends.append(jnp.exp2(end))
        local = lax.dot_general(
            b, jnp.concatenate(scaled, axis=1), (((0,), (0,)), ((), ())), preferred_element_type=F32
        )
        if group:
            local = jnp.concatenate(ends, axis=1) * carry[...] + local
        carry[...] = local
    s_out[...] = carry[...]
    send_out[0:LANES, base * LANES :] = carry[...].astype(BF16)
    side = lax.broadcasted_iota(jnp.int32, (8, LANES), 1) < LANES // 2
    for i, head in enumerate(heads):
        total = jnp.where(side, column(tot_ref[...], head), column(tot_ref[...], head + 1))
        one, rest = split(total)
        two, three = split(total - one.astype(F32))
        place = lax.broadcasted_iota(jnp.int32, (8, LANES), 0)
        parts = jnp.where(place == 0, one.astype(F32), two.astype(F32))
        parts = jnp.where(place >= 2, three.astype(F32), parts)
        parts = jnp.where(place >= 3, 0.0, parts)
        send_out[LANES:, lanes(base + i)] = jnp.concatenate([parts, jnp.zeros_like(parts)], axis=0).astype(
            BF16
        )


def join_kernel(heads, sizes, halves, ints, mine_ref, their_ref, table_ref, tot_ref, r_ref, *refs):
    count = len(sizes)
    y_refs, s_refs = refs[:count], refs[count : 2 * count]
    send_out, keep_out, fin_out = refs[2 * count :]
    later = ints[4] > 0
    core = ints[3]
    where = [(j, k) for j, size in enumerate(sizes) for k in range(size)]
    span = send_out.shape[0]
    received = r_ref[0:LANES, :].astype(F32)
    entering = (received * jnp.where(later, 1.0, 0.0)).astype(BF16)
    from_head = lax.broadcasted_iota(jnp.int32, (2 * LANES, LANES), 0) % LANES
    second = lax.broadcasted_iota(jnp.int32, (2 * LANES, LANES), 1) // (LANES // 2)
    spread = jnp.concatenate(
        [jnp.where(from_head == ROW + head + second, 1.0, 0.0).astype(BF16) for head in heads], axis=1
    )
    for out, at in ((send_out, (1 - core) * span), (keep_out, core * span)):
        rows = pl.ds(pl.multiple_of(at, span), span)
        lane = lax.broadcasted_iota(jnp.int32, (span, LANES), 1)
        decay = jnp.exp2(jnp.where(lane < ROW, 0.0, table_ref[rows, :]))
        decay = dot(jnp.concatenate(split(decay), axis=1), spread)
        _, c = sorted_bc(ints, mine_ref[rows, :], their_ref[rows, :])
        carried = dot(c, entering)
        for i in range(len(heads)):
            j, k = where[i]
            out[:, lanes(i)] = (
                y_refs[j][rows, lanes(k)] + decay[:, lanes(i)] * carried[:, lanes(i)]
            )
    side = lax.broadcasted_iota(jnp.int32, (8, LANES), 1) < LANES // 2
    tot = tot_ref[...]
    for i, (early, late) in enumerate(halves):

        def own_state(p):
            j, k = where[p]
            return s_refs[j][:, lanes(k)]

        parts = r_ref[LANES:, lanes(early)].astype(F32)
        their_total = parts[0:1] + parts[1:2] + parts[2:3]
        my_total = jnp.where(side, column(tot, heads[late]), column(tot, heads[late] + 1))[0:1]
        at_first = jnp.exp2(their_total) * own_state(early) + received[:, lanes(early)]
        at_last = jnp.exp2(my_total) * received[:, lanes(late)] + own_state(late)
        both = jnp.where(later, at_last, at_first)
        fin_out[i * LANES : (i + 1) * LANES, :] = both.T.astype(fin_out.dtype)


def norm_kernel(places, ints, gain_ref, ka_ref, kb_ref, ra_ref, rb_ref, out_ref):
    step = pl.program_id(0)
    core = ints[3]
    rows = out_ref.shape[0]
    first = ints[2] + (core * pl.num_programs(0) + step) * rows
    ok = valid_rows(first, rows, ints[0], ints[1])
    blocks = []
    for who, refs in ((core, (ka_ref, kb_ref)), (1 - core, (ra_ref, rb_ref))):
        for ref, wheres in zip(refs, places, strict=True):
            for i, where in enumerate(wheres):
                at = pl.multiple_of((where + 5 * who) * LANES, LANES)
                blocks.append((at, ref, i))
    total = jnp.zeros((rows, LANES), F32)
    for _, ref, i in blocks:
        v = ref[:, lanes(i)]
        total = total + v * v
    mean = jnp.sum(total, axis=1, keepdims=True) * (1.0 / out_ref.shape[1])
    factor = lax.rsqrt(mean + EPS) * ok
    for at, ref, i in blocks:
        v = ref[:, lanes(i)]
        out_ref[:, pl.ds(at, LANES)] = (v * factor * gain_ref[0:1, pl.ds(at, LANES)]).astype(BF16)


def head_of(lane, core, share):
    return jnp.where(lane < 2 * share, lane + core * share + (lane // share) * share, -1)


def chosen_heads(core, heads, rows):
    row = lax.broadcasted_iota(jnp.int32, (rows, LANES), 0)
    lane = lax.broadcasted_iota(jnp.int32, (rows, LANES), 1)
    return jnp.where(row == head_of(lane, core, heads // 4), 1.0, 0.0)


def columns_of(source, core, inner):
    first = inner // 4 // LANES
    blocks = [inner // LANES + core]
    for i in range(first):
        blocks += [first * core + i, 2 * first + first * core + i]
    return [source[:, pl.ds(pl.multiple_of(at * LANES, LANES), LANES)] for at in blocks]


def sort_kernel(inner, ints, mix, step, kept_out, given_out):
    for out, core in ((kept_out, ints[1]), (given_out, 1 - ints[1])):
        parts = columns_of(mix, core, inner)
        out[:, lanes(0)] = parts[0]
        out[:, lanes(1)] = dot(step[...], chosen_heads(core, step.shape[1], step.shape[1]).astype(BF16)).astype(BF16)
        for i, part in enumerate(parts[1:]):
            out[:, lanes(2 + i)] = part


def stack_kernel(ints, kept, got, *outs):
    rows = kept.shape[0]
    core = ints[1]
    at = 0
    for out in outs:
        width = out.shape[1]
        out[pl.ds(pl.multiple_of(core * rows, rows), rows), :] = kept[:, at : at + width]
        out[pl.ds(pl.multiple_of((1 - core) * rows, rows), rows), :] = got[:, at : at + width]
        at += width


def settings_kernel(
    inner, place, deal, lengths, starts, small, ints_out, taps_out, rates_out, skip_out
):
    request, wanted, near = jnp.int32(0), jnp.int32(0), jnp.int32(0)
    req = place[4]
    for i in range(deal.shape[0]):
        request = jnp.where(req == i, deal[i], request)
        wanted = jnp.where(deal[i] == req, i, wanted)
        near = jnp.where(deal[i] == jnp.bitwise_xor(req, 1), i, near)
    start, length = jnp.int32(0), jnp.int32(0)
    for i in range(deal.shape[0]):
        start = jnp.where(request == i, starts[i], start)
        length = jnp.where(request == i, lengths[i], length)
    ints_out[0] = start
    ints_out[1] = start + length
    for i in range(4):
        ints_out[2 + i] = place[i]
    ints_out[6] = wanted
    ints_out[7] = near
    core = place[1]
    for i, part in enumerate(columns_of(small, core, inner)):
        row = lax.broadcasted_iota(jnp.int32, (8, LANES), 0)
        taps_out[:, lanes(i)] = jnp.where(row < 5, part[0:8], 0.0)
    heads = inner // LANES * 2
    exact = functools.partial(
        jnp.dot, precision=lax.Precision.HIGHEST, preferred_element_type=F32
    )
    own = exact(small[8:16, 0:LANES], chosen_heads(core, heads, LANES))
    rates_out[...] = own
    row = lax.broadcasted_iota(jnp.int32, (LANES, inner // 2), 0)
    lane = lax.broadcasted_iota(jnp.int32, (LANES, inner // 2), 1)
    pair, second = lane // LANES, (lane % LANES) // (LANES // 2)
    mine = (pair % 2) * (heads // 4) + 2 * (pair // 2) + second
    skip_out[...] = exact(own, jnp.where(row == mine, 1.0, 0.0))


def chosen(req, row, here, one, two):
    rel = jnp.bitwise_xor(row, req)
    far, near = (rel // 4) % 2 == 1, (rel // 2) % 2 == 1
    return jnp.where(
        near, jnp.where(far, two[1], two[0]), jnp.where(far, one[...], here[...])
    )


def pick_kernel(place, ints, here, one, two, out):
    out[...] = chosen(place[4], ints[7], here, one, two)


def last_kernel(place, ints, here, one, two, three, *refs):
    odd = jnp.bitwise_xor(ints[6], place[4]) % 2 == 1
    best = chosen(place[4], ints[6], here, one, two)
    out, base = refs[-1], 0
    for earlier in refs[:-1]:
        base = earlier.shape[0]
        out[0:base, :] = earlier[...]
    out[base:, :] = jnp.where(odd, three[...], best).astype(F32)


def swapped(x, masks):
    count = lax.axis_size("req") * lax.axis_size("seq")
    return lax.ppermute(x, AXES, [(i, i ^ masks[i % 2]) for i in range(count)])


def on_device(
    tokens, mix_weight, step_weight, conv_weight, conv_bias, step_bias, decay_rate, skip_gain,
    norm_gain, prompt_len, prompt_start, deal,
):
    seq_index = lax.axis_index("seq")
    req_index = lax.axis_index("req")
    core, along = seq_index % 2, seq_index // 2
    rows = tokens[0]
    span, depth = rows.shape
    inner = norm_gain.shape[0]
    heads = decay_rate.shape[0]
    head_dim = inner // heads
    nstate = (mix_weight.shape[1] - inner) // 2
    share = heads // 4
    quarter = inner // 4
    chip = req_index * 2 + along
    place = jnp.stack([along * 2 * span, core, along, chip, req_index])
    state = {}

    def after(*values):
        if "token" not in state:
            return values if len(values) > 1 else values[0]
        *out, state["token"] = lax.optimization_barrier((*values, state["token"]))
        return tuple(out) if len(out) > 1 else out[0]

    widths = [(len(held) + (2 if i == 0 else 0)) * LANES for i, held in enumerate(PAIRS)]
    total = sum(widths)
    portion = mix_weight.shape[0]
    kept, given = pl.pallas_call(
        functools.partial(sort_kernel, inner),
        in_specs=[SMEM, VMEM, VMEM],
        out_specs=[VMEM] * 2,
        out_shape=[jax.ShapeDtypeStruct((portion, total), BF16)] * 2,
        compiler_params=params(8),
        cost_estimate=LIGHT,
        name="sort",
    )(place, mix_weight, step_weight)
    got = swapped(given, (1, 1))
    blocks = pl.pallas_call(
        stack_kernel,
        in_specs=[SMEM, VMEM, VMEM],
        out_specs=[VMEM] * len(widths),
        out_shape=[jax.ShapeDtypeStruct((2 * portion, width), BF16) for width in widths],
        compiler_params=params(8),
        cost_estimate=LIGHT,
        name="stack",
    )(place, kept, got)
    blocks = list(blocks)
    arrived = [None] * len(widths)

    chip_rows = 2 * span
    groups = chip_rows // GROUP

    def scratch(width, spans):
        return [
            pltpu.VMEM((depth, width), BF16),
            pltpu.VMEM((spans, chip_rows + 8, LANES), F32),
        ]

    extra = len(PAIRS[0])

    def projected(ints, own, other, low, high, taps, rates):
        width = widths[0]
        return pl.pallas_call(
            first_kernel,
            in_specs=[SMEM] + [VMEM] * 6,
            out_specs=[VMEM] * 5,
            scratch_shapes=scratch(width, 1 + extra) + [pltpu.VMEM((chip_rows, LANES), F32)],
            out_shape=[
                jax.ShapeDtypeStruct((chip_rows, LANES), BF16),
                jax.ShapeDtypeStruct((chip_rows, extra * LANES), BF16),
                jax.ShapeDtypeStruct((chip_rows, LANES), F32),
                jax.ShapeDtypeStruct((groups, 32, GROUP), F32),
                jax.ShapeDtypeStruct((8, LANES), F32),
            ],
            compiler_params=params(28),
            cost_estimate=LIGHT,
            name="first",
        )(ints, own, other, low, high, taps, rates)

    def scanned(index, ints, own, other, low, high, taps, skip, x0, mine, theirs, table, kt, tot, *earlier):
        more = extra if index == 1 else 0
        held = (PAIRS[0] if more else ()) + PAIRS[index]
        pairs = len(held)
        new = pairs - more
        firsts = [first_head(p, share) for p in held]
        width = widths[index]
        return pl.pallas_call(
            functools.partial(scan_kernel, index, held, firsts, more),
            in_specs=[SMEM] + [VMEM] * (12 + len(earlier)),
            out_specs=[VMEM] * 3,
            scratch_shapes=scratch(width, new) + [pltpu.VMEM((LANES, pairs * LANES), F32)],
            out_shape=[
                jax.ShapeDtypeStruct((chip_rows, pairs * LANES), F32),
                jax.ShapeDtypeStruct((LANES, pairs * LANES), F32),
                jax.ShapeDtypeStruct(
                    (LANES + 16, pairs * LANES + sum(a.shape[1] for a in earlier)), BF16
                ),
            ],
            compiler_params=params(28),
            cost_estimate=LIGHT,
            name="scan",
        )(
            ints, own, other, low, high, taps,
            x0, mine, theirs, table, kt, tot, skip, *earlier,
        )

    def joined(held, ints, mine, theirs, table, tot, ys, ss, r):
        pairs = len(held)
        halves = [(i, i + 1) for i in range(0, pairs, 2)]
        sizes = [y.shape[1] // LANES for y in ys]
        return pl.pallas_call(
            functools.partial(join_kernel, [first_head(p, share) for p in held], sizes, halves),
            in_specs=[SMEM] + [VMEM] * (5 + 2 * len(ys)),
            out_specs=[VMEM] * 3,
            out_shape=[
                jax.ShapeDtypeStruct((span, pairs * LANES), F32),
                jax.ShapeDtypeStruct((span, pairs * LANES), F32),
                jax.ShapeDtypeStruct((len(halves) * LANES, nstate), BF16),
            ],
            compiler_params=params(28),
            cost_estimate=LIGHT,
            name="join",
        )(ints, mine, theirs, table, tot, r, *ys, *ss)

    early_pairs, late_pairs = sum(PAIRS[:CUT], ()), sum(PAIRS[CUT:], ())

    def normed(ints, keep_a, keep_b, got_a, got_b):
        places = [
            [(p % 2) * (2 * quarter // LANES) + p // 2 for p in held]
            for held in (early_pairs, late_pairs)
        ]
        block = span // 2
        return pl.pallas_call(
            functools.partial(norm_kernel, places),
            grid_spec=pltpu.PrefetchScalarGridSpec(
                num_scalar_prefetch=1,
                grid=(span // block,),
                in_specs=[pl.BlockSpec((1, inner), lambda i, ints: (0, 0))]
                + [
                    pl.BlockSpec((block, a.shape[1]), lambda i, ints: (i, 0))
                    for a in (keep_a, keep_b, got_a, got_b)
                ],
                out_specs=pl.BlockSpec((block, inner), lambda i, ints: (i, 0)),
            ),
            out_shape=jax.ShapeDtypeStruct((span, inner), BF16),
            compiler_params=params(28),
            cost_estimate=LIGHT,
            name="norm",
        )(ints, norm_gain[None], keep_a, keep_b, got_a, got_b)

    def picked(kernel, kind, *arrays, more=0):
        return pl.pallas_call(
            kernel,
            in_specs=[SMEM] * 2 + [VMEM] * len(arrays),
            out_specs=VMEM,
            out_shape=jax.ShapeDtypeStruct((arrays[0].shape[0] + more, nstate), kind),
            compiler_params=params(8),
            cost_estimate=LIGHT,
            name="pick",
        )(place, v["ints"], *arrays)

    v = state
    last = len(PAIRS) - 1
    for event in SCHEDULE:
        if event[0].isdigit():
            i, step = (int(part) for part in event.split("."))
            if step:
                blocks[i] = jnp.concatenate(after(blocks[i], arrived[i]), axis=0)
                v["token"] = blocks[i]
            route = ROUTES[i]
            arrived[i] = swapped(blocks[i], (FLIPS[route[0][step]], FLIPS[route[1][step]]))
        elif event == "tokens":
            v["other"] = swapped(rows, (1, 1))
        elif event == "halo":
            other = after(v["other"])
            edge = jnp.where(core == 1, rows[span - HALO :], other[span - HALO :])
            count = lax.axis_size("req") * lax.axis_size("seq")
            route = [(i, i + 2) for i in range(count) if (i // 2) % 2 == 0]
            v["token"] = edge
            v["halo"] = lax.ppermute(edge, AXES, route)
        elif event == "settings":
            half = inner // 2

            conv_w, conv_b, step_b, rate, gain = after(
                conv_weight, conv_bias, step_bias, decay_rate, skip_gain
            )

            def row(values):
                return jnp.pad(values, (0, conv_weight.shape[1] - values.shape[0]))[None]

            small = jnp.concatenate(
                [conv_w, conv_b[None], jnp.zeros((3, conv_w.shape[1]), F32)]
                + [row(step_b), row(rate * (-LOG2E)), row(gain)]
                + [jnp.zeros((5, conv_weight.shape[1]), F32)],
                axis=0,
            )
            v["ints"], v["taps"], v["rates"], v["skip"] = pl.pallas_call(
                functools.partial(settings_kernel, inner),
                in_specs=[SMEM] * 4 + [VMEM],
                out_specs=[SMEM] + [VMEM] * 3,
                out_shape=[
                    jax.ShapeDtypeStruct((8,), jnp.int32),
                    jax.ShapeDtypeStruct((8, half + LANES), F32),
                    jax.ShapeDtypeStruct((8, LANES), F32),
                    jax.ShapeDtypeStruct((8, half), F32),
                ],
                compiler_params=params(8),
                cost_estimate=LIGHT,
                name="settings",
            )(after(place), deal, prompt_len, prompt_start, small)
            v["token"] = v["rates"]
        elif event == "own":
            v["own"] = jnp.concatenate([after(v["halo"]), rows], axis=0)
            v["token"] = v["own"]
        elif event == "K0":
            ints = after(v["ints"])
            bc, x0, table, kt, tot = projected(
                ints, v["own"], v["other"], blocks[0], arrived[0], v["taps"], v["rates"]
            )
            v["token"] = tot
            v["bc"] = swapped(bc, (1, 1))
        elif event[0] == "K":
            i = int(event[1:])
            if i == 1:
                theirs = after(v["bc"])
            ints = after(v["ints"])
            v["y", i], v["s", i], v["t", i] = scanned(
                i, ints, v["own"], v["other"], blocks[i], arrived[i], v["taps"], v["skip"],
                x0, bc, theirs, table, kt, tot, *([v["t", i - 1]] if i > 1 and i != CUT else []),
            )
            v["token"] = v["t", i]
        elif event in ("xA", "xB"):
            v["r", event[1]] = swapped(v["t", CUT - 1 if event == "xA" else last], (2, 2))
        elif event in ("JA", "JB"):
            which = range(1, CUT) if event == "JA" else range(CUT, last + 1)
            held = early_pairs if event == "JA" else late_pairs
            ints, r = after(v["ints"], v["r", event[1]])
            send, v["keep", event[1]], v["fin", event[1]] = joined(
                held, ints, bc, theirs, table, tot, [v["y", i] for i in which], [v["s", i] for i in which], r
            )
            v["token"] = v["fin", event[1]]
            v["got", event[1]] = swapped(send, (1, 1))
        elif event[0] == "f":
            key = event[1]
            if event[2] == "0":
                v["one", key] = swapped(v["fin", key], (16, 16))
            elif event[2] == "1":
                v["pair", key] = jnp.stack(after(v["fin", key], v["one", key]))
                v["token"] = v["pair", key]
                v["two", key] = swapped(v["pair", key], (8, 8))
            elif event[2] == "2":
                cand = (v["fin", key], v["one", key], after(v["two", key]))
                v["cand", key] = cand
                v["picked", key] = picked(pick_kernel, BF16, *cand)
                v["token"] = v["picked", key]
                v["three", key] = swapped(v["picked", key], (4, 4))
            else:
                three = after(v["three", key])
                earlier = [v["final", "A"]] if key == "B" else []
                more = sum(a.shape[0] for a in earlier)
                v["final", key] = picked(
                    last_kernel, F32, *v["cand", key], three, *earlier, more=more
                )
                v["token"] = v["final", key]
        else:
            ints = after(v["ints"])
            result = normed(ints, v["keep", "A"], v["keep", "B"], v["got", "A"], v["got", "B"])
            v["token"] = result
    return (result[None], v["final", "B"].reshape(1, share, head_dim, nstate))


def passed_along(block, axis, distance):
    devices = range(lax.axis_size(axis))
    route = [(i - distance, i) for i in devices if i - distance in devices]
    return lax.ppermute(block, axis, route)


def carried_in(part, axis, combine, identity):
    place = lax.axis_index(axis)
    gathered = jax.tree.map(lambda a: lax.all_gather(a, axis), part)
    state = jax.tree.map(lambda a, e: jnp.zeros_like(a) + jnp.asarray(e, a.dtype), part, identity)

    def one(step, state):
        return combine(
            state, jax.tree.map(lambda a: lax.dynamic_index_in_dim(a, step, 0, False), gathered)
        )

    return lax.fori_loop(0, place, one, state)


def broadcast(x, axis, root):
    mine = lax.axis_index(axis) == root
    return lax.psum(jnp.where(mine, x, jnp.zeros_like(x)), axis)


def on_device_general(
    tokens,
    mix_weight,
    step_weight,
    conv_weight,
    conv_bias,
    step_bias,
    decay_rate,
    skip_gain,
    norm_gain,
    prompt_len,
    prompt_start,
    deal,
):
    seq_count = lax.axis_size("seq")
    seq_index = lax.axis_index("seq")
    req_index = lax.axis_index("req")
    rows = tokens[0]
    span = rows.shape[0]
    total_reqs = deal.shape[0]
    slots = jnp.arange(total_reqs, dtype=jnp.int32)
    request = jnp.sum(jnp.where(slots == req_index, deal, 0))
    length = jnp.sum(jnp.where(slots == request, prompt_len, 0))
    start = jnp.sum(jnp.where(slots == request, prompt_start, 0))
    place = seq_index * span + jnp.arange(span, dtype=jnp.int32)
    valid = ((place >= start) & (place < start + length)).astype(jnp.float32)
    whole_mix, whole_step = (
        lax.all_gather(mix_weight, ("req", "seq"), axis=0, tiled=True),
        lax.all_gather(step_weight, ("req", "seq"), axis=0, tiled=True),
    )
    mixed = jnp.dot(rows, whole_mix, preferred_element_type=jnp.float32)
    raw_step = jnp.dot(rows, whole_step, preferred_element_type=jnp.float32)
    mixed = (mixed * valid[:, None]).astype(jnp.bfloat16)
    taps = conv_weight.shape[0]
    edge = passed_along(mixed[span - (taps - 1) :], "seq", 1)
    padded = jnp.concatenate([edge, mixed], axis=0)
    conv_sum = jnp.zeros(mixed.shape, jnp.float32) + conv_bias[None, :]
    for offset in range(taps):
        conv_sum = conv_sum + conv_weight[offset][None, :] * padded[offset : offset + span].astype(
            jnp.float32
        )
    convolved = jax.nn.silu(conv_sum).astype(jnp.bfloat16)
    heads = decay_rate.shape[0]
    inner = norm_gain.shape[0]
    head_dim = inner // heads
    nstate = (mixed.shape[1] - inner) // 2
    blocks = span // GROUP
    inputs = convolved[:, :inner].reshape(span, heads, head_dim)
    mixed_b = convolved[:, inner : inner + nstate]
    mixed_c = convolved[:, inner + nstate :]
    step_size = jax.nn.softplus(raw_step + step_bias[None, :]) * valid[:, None]
    pieces = (
        inputs.reshape(blocks, GROUP, heads, head_dim),
        mixed_b.reshape(blocks, GROUP, nstate),
        mixed_c.reshape(blocks, GROUP, nstate),
        step_size.reshape(blocks, GROUP, heads),
    )

    def local_group(block):
        part_in, part_b, part_c, part_step = block
        cum_decay = jnp.cumsum(-part_step * decay_rate[None, :], axis=0)
        places = jnp.arange(GROUP, dtype=jnp.int32)
        causal = places[:, None] >= places[None, :]
        spread = cum_decay[:, None, :] - cum_decay[None, :, :]
        spread = jnp.where(causal[:, :, None], spread, -1e30)
        scores = jnp.einsum("qn,kn->qk", part_c, part_b, preferred_element_type=jnp.float32)
        mixing = (jnp.exp(spread) * scores[:, :, None] * part_step[None, :, :]).astype(jnp.bfloat16)
        inner_out = jnp.einsum("qkh,khp->qhp", mixing, part_in, preferred_element_type=jnp.float32)
        to_end = jnp.exp(cum_decay[-1][None, :] - cum_decay) * part_step
        scaled = (to_end[:, :, None] * part_in.astype(jnp.float32)).astype(jnp.bfloat16)
        local = jnp.einsum("khp,kn->hpn", scaled, part_b, preferred_element_type=jnp.float32)
        return (inner_out, cum_decay, local)

    inner_out, cum_decay, group_state = lax.map(local_group, pieces)
    totals = cum_decay[:, -1, :]

    def advance(carry, item):
        group_total, group_local = item
        return (jnp.exp(group_total)[:, None, None] * carry + group_local, carry)

    dev_state, entry_zero = lax.scan(
        advance, jnp.zeros((heads, head_dim, nstate), jnp.float32), (totals, group_state)
    )
    before = jnp.cumsum(totals, axis=0) - totals
    dev_decay = jnp.exp(jnp.sum(totals, axis=0))

    def chain(earlier, later):
        return (earlier[0] * later[0], later[0][:, None, None] * earlier[1] + later[1])

    incoming_decay, incoming = carried_in(
        (dev_decay, dev_state), "seq", chain, (jnp.ones_like(dev_decay), jnp.zeros_like(dev_state))
    )
    entry = entry_zero + jnp.exp(before)[:, :, None, None] * incoming[None]
    carried = jnp.einsum(
        "cqn,chpn->cqhp", pieces[2].astype(jnp.float32), entry, precision=lax.Precision.HIGHEST
    )
    carried = carried * jnp.exp(cum_decay)[:, :, :, None]
    outputs = (inner_out + carried).reshape(span, heads, head_dim) + skip_gain[
        None, :, None
    ] * inputs.astype(jnp.float32)
    flat = outputs.reshape(span, inner)
    factor = lax.rsqrt(jnp.mean(flat * flat, axis=1, keepdims=True) + EPS)
    result = (flat * factor * norm_gain[None, :] * valid[:, None]).astype(jnp.bfloat16)[None]
    share = heads // seq_count
    leaving = dev_decay[:, None, None] * incoming + dev_state
    last_state = broadcast(leaving, "seq", seq_count - 1)
    own_state = lax.dynamic_slice_in_dim(last_state, seq_index * share, share, 0)[None]
    wanted = jnp.sum(jnp.where(deal == req_index, slots, 0))
    piece = lax.all_gather(own_state, "req", axis=0, tiled=True)
    count = piece.shape[0]
    chosen = jnp.arange(count, dtype=jnp.int32) == wanted
    final_state = jnp.zeros_like(own_state) + jnp.sum(
        jnp.where(chosen[:, None, None, None], piece, 0.0), axis=0, keepdims=True
    )
    return (result, final_state)


def solution(mesh):
    fits = mesh.shape["req"] == 8 and mesh.shape["seq"] == 4
    return jax.shard_map(
        on_device if fits else on_device_general,
        mesh=mesh,
        in_specs=(
            P("req", "seq", None),
            P(("req", "seq"), None),
            P(("req", "seq"), None),
        )
        + (P(),) * 9,
        out_specs=(P("req", "seq", None), P("req", "seq", None, None)),
        check_vma=False,
    )
```

```python
import functools

import jax
import jax.numpy as jnp
from jax import lax
from jax.experimental import pallas as pl
from jax.experimental.pallas import tpu as pltpu
from jax.sharding import PartitionSpec as P

GROUP = 256
EPS = 1e-05
LOG2E = 1.4426950408889634
LANES = 128
HALO = 16
KEYS, ROW = 32, 64
F32 = jnp.float32
BF16 = jnp.bfloat16
AXES = ("req", "seq")
FLIPS = {"a": 16, "b": 8, "y": 4, "x": 2}
ROUTES = (("axyb", "abxy"), ("abyx", "axby"), ("ayxb", "abyx"), ("axyb", "abxy"))
PAIRS = ((0,), (1, 2, 3), (4, 5, 6, 7), (8, 9))
CUT = 2
SCHEDULE = (
    "0.0", "1.0", "tokens", "0.1", "2.0", "1.1", "0.2", "halo", "settings", "3.0",
    "2.1", "1.2", "0.3", "own", "3.1", "2.2", "1.3", "3.2", "2.3", "K0",
    "K1", "xA", "3.3", "K2", "JA", "fA0", "K3", "xB", "fA1", "JB",
    "fB0", "fA2", "fB1", "norm", "fA3", "fB2", "fB3",
)
VMEM = pl.BlockSpec(memory_space=pltpu.VMEM)
LIGHT = pl.CostEstimate(flops=1000, bytes_accessed=1000, transcendentals=0)
SMEM = pl.BlockSpec(memory_space=pltpu.SMEM)


def dot(a, b):
    return jnp.dot(a, b, preferred_element_type=F32)


def params(vmem_mib):
    return pltpu.CompilerParams(vmem_limit_bytes=vmem_mib * 1024 * 1024)


def first_head(pair, share):
    return (pair % 2) * share + 2 * (pair // 2)


def lanes(i):
    return slice(i * LANES, (i + 1) * LANES)


def valid_rows(first, rows, start, end):
    place = first + lax.broadcasted_iota(jnp.int32, (rows, LANES), 0)
    return jnp.where((place >= start) & (place < end), 1.0, 0.0).astype(F32)


def column(a, head):
    return jnp.broadcast_to(a[:, head : head + 1], (a.shape[0], LANES))


def split(a):
    upper = a.astype(BF16)
    return upper, (a - upper.astype(F32)).astype(BF16)


def project(chunk, ints, own, other, low, high, whole, padded, raw):
    block = low.shape[0] // 8
    start, end, first, core = ints[0], ints[1], ints[2], ints[3]
    for p in range(16):
        one, two = (
            sum(FLIPS[step] // 2 for i, step in enumerate(route) if (p >> i) & 1)
            for route in ROUTES[chunk]
        )
        chip = jnp.bitwise_xor(ints[5], jnp.where(core == 0, one, two))
        source = low if p < 8 else high
        row = pl.multiple_of(chip * block, block)
        whole[pl.ds(row, block), :] = source[(p % 8) * block : (p % 8 + 1) * block, :]
    span = other.shape[0]
    spans = [i for i in range(low.shape[1] // LANES) if raw is None or i != 1]
    mine = dot(own[...], whole[...])
    theirs = dot(other[...], whole[...])
    at_mine = pl.multiple_of(core * span, span)
    at_theirs = pl.multiple_of((1 - core) * span, span)
    ok_edge = valid_rows(first - 8, 8, start, end)
    ok_mine = valid_rows(first + at_mine, span, start, end)
    ok_theirs = valid_rows(first + at_theirs, span, start, end)

    def rounded(a, ok):
        return (a * ok).astype(BF16).astype(F32)

    for at, lane in enumerate(spans):
        edge = mine[0:HALO, lanes(lane)][HALO - 8 :]
        padded[at, 0:8, :] = rounded(edge, ok_edge)
        padded[at, pl.ds(8 + at_mine, span), :] = rounded(mine[HALO:, lanes(lane)], ok_mine)
        padded[at, pl.ds(8 + at_theirs, span), :] = rounded(theirs[:, lanes(lane)], ok_theirs)
    if raw is not None:
        raw[pl.ds(at_mine, span), :] = mine[HALO:, lanes(1)]
        raw[pl.ds(at_theirs, span), :] = theirs[:, lanes(1)]


def convolved(at, tap, group, taps, padded):
    total = taps[4:5, lanes(tap)]
    for k in range(4):
        rows = padded[at, group * GROUP + 5 + k : (group + 1) * GROUP + 5 + k, :]
        total = total + taps[k : k + 1, lanes(tap)] * rows
    half = 0.5 * total
    return (half + half * jnp.tanh(half)).astype(BF16)


def first_kernel(
    ints, own, other, low, high, taps, rates,
    bc_out, x_out, table_out, kt_out, tot_out,
    whole, padded, raw,
):
    project(0, ints, own, other, low, high, whole, padded, raw)
    row = lax.broadcasted_iota(jnp.int32, (GROUP, GROUP), 0)
    col = lax.broadcasted_iota(jnp.int32, (GROUP, GROUP), 1)
    below = jnp.where(row >= col, 1.0, 0.0).astype(BF16)
    before = jnp.zeros((1, LANES), F32)
    for group in range(bc_out.shape[0] // GROUP):
        rows = slice(group * GROUP, (group + 1) * GROUP)
        bc_out[rows, :] = convolved(0, 0, group, taps, padded)
        for at in range(1, padded.shape[0]):
            x_out[rows, lanes(at - 1)] = convolved(at, at, group, taps, padded)
        ok = valid_rows(ints[2] + group * GROUP, GROUP, ints[0], ints[1])
        step = raw[rows, :] + rates[0:1, :]
        size = (jnp.maximum(step, 0.0) + jnp.log1p(jnp.exp(-jnp.abs(step)))) * ok
        decay = size * rates[1:2, :]
        high_part, rest = split(decay)
        rest = decay - high_part.astype(F32)
        mid_part, low_part = split(rest)
        cum = dot(below, high_part) + dot(below, mid_part) + dot(below, low_part)
        from_key = jnp.log2(size) - cum
        kt_out[group] = from_key.T[0:32, :]
        lane = lax.broadcasted_iota(jnp.int32, (GROUP, LANES), 1)
        table = jnp.where(lane < KEYS, cum, pltpu.roll(from_key, KEYS, 1))
        table_out[rows, :] = jnp.where(lane < ROW, table, pltpu.roll(cum + before, ROW, 1))
        before = before + cum[GROUP - 1 : GROUP, :]
    tot_out[...] = jnp.broadcast_to(before, tot_out.shape)


def sorted_bc(ints, mine, theirs):
    first = ints[3] == 0
    return jnp.where(first, mine, theirs), jnp.where(first, theirs, mine)


def scan_kernel(
    chunk, held, heads, extra, ints, own, other, low, high, taps, x_ref, mine_ref, their_ref, table_ref,
    kt_ref, tot_ref, skip_ref, *refs,
):
    y_out, s_out, send_out, whole, padded, carry = refs[-6:]
    project(chunk, ints, own, other, low, high, whole, padded, None)
    base = 0
    for earlier in refs[:-6]:
        base = earlier.shape[1] // LANES
        send_out[:, 0 : base * LANES] = earlier[...]
    half = GROUP // 2
    row = lax.broadcasted_iota(jnp.int32, (half, half), 0)
    col = lax.broadcasted_iota(jnp.int32, (half, half), 1)
    causal = row >= col
    left = lax.broadcasted_iota(jnp.int32, (GROUP, LANES), 1) < LANES // 2
    zero = jnp.zeros((GROUP, LANES), BF16)
    for group in range(y_out.shape[0] // GROUP):
        rows = slice(group * GROUP, (group + 1) * GROUP)
        b, c = sorted_bc(ints, mine_ref[rows, :], their_ref[rows, :])
        scores = lax.dot_general(c, b, (((1,), (1,)), ((), ())), preferred_element_type=F32)
        table, kt = table_ref[rows, :], kt_ref[group]
        carried = None
        if group:
            upper, lower = split(carry[...])
            carried = dot(jnp.concatenate([c, c], axis=1), jnp.concatenate([upper, lower], axis=0))
        scaled, ends = [], []
        for i, head in enumerate(heads):
            if i < extra:
                x = x_ref[rows, lanes(i)]
            else:
                x = convolved(i - extra, held[i] + 1, group, taps, padded)
            top, bottom, spread = [], [], []
            for h in (head, head + 1):
                q = column(table, h)
                spread.append(q)
                k0 = jnp.broadcast_to(kt[h : h + 1, 0:half], (half, half))
                k1 = jnp.broadcast_to(kt[h : h + 1, half:], (half, half))
                m00 = jnp.where(causal, jnp.exp2(q[0:half] + k0) * scores[0:half, 0:half], 0.0)
                m10 = jnp.exp2(q[half:] + k0) * scores[half:, 0:half]
                m11 = jnp.where(causal, jnp.exp2(q[half:] + k1) * scores[half:, half:], 0.0)
                top.append(m00.astype(BF16))
                bottom.append(m10.astype(BF16))
                bottom.append(m11.astype(BF16))
            x0, x1 = jnp.where(left, x, zero), jnp.where(left, zero, x)
            y_top = dot(
                jnp.concatenate(top, axis=1), jnp.concatenate([x0[0:half], x1[0:half]], axis=0)
            )
            y_bottom = dot(jnp.concatenate(bottom, axis=1), jnp.concatenate([x0, x1], axis=0))
            q = jnp.where(left, spread[0], spread[1])
            xf = x.astype(F32)
            rest = skip_ref[2:3, lanes(held[i])] * xf
            if group:
                rest = rest + jnp.exp2(q) * carried[:, lanes(i)]
            y_out[group * GROUP : group * GROUP + half, lanes(i)] = y_top + rest[0:half]
            y_out[group * GROUP + half : (group + 1) * GROUP, lanes(i)] = y_bottom + rest[half:]
            k = jnp.where(left, column(table, KEYS + head), column(table, KEYS + head + 1))
            end = q[GROUP - 1 : GROUP, :]
            scaled.append((jnp.exp2(k + end) * xf).astype(BF16))
            ends.append(jnp.exp2(end))
        local = lax.dot_general(
            b, jnp.concatenate(scaled, axis=1), (((0,), (0,)), ((), ())), preferred_element_type=F32
        )
        if group:
            local = jnp.concatenate(ends, axis=1) * carry[...] + local
        carry[...] = local
    s_out[...] = carry[...]
    send_out[0:LANES, base * LANES :] = carry[...].astype(BF16)
    side = lax.broadcasted_iota(jnp.int32, (8, LANES), 1) < LANES // 2
    for i, head in enumerate(heads):
        total = jnp.where(side, column(tot_ref[...], head), column(tot_ref[...], head + 1))
        one, rest = split(total)
        two, three = split(total - one.astype(F32))
        place = lax.broadcasted_iota(jnp.int32, (8, LANES), 0)
        parts = jnp.where(place == 0, one.astype(F32), two.astype(F32))
        parts = jnp.where(place >= 2, three.astype(F32), parts)
        parts = jnp.where(place >= 3, 0.0, parts)
        send_out[LANES:, lanes(base + i)] = jnp.concatenate([parts, jnp.zeros_like(parts)], axis=0).astype(
            BF16
        )


def join_kernel(heads, sizes, halves, ints, mine_ref, their_ref, table_ref, tot_ref, r_ref, *refs):
    count = len(sizes)
    y_refs, s_refs = refs[:count], refs[count : 2 * count]
    send_out, keep_out, fin_out = refs[2 * count :]
    later = ints[4] > 0
    core = ints[3]
    where = [(j, k) for j, size in enumerate(sizes) for k in range(size)]
    span = send_out.shape[0]
    received = r_ref[0:LANES, :].astype(F32)
    entering = (received * jnp.where(later, 1.0, 0.0)).astype(BF16)
    from_head = lax.broadcasted_iota(jnp.int32, (2 * LANES, LANES), 0) % LANES
    second = lax.broadcasted_iota(jnp.int32, (2 * LANES, LANES), 1) // (LANES // 2)
    spread = jnp.concatenate(
        [jnp.where(from_head == ROW + head + second, 1.0, 0.0).astype(BF16) for head in heads], axis=1
    )
    for out, at in ((send_out, (1 - core) * span), (keep_out, core * span)):
        rows = pl.ds(pl.multiple_of(at, span), span)
        lane = lax.broadcasted_iota(jnp.int32, (span, LANES), 1)
        decay = jnp.exp2(jnp.where(lane < ROW, 0.0, table_ref[rows, :]))
        decay = dot(jnp.concatenate(split(decay), axis=1), spread)
        _, c = sorted_bc(ints, mine_ref[rows, :], their_ref[rows, :])
        carried = dot(c, entering)
        for i in range(len(heads)):
            j, k = where[i]
            out[:, lanes(i)] = (
                y_refs[j][rows, lanes(k)] + decay[:, lanes(i)] * carried[:, lanes(i)]
            )
    side = lax.broadcasted_iota(jnp.int32, (8, LANES), 1) < LANES // 2
    tot = tot_ref[...]
    for i, (early, late) in enumerate(halves):

        def own_state(p):
            j, k = where[p]
            return s_refs[j][:, lanes(k)]

        parts = r_ref[LANES:, lanes(early)].astype(F32)
        their_total = parts[0:1] + parts[1:2] + parts[2:3]
        my_total = jnp.where(side, column(tot, heads[late]), column(tot, heads[late] + 1))[0:1]
        at_first = jnp.exp2(their_total) * own_state(early) + received[:, lanes(early)]
        at_last = jnp.exp2(my_total) * received[:, lanes(late)] + own_state(late)
        both = jnp.where(later, at_last, at_first)
        fin_out[i * LANES : (i + 1) * LANES, :] = both.T.astype(fin_out.dtype)


def norm_kernel(places, ints, gain_ref, ka_ref, kb_ref, ra_ref, rb_ref, out_ref):
    step = pl.program_id(0)
    core = ints[3]
    rows = out_ref.shape[0]
    first = ints[2] + (core * pl.num_programs(0) + step) * rows
    ok = valid_rows(first, rows, ints[0], ints[1])
    blocks = []
    for who, refs in ((core, (ka_ref, kb_ref)), (1 - core, (ra_ref, rb_ref))):
        for ref, wheres in zip(refs, places, strict=True):
            for i, where in enumerate(wheres):
                at = pl.multiple_of((where + 5 * who) * LANES, LANES)
                blocks.append((at, ref, i))
    total = jnp.zeros((rows, LANES), F32)
    for _, ref, i in blocks:
        v = ref[:, lanes(i)]
        total = total + v * v
    mean = jnp.sum(total, axis=1, keepdims=True) * (1.0 / out_ref.shape[1])
    factor = lax.rsqrt(mean + EPS) * ok
    for at, ref, i in blocks:
        v = ref[:, lanes(i)]
        out_ref[:, pl.ds(at, LANES)] = (v * factor * gain_ref[0:1, pl.ds(at, LANES)]).astype(BF16)


def head_of(lane, core, share):
    return jnp.where(lane < 2 * share, lane + core * share + (lane // share) * share, -1)


def chosen_heads(core, heads, rows):
    row = lax.broadcasted_iota(jnp.int32, (rows, LANES), 0)
    lane = lax.broadcasted_iota(jnp.int32, (rows, LANES), 1)
    return jnp.where(row == head_of(lane, core, heads // 4), 1.0, 0.0)


def columns_of(source, core, inner):
    first = inner // 4 // LANES
    blocks = [inner // LANES + core]
    for i in range(first):
        blocks += [first * core + i, 2 * first + first * core + i]
    return [source[:, pl.ds(pl.multiple_of(at * LANES, LANES), LANES)] for at in blocks]


def sort_kernel(inner, ints, mix, step, kept_out, given_out):
    for out, core in ((kept_out, ints[1]), (given_out, 1 - ints[1])):
        parts = columns_of(mix, core, inner)
        out[:, lanes(0)] = parts[0]
        out[:, lanes(1)] = dot(step[...], chosen_heads(core, step.shape[1], step.shape[1]).astype(BF16)).astype(BF16)
        for i, part in enumerate(parts[1:]):
            out[:, lanes(2 + i)] = part


def stack_kernel(ints, kept, got, *outs):
    rows = kept.shape[0]
    core = ints[1]
    at = 0
    for out in outs:
        width = out.shape[1]
        out[pl.ds(pl.multiple_of(core * rows, rows), rows), :] = kept[:, at : at + width]
        out[pl.ds(pl.multiple_of((1 - core) * rows, rows), rows), :] = got[:, at : at + width]
        at += width


def settings_kernel(
    inner, place, deal, lengths, starts, small, ints_out, taps_out, rates_out, skip_out
):
    request, wanted, near = jnp.int32(0), jnp.int32(0), jnp.int32(0)
    req = place[4]
    for i in range(deal.shape[0]):
        request = jnp.where(req == i, deal[i], request)
        wanted = jnp.where(deal[i] == req, i, wanted)
        near = jnp.where(deal[i] == jnp.bitwise_xor(req, 1), i, near)
    start, length = jnp.int32(0), jnp.int32(0)
    for i in range(deal.shape[0]):
        start = jnp.where(request == i, starts[i], start)
        length = jnp.where(request == i, lengths[i], length)
    ints_out[0] = start
    ints_out[1] = start + length
    for i in range(4):
        ints_out[2 + i] = place[i]
    ints_out[6] = wanted
    ints_out[7] = near
    core = place[1]
    for i, part in enumerate(columns_of(small, core, inner)):
        row = lax.broadcasted_iota(jnp.int32, (8, LANES), 0)
        taps_out[:, lanes(i)] = jnp.where(row < 5, part[0:8], 0.0)
    heads = inner // LANES * 2
    exact = functools.partial(
        jnp.dot, precision=lax.Precision.HIGHEST, preferred_element_type=F32
    )
    own = exact(small[8:16, 0:LANES], chosen_heads(core, heads, LANES))
    rates_out[...] = own
    row = lax.broadcasted_iota(jnp.int32, (LANES, inner // 2), 0)
    lane = lax.broadcasted_iota(jnp.int32, (LANES, inner // 2), 1)
    pair, second = lane // LANES, (lane % LANES) // (LANES // 2)
    mine = (pair % 2) * (heads // 4) + 2 * (pair // 2) + second
    skip_out[...] = exact(own, jnp.where(row == mine, 1.0, 0.0))


def chosen(req, row, here, one, two):
    rel = jnp.bitwise_xor(row, req)
    far, near = (rel // 4) % 2 == 1, (rel // 2) % 2 == 1
    return jnp.where(
        near, jnp.where(far, two[1], two[0]), jnp.where(far, one[...], here[...])
    )


def pick_kernel(place, ints, here, one, two, out):
    out[...] = chosen(place[4], ints[7], here, one, two)


def last_kernel(place, ints, here, one, two, three, *refs):
    odd = jnp.bitwise_xor(ints[6], place[4]) % 2 == 1
    best = chosen(place[4], ints[6], here, one, two)
    out, base = refs[-1], 0
    for earlier in refs[:-1]:
        base = earlier.shape[0]
        out[0:base, :] = earlier[...]
    out[base:, :] = jnp.where(odd, three[...], best).astype(F32)


def swapped(x, masks):
    count = lax.axis_size("req") * lax.axis_size("seq")
    return lax.ppermute(x, AXES, [(i, i ^ masks[i % 2]) for i in range(count)])


def on_device(
    tokens, mix_weight, step_weight, conv_weight, conv_bias, step_bias, decay_rate, skip_gain,
    norm_gain, prompt_len, prompt_start, deal,
):
    seq_index = lax.axis_index("seq")
    req_index = lax.axis_index("req")
    core, along = seq_index % 2, seq_index // 2
    rows = tokens[0]
    span, depth = rows.shape
    inner = norm_gain.shape[0]
    heads = decay_rate.shape[0]
    head_dim = inner // heads
    nstate = (mix_weight.shape[1] - inner) // 2
    share = heads // 4
    quarter = inner // 4
    chip = req_index * 2 + along
    place = jnp.stack([along * 2 * span, core, along, chip, req_index])
    state = {}

    def after(*values):
        if "token" not in state:
            return values if len(values) > 1 else values[0]
        *out, state["token"] = lax.optimization_barrier((*values, state["token"]))
        return tuple(out) if len(out) > 1 else out[0]

    widths = [(len(held) + (2 if i == 0 else 0)) * LANES for i, held in enumerate(PAIRS)]
    total = sum(widths)
    portion = mix_weight.shape[0]
    kept, given = pl.pallas_call(
        functools.partial(sort_kernel, inner),
        in_specs=[SMEM, VMEM, VMEM],
        out_specs=[VMEM] * 2,
        out_shape=[jax.ShapeDtypeStruct((portion, total), BF16)] * 2,
        compiler_params=params(8),
        cost_estimate=LIGHT,
        name="sort",
    )(place, mix_weight, step_weight)
    got = swapped(given, (1, 1))
    blocks = pl.pallas_call(
        stack_kernel,
        in_specs=[SMEM, VMEM, VMEM],
        out_specs=[VMEM] * len(widths),
        out_shape=[jax.ShapeDtypeStruct((2 * portion, width), BF16) for width in widths],
        compiler_params=params(8),
        cost_estimate=LIGHT,
        name="stack",
    )(place, kept, got)
    blocks = list(blocks)
    arrived = [None] * len(widths)

    chip_rows = 2 * span
    groups = chip_rows // GROUP

    def scratch(width, spans):
        return [
            pltpu.VMEM((depth, width), BF16),
            pltpu.VMEM((spans, chip_rows + 8, LANES), F32),
        ]

    extra = len(PAIRS[0])

    def projected(ints, own, other, low, high, taps, rates):
        width = widths[0]
        return pl.pallas_call(
            first_kernel,
            in_specs=[SMEM] + [VMEM] * 6,
            out_specs=[VMEM] * 5,
            scratch_shapes=scratch(width, 1 + extra) + [pltpu.VMEM((chip_rows, LANES), F32)],
            out_shape=[
                jax.ShapeDtypeStruct((chip_rows, LANES), BF16),
                jax.ShapeDtypeStruct((chip_rows, extra * LANES), BF16),
                jax.ShapeDtypeStruct((chip_rows, LANES), F32),
                jax.ShapeDtypeStruct((groups, 32, GROUP), F32),
                jax.ShapeDtypeStruct((8, LANES), F32),
            ],
            compiler_params=params(28),
            cost_estimate=LIGHT,
            name="first",
        )(ints, own, other, low, high, taps, rates)

    def scanned(index, ints, own, other, low, high, taps, skip, x0, mine, theirs, table, kt, tot, *earlier):
        more = extra if index == 1 else 0
        held = (PAIRS[0] if more else ()) + PAIRS[index]
        pairs = len(held)
        new = pairs - more
        firsts = [first_head(p, share) for p in held]
        width = widths[index]
        return pl.pallas_call(
            functools.partial(scan_kernel, index, held, firsts, more),
            in_specs=[SMEM] + [VMEM] * (12 + len(earlier)),
            out_specs=[VMEM] * 3,
            scratch_shapes=scratch(width, new) + [pltpu.VMEM((LANES, pairs * LANES), F32)],
            out_shape=[
                jax.ShapeDtypeStruct((chip_rows, pairs * LANES), F32),
                jax.ShapeDtypeStruct((LANES, pairs * LANES), F32),
                jax.ShapeDtypeStruct(
                    (LANES + 16, pairs * LANES + sum(a.shape[1] for a in earlier)), BF16
                ),
            ],
            compiler_params=params(28),
            cost_estimate=LIGHT,
            name="scan",
        )(
            ints, own, other, low, high, taps,
            x0, mine, theirs, table, kt, tot, skip, *earlier,
        )

    def joined(held, ints, mine, theirs, table, tot, ys, ss, r):
        pairs = len(held)
        halves = [(i, i + 1) for i in range(0, pairs, 2)]
        sizes = [y.shape[1] // LANES for y in ys]
        return pl.pallas_call(
            functools.partial(join_kernel, [first_head(p, share) for p in held], sizes, halves),
            in_specs=[SMEM] + [VMEM] * (5 + 2 * len(ys)),
            out_specs=[VMEM] * 3,
            out_shape=[
                jax.ShapeDtypeStruct((span, pairs * LANES), F32),
                jax.ShapeDtypeStruct((span, pairs * LANES), F32),
                jax.ShapeDtypeStruct((len(halves) * LANES, nstate), BF16),
            ],
            compiler_params=params(28),
            cost_estimate=LIGHT,
            name="join",
        )(ints, mine, theirs, table, tot, r, *ys, *ss)

    early_pairs, late_pairs = sum(PAIRS[:CUT], ()), sum(PAIRS[CUT:], ())

    def normed(ints, keep_a, keep_b, got_a, got_b):
        places = [
            [(p % 2) * (2 * quarter // LANES) + p // 2 for p in held]
            for held in (early_pairs, late_pairs)
        ]
        block = span // 2
        return pl.pallas_call(
            functools.partial(norm_kernel, places),
            grid_spec=pltpu.PrefetchScalarGridSpec(
                num_scalar_prefetch=1,
                grid=(span // block,),
                in_specs=[pl.BlockSpec((1, inner), lambda i, ints: (0, 0))]
                + [
                    pl.BlockSpec((block, a.shape[1]), lambda i, ints: (i, 0))
                    for a in (keep_a, keep_b, got_a, got_b)
                ],
                out_specs=pl.BlockSpec((block, inner), lambda i, ints: (i, 0)),
            ),
            out_shape=jax.ShapeDtypeStruct((span, inner), BF16),
            compiler_params=params(28),
            cost_estimate=LIGHT,
            name="norm",
        )(ints, norm_gain[None], keep_a, keep_b, got_a, got_b)

    def picked(kernel, kind, *arrays, more=0):
        return pl.pallas_call(
            kernel,
            in_specs=[SMEM] * 2 + [VMEM] * len(arrays),
            out_specs=VMEM,
            out_shape=jax.ShapeDtypeStruct((arrays[0].shape[0] + more, nstate), kind),
            compiler_params=params(8),
            cost_estimate=LIGHT,
            name="pick",
        )(place, v["ints"], *arrays)

    v = state
    last = len(PAIRS) - 1
    for event in SCHEDULE:
        if event[0].isdigit():
            i, step = (int(part) for part in event.split("."))
            if step:
                blocks[i] = jnp.concatenate(after(blocks[i], arrived[i]), axis=0)
                v["token"] = blocks[i]
            route = ROUTES[i]
            arrived[i] = swapped(blocks[i], (FLIPS[route[0][step]], FLIPS[route[1][step]]))
        elif event == "tokens":
            given_rows, _ = lax.optimization_barrier((rows, blocks[0]))
            v["other"] = swapped(given_rows, (1, 1))
        elif event == "halo":
            other = after(v["other"])
            edge = jnp.where(core == 1, rows[span - HALO :], other[span - HALO :])
            count = lax.axis_size("req") * lax.axis_size("seq")
            route = [(i, i + 2) for i in range(count) if (i // 2) % 2 == 0]
            v["token"] = edge
            v["halo"] = lax.ppermute(edge, AXES, route)
        elif event == "settings":
            half = inner // 2

            conv_w, conv_b, step_b, rate, gain = after(
                conv_weight, conv_bias, step_bias, decay_rate, skip_gain
            )

            def row(values):
                return jnp.pad(values, (0, conv_weight.shape[1] - values.shape[0]))[None]

            small = jnp.concatenate(
                [conv_w, conv_b[None], jnp.zeros((3, conv_w.shape[1]), F32)]
                + [row(step_b), row(rate * (-LOG2E)), row(gain)]
                + [jnp.zeros((5, conv_weight.shape[1]), F32)],
                axis=0,
            )
            v["ints"], v["taps"], v["rates"], v["skip"] = pl.pallas_call(
                functools.partial(settings_kernel, inner),
                in_specs=[SMEM] * 4 + [VMEM],
                out_specs=[SMEM] + [VMEM] * 3,
                out_shape=[
                    jax.ShapeDtypeStruct((8,), jnp.int32),
                    jax.ShapeDtypeStruct((8, half + LANES), F32),
                    jax.ShapeDtypeStruct((8, LANES), F32),
                    jax.ShapeDtypeStruct((8, half), F32),
                ],
                compiler_params=params(8),
                cost_estimate=LIGHT,
                name="settings",
            )(after(place), deal, prompt_len, prompt_start, small)
            v["token"] = v["rates"]
        elif event == "own":
            v["own"] = jnp.concatenate([after(v["halo"]), rows], axis=0)
            v["token"] = v["own"]
        elif event == "K0":
            ints = after(v["ints"])
            bc, x0, table, kt, tot = projected(
                ints, v["own"], v["other"], blocks[0], arrived[0], v["taps"], v["rates"]
            )
            v["token"] = tot
            v["bc"] = swapped(bc, (1, 1))
        elif event[0] == "K":
            i = int(event[1:])
            if i == 1:
                theirs = after(v["bc"])
            ints = after(v["ints"])
            v["y", i], v["s", i], v["t", i] = scanned(
                i, ints, v["own"], v["other"], blocks[i], arrived[i], v["taps"], v["skip"],
                x0, bc, theirs, table, kt, tot, *([v["t", i - 1]] if i > 1 and i != CUT else []),
            )
            v["token"] = v["t", i]
        elif event in ("xA", "xB"):
            v["r", event[1]] = swapped(v["t", CUT - 1 if event == "xA" else last], (2, 2))
        elif event in ("JA", "JB"):
            which = range(1, CUT) if event == "JA" else range(CUT, last + 1)
            held = early_pairs if event == "JA" else late_pairs
            ints, r = after(v["ints"], v["r", event[1]])
            send, v["keep", event[1]], v["fin", event[1]] = joined(
                held, ints, bc, theirs, table, tot, [v["y", i] for i in which], [v["s", i] for i in which], r
            )
            v["token"] = v["fin", event[1]]
            v["got", event[1]] = swapped(send, (1, 1))
        elif event[0] == "f":
            key = event[1]
            if event[2] == "0":
                v["one", key] = swapped(v["fin", key], (16, 16))
            elif event[2] == "1":
                v["pair", key] = jnp.stack(after(v["fin", key], v["one", key]))
                v["token"] = v["pair", key]
                v["two", key] = swapped(v["pair", key], (8, 8))
            elif event[2] == "2":
                cand = (v["fin", key], v["one", key], after(v["two", key]))
                v["cand", key] = cand
                v["picked", key] = picked(pick_kernel, BF16, *cand)
                v["token"] = v["picked", key]
                v["three", key] = swapped(v["picked", key], (4, 4))
            else:
                three = after(v["three", key])
                earlier = [v["final", "A"]] if key == "B" else []
                more = sum(a.shape[0] for a in earlier)
                v["final", key] = picked(
                    last_kernel, F32, *v["cand", key], three, *earlier, more=more
                )
                v["token"] = v["final", key]
        else:
            ints = after(v["ints"])
            result = normed(ints, v["keep", "A"], v["keep", "B"], v["got", "A"], v["got", "B"])
            v["token"] = result
    return (result[None], v["final", "B"].reshape(1, share, head_dim, nstate))


def passed_along(block, axis, distance):
    devices = range(lax.axis_size(axis))
    route = [(i - distance, i) for i in devices if i - distance in devices]
    return lax.ppermute(block, axis, route)


def carried_in(part, axis, combine, identity):
    place = lax.axis_index(axis)
    gathered = jax.tree.map(lambda a: lax.all_gather(a, axis), part)
    state = jax.tree.map(lambda a, e: jnp.zeros_like(a) + jnp.asarray(e, a.dtype), part, identity)

    def one(step, state):
        return combine(
            state, jax.tree.map(lambda a: lax.dynamic_index_in_dim(a, step, 0, False), gathered)
        )

    return lax.fori_loop(0, place, one, state)


def broadcast(x, axis, root):
    mine = lax.axis_index(axis) == root
    return lax.psum(jnp.where(mine, x, jnp.zeros_like(x)), axis)


def on_device_general(
    tokens,
    mix_weight,
    step_weight,
    conv_weight,
    conv_bias,
    step_bias,
    decay_rate,
    skip_gain,
    norm_gain,
    prompt_len,
    prompt_start,
    deal,
):
    seq_count = lax.axis_size("seq")
    seq_index = lax.axis_index("seq")
    req_index = lax.axis_index("req")
    rows = tokens[0]
    span = rows.shape[0]
    total_reqs = deal.shape[0]
    slots = jnp.arange(total_reqs, dtype=jnp.int32)
    request = jnp.sum(jnp.where(slots == req_index, deal, 0))
    length = jnp.sum(jnp.where(slots == request, prompt_len, 0))
    start = jnp.sum(jnp.where(slots == request, prompt_start, 0))
    place = seq_index * span + jnp.arange(span, dtype=jnp.int32)
    valid = ((place >= start) & (place < start + length)).astype(jnp.float32)
    whole_mix, whole_step = (
        lax.all_gather(mix_weight, ("req", "seq"), axis=0, tiled=True),
        lax.all_gather(step_weight, ("req", "seq"), axis=0, tiled=True),
    )
    mixed = jnp.dot(rows, whole_mix, preferred_element_type=jnp.float32)
    raw_step = jnp.dot(rows, whole_step, preferred_element_type=jnp.float32)
    mixed = (mixed * valid[:, None]).astype(jnp.bfloat16)
    taps = conv_weight.shape[0]
    edge = passed_along(mixed[span - (taps - 1) :], "seq", 1)
    padded = jnp.concatenate([edge, mixed], axis=0)
    conv_sum = jnp.zeros(mixed.shape, jnp.float32) + conv_bias[None, :]
    for offset in range(taps):
        conv_sum = conv_sum + conv_weight[offset][None, :] * padded[offset : offset + span].astype(
            jnp.float32
        )
    convolved = jax.nn.silu(conv_sum).astype(jnp.bfloat16)
    heads = decay_rate.shape[0]
    inner = norm_gain.shape[0]
    head_dim = inner // heads
    nstate = (mixed.shape[1] - inner) // 2
    blocks = span // GROUP
    inputs = convolved[:, :inner].reshape(span, heads, head_dim)
    mixed_b = convolved[:, inner : inner + nstate]
    mixed_c = convolved[:, inner + nstate :]
    step_size = jax.nn.softplus(raw_step + step_bias[None, :]) * valid[:, None]
    pieces = (
        inputs.reshape(blocks, GROUP, heads, head_dim),
        mixed_b.reshape(blocks, GROUP, nstate),
        mixed_c.reshape(blocks, GROUP, nstate),
        step_size.reshape(blocks, GROUP, heads),
    )

    def local_group(block):
        part_in, part_b, part_c, part_step = block
        cum_decay = jnp.cumsum(-part_step * decay_rate[None, :], axis=0)
        places = jnp.arange(GROUP, dtype=jnp.int32)
        causal = places[:, None] >= places[None, :]
        spread = cum_decay[:, None, :] - cum_decay[None, :, :]
        spread = jnp.where(causal[:, :, None], spread, -1e30)
        scores = jnp.einsum("qn,kn->qk", part_c, part_b, preferred_element_type=jnp.float32)
        mixing = (jnp.exp(spread) * scores[:, :, None] * part_step[None, :, :]).astype(jnp.bfloat16)
        inner_out = jnp.einsum("qkh,khp->qhp", mixing, part_in, preferred_element_type=jnp.float32)
        to_end = jnp.exp(cum_decay[-1][None, :] - cum_decay) * part_step
        scaled = (to_end[:, :, None] * part_in.astype(jnp.float32)).astype(jnp.bfloat16)
        local = jnp.einsum("khp,kn->hpn", scaled, part_b, preferred_element_type=jnp.float32)
        return (inner_out, cum_decay, local)

    inner_out, cum_decay, group_state = lax.map(local_group, pieces)
    totals = cum_decay[:, -1, :]

    def advance(carry, item):
        group_total, group_local = item
        return (jnp.exp(group_total)[:, None, None] * carry + group_local, carry)

    dev_state, entry_zero = lax.scan(
        advance, jnp.zeros((heads, head_dim, nstate), jnp.float32), (totals, group_state)
    )
    before = jnp.cumsum(totals, axis=0) - totals
    dev_decay = jnp.exp(jnp.sum(totals, axis=0))

    def chain(earlier, later):
        return (earlier[0] * later[0], later[0][:, None, None] * earlier[1] + later[1])

    incoming_decay, incoming = carried_in(
        (dev_decay, dev_state), "seq", chain, (jnp.ones_like(dev_decay), jnp.zeros_like(dev_state))
    )
    entry = entry_zero + jnp.exp(before)[:, :, None, None] * incoming[None]
    carried = jnp.einsum(
        "cqn,chpn->cqhp", pieces[2].astype(jnp.float32), entry, precision=lax.Precision.HIGHEST
    )
    carried = carried * jnp.exp(cum_decay)[:, :, :, None]
    outputs = (inner_out + carried).reshape(span, heads, head_dim) + skip_gain[
        None, :, None
    ] * inputs.astype(jnp.float32)
    flat = outputs.reshape(span, inner)
    factor = lax.rsqrt(jnp.mean(flat * flat, axis=1, keepdims=True) + EPS)
    result = (flat * factor * norm_gain[None, :] * valid[:, None]).astype(jnp.bfloat16)[None]
    share = heads // seq_count
    leaving = dev_decay[:, None, None] * incoming + dev_state
    last_state = broadcast(leaving, "seq", seq_count - 1)
    own_state = lax.dynamic_slice_in_dim(last_state, seq_index * share, share, 0)[None]
    wanted = jnp.sum(jnp.where(deal == req_index, slots, 0))
    piece = lax.all_gather(own_state, "req", axis=0, tiled=True)
    count = piece.shape[0]
    chosen = jnp.arange(count, dtype=jnp.int32) == wanted
    final_state = jnp.zeros_like(own_state) + jnp.sum(
        jnp.where(chosen[:, None, None, None], piece, 0.0), axis=0, keepdims=True
    )
    return (result, final_state)


def solution(mesh):
    fits = mesh.shape["req"] == 8 and mesh.shape["seq"] == 4
    return jax.shard_map(
        on_device if fits else on_device_general,
        mesh=mesh,
        in_specs=(
            P("req", "seq", None),
            P(("req", "seq"), None),
            P(("req", "seq"), None),
        )
        + (P(),) * 9,
        out_specs=(P("req", "seq", None), P("req", "seq", None, None)),
        check_vma=False,
    )
```

```python
import functools

import jax
import jax.numpy as jnp
from jax import lax
from jax.experimental import pallas as pl
from jax.experimental.pallas import tpu as pltpu
from jax.sharding import PartitionSpec as P

GROUP = 256
EPS = 1e-05
LOG2E = 1.4426950408889634
LANES = 128
HALO = 16
KEYS, ROW = 32, 64
F32 = jnp.float32
BF16 = jnp.bfloat16
AXES = ("req", "seq")
FLIPS = {"a": 16, "b": 8, "y": 4, "x": 2}
ROUTES = (("axyb", "abxy"), ("abyx", "axby"), ("ayxb", "abyx"), ("axyb", "abxy"))
PAIRS = ((0,), (1, 2, 3), (4, 5, 6, 7), (8, 9))
CUT = 2
SCHEDULE = (
    "0.0", "1.0", "settings", "tokens", "0.1", "2.0", "1.1", "0.2", "halo", "3.0",
    "2.1", "1.2", "0.3", "own", "3.1", "2.2", "1.3", "3.2", "2.3", "K0",
    "K1", "xA", "3.3", "K2", "JA", "fA0", "K3", "xB", "fA1", "JB",
    "fB0", "fA2", "fB1", "norm", "fA3", "fB2", "fB3",
)
VMEM = pl.BlockSpec(memory_space=pltpu.VMEM)
LIGHT = pl.CostEstimate(flops=1000, bytes_accessed=1000, transcendentals=0)
SMEM = pl.BlockSpec(memory_space=pltpu.SMEM)


def dot(a, b):
    return jnp.dot(a, b, preferred_element_type=F32)


def params(vmem_mib):
    return pltpu.CompilerParams(vmem_limit_bytes=vmem_mib * 1024 * 1024)


def first_head(pair, share):
    return (pair % 2) * share + 2 * (pair // 2)


def lanes(i):
    return slice(i * LANES, (i + 1) * LANES)


def valid_rows(first, rows, start, end):
    place = first + lax.broadcasted_iota(jnp.int32, (rows, LANES), 0)
    return jnp.where((place >= start) & (place < end), 1.0, 0.0).astype(F32)


def column(a, head):
    return jnp.broadcast_to(a[:, head : head + 1], (a.shape[0], LANES))


def split(a):
    upper = a.astype(BF16)
    return upper, (a - upper.astype(F32)).astype(BF16)


def project(chunk, ints, own, other, low, high, whole, padded, raw):
    block = low.shape[0] // 8
    start, end, first, core = ints[0], ints[1], ints[2], ints[3]
    for p in range(16):
        one, two = (
            sum(FLIPS[step] // 2 for i, step in enumerate(route) if (p >> i) & 1)
            for route in ROUTES[chunk]
        )
        chip = jnp.bitwise_xor(ints[5], jnp.where(core == 0, one, two))
        source = low if p < 8 else high
        row = pl.multiple_of(chip * block, block)
        whole[pl.ds(row, block), :] = source[(p % 8) * block : (p % 8 + 1) * block, :]
    span = other.shape[0]
    spans = [i for i in range(low.shape[1] // LANES) if raw is None or i != 1]
    mine = dot(own[...], whole[...])
    theirs = dot(other[...], whole[...])
    at_mine = pl.multiple_of(core * span, span)
    at_theirs = pl.multiple_of((1 - core) * span, span)
    ok_edge = valid_rows(first - 8, 8, start, end)
    ok_mine = valid_rows(first + at_mine, span, start, end)
    ok_theirs = valid_rows(first + at_theirs, span, start, end)

    def rounded(a, ok):
        return (a * ok).astype(BF16).astype(F32)

    for at, lane in enumerate(spans):
        edge = mine[0:HALO, lanes(lane)][HALO - 8 :]
        padded[at, 0:8, :] = rounded(edge, ok_edge)
        padded[at, pl.ds(8 + at_mine, span), :] = rounded(mine[HALO:, lanes(lane)], ok_mine)
        padded[at, pl.ds(8 + at_theirs, span), :] = rounded(theirs[:, lanes(lane)], ok_theirs)
    if raw is not None:
        raw[pl.ds(at_mine, span), :] = mine[HALO:, lanes(1)]
        raw[pl.ds(at_theirs, span), :] = theirs[:, lanes(1)]


def convolved(at, tap, group, taps, padded):
    total = taps[4:5, lanes(tap)]
    for k in range(4):
        rows = padded[at, group * GROUP + 5 + k : (group + 1) * GROUP + 5 + k, :]
        total = total + taps[k : k + 1, lanes(tap)] * rows
    half = 0.5 * total
    return (half + half * jnp.tanh(half)).astype(BF16)


def first_kernel(
    ints, own, other, low, high, taps, rates,
    bc_out, x_out, table_out, kt_out, tot_out,
    whole, padded, raw,
):
    project(0, ints, own, other, low, high, whole, padded, raw)
    row = lax.broadcasted_iota(jnp.int32, (GROUP, GROUP), 0)
    col = lax.broadcasted_iota(jnp.int32, (GROUP, GROUP), 1)
    below = jnp.where(row >= col, 1.0, 0.0).astype(BF16)
    before = jnp.zeros((1, LANES), F32)
    for group in range(bc_out.shape[0] // GROUP):
        rows = slice(group * GROUP, (group + 1) * GROUP)
        bc_out[rows, :] = convolved(0, 0, group, taps, padded)
        for at in range(1, padded.shape[0]):
            x_out[rows, lanes(at - 1)] = convolved(at, at, group, taps, padded)
        ok = valid_rows(ints[2] + group * GROUP, GROUP, ints[0], ints[1])
        step = raw[rows, :] + rates[0:1, :]
        size = (jnp.maximum(step, 0.0) + jnp.log1p(jnp.exp(-jnp.abs(step)))) * ok
        decay = size * rates[1:2, :]
        high_part, rest = split(decay)
        rest = decay - high_part.astype(F32)
        mid_part, low_part = split(rest)
        cum = dot(below, high_part) + dot(below, mid_part) + dot(below, low_part)
        from_key = jnp.log2(size) - cum
        kt_out[group] = from_key.T[0:32, :]
        lane = lax.broadcasted_iota(jnp.int32, (GROUP, LANES), 1)
        table = jnp.where(lane < KEYS, cum, pltpu.roll(from_key, KEYS, 1))
        table_out[rows, :] = jnp.where(lane < ROW, table, pltpu.roll(cum + before, ROW, 1))
        before = before + cum[GROUP - 1 : GROUP, :]
    tot_out[...] = jnp.broadcast_to(before, tot_out.shape)


def sorted_bc(ints, mine, theirs):
    first = ints[3] == 0
    return jnp.where(first, mine, theirs), jnp.where(first, theirs, mine)


def scan_kernel(
    chunk, held, heads, extra, ints, own, other, low, high, taps, x_ref, mine_ref, their_ref, table_ref,
    kt_ref, tot_ref, skip_ref, *refs,
):
    y_out, s_out, send_out, whole, padded, carry = refs[-6:]
    project(chunk, ints, own, other, low, high, whole, padded, None)
    base = 0
    for earlier in refs[:-6]:
        base = earlier.shape[1] // LANES
        send_out[:, 0 : base * LANES] = earlier[...]
    half = GROUP // 2
    row = lax.broadcasted_iota(jnp.int32, (half, half), 0)
    col = lax.broadcasted_iota(jnp.int32, (half, half), 1)
    causal = row >= col
    left = lax.broadcasted_iota(jnp.int32, (GROUP, LANES), 1) < LANES // 2
    zero = jnp.zeros((GROUP, LANES), BF16)
    for group in range(y_out.shape[0] // GROUP):
        rows = slice(group * GROUP, (group + 1) * GROUP)
        b, c = sorted_bc(ints, mine_ref[rows, :], their_ref[rows, :])
        scores = lax.dot_general(c, b, (((1,), (1,)), ((), ())), preferred_element_type=F32)
        table, kt = table_ref[rows, :], kt_ref[group]
        carried = None
        if group:
            upper, lower = split(carry[...])
            carried = dot(jnp.concatenate([c, c], axis=1), jnp.concatenate([upper, lower], axis=0))
        scaled, ends = [], []
        for i, head in enumerate(heads):
            if i < extra:
                x = x_ref[rows, lanes(i)]
            else:
                x = convolved(i - extra, held[i] + 1, group, taps, padded)
            top, bottom, spread = [], [], []
            for h in (head, head + 1):
                q = column(table, h)
                spread.append(q)
                k0 = jnp.broadcast_to(kt[h : h + 1, 0:half], (half, half))
                k1 = jnp.broadcast_to(kt[h : h + 1, half:], (half, half))
                m00 = jnp.where(causal, jnp.exp2(q[0:half] + k0) * scores[0:half, 0:half], 0.0)
                m10 = jnp.exp2(q[half:] + k0) * scores[half:, 0:half]
                m11 = jnp.where(causal, jnp.exp2(q[half:] + k1) * scores[half:, half:], 0.0)
                top.append(m00.astype(BF16))
                bottom.append(m10.astype(BF16))
                bottom.append(m11.astype(BF16))
            x0, x1 = jnp.where(left, x, zero), jnp.where(left, zero, x)
            y_top = dot(
                jnp.concatenate(top, axis=1), jnp.concatenate([x0[0:half], x1[0:half]], axis=0)
            )
            y_bottom = dot(jnp.concatenate(bottom, axis=1), jnp.concatenate([x0, x1], axis=0))
            q = jnp.where(left, spread[0], spread[1])
            xf = x.astype(F32)
            rest = skip_ref[2:3, lanes(held[i])] * xf
            if group:
                rest = rest + jnp.exp2(q) * carried[:, lanes(i)]
            y_out[group * GROUP : group * GROUP + half, lanes(i)] = y_top + rest[0:half]
            y_out[group * GROUP + half : (group + 1) * GROUP, lanes(i)] = y_bottom + rest[half:]
            k = jnp.where(left, column(table, KEYS + head), column(table, KEYS + head + 1))
            end = q[GROUP - 1 : GROUP, :]
            scaled.append((jnp.exp2(k + end) * xf).astype(BF16))
            ends.append(jnp.exp2(end))
        local = lax.dot_general(
            b, jnp.concatenate(scaled, axis=1), (((0,), (0,)), ((), ())), preferred_element_type=F32
        )
        if group:
            local = jnp.concatenate(ends, axis=1) * carry[...] + local
        carry[...] = local
    s_out[...] = carry[...]
    send_out[0:LANES, base * LANES :] = carry[...].astype(BF16)
    side = lax.broadcasted_iota(jnp.int32, (8, LANES), 1) < LANES // 2
    for i, head in enumerate(heads):
        total = jnp.where(side, column(tot_ref[...], head), column(tot_ref[...], head + 1))
        one, rest = split(total)
        two, three = split(total - one.astype(F32))
        place = lax.broadcasted_iota(jnp.int32, (8, LANES), 0)
        parts = jnp.where(place == 0, one.astype(F32), two.astype(F32))
        parts = jnp.where(place >= 2, three.astype(F32), parts)
        parts = jnp.where(place >= 3, 0.0, parts)
        send_out[LANES:, lanes(base + i)] = jnp.concatenate([parts, jnp.zeros_like(parts)], axis=0).astype(
            BF16
        )


def join_kernel(heads, sizes, halves, ints, mine_ref, their_ref, table_ref, tot_ref, r_ref, *refs):
    count = len(sizes)
    y_refs, s_refs = refs[:count], refs[count : 2 * count]
    send_out, keep_out, fin_out = refs[2 * count :]
    later = ints[4] > 0
    core = ints[3]
    where = [(j, k) for j, size in enumerate(sizes) for k in range(size)]
    span = send_out.shape[0]
    received = r_ref[0:LANES, :].astype(F32)
    entering = (received * jnp.where(later, 1.0, 0.0)).astype(BF16)
    from_head = lax.broadcasted_iota(jnp.int32, (2 * LANES, LANES), 0) % LANES
    second = lax.broadcasted_iota(jnp.int32, (2 * LANES, LANES), 1) // (LANES // 2)
    spread = jnp.concatenate(
        [jnp.where(from_head == ROW + head + second, 1.0, 0.0).astype(BF16) for head in heads], axis=1
    )
    for out, at in ((send_out, (1 - core) * span), (keep_out, core * span)):
        rows = pl.ds(pl.multiple_of(at, span), span)
        lane = lax.broadcasted_iota(jnp.int32, (span, LANES), 1)
        decay = jnp.exp2(jnp.where(lane < ROW, 0.0, table_ref[rows, :]))
        decay = dot(jnp.concatenate(split(decay), axis=1), spread)
        _, c = sorted_bc(ints, mine_ref[rows, :], their_ref[rows, :])
        carried = dot(c, entering)
        for i in range(len(heads)):
            j, k = where[i]
            out[:, lanes(i)] = (
                y_refs[j][rows, lanes(k)] + decay[:, lanes(i)] * carried[:, lanes(i)]
            )
    side = lax.broadcasted_iota(jnp.int32, (8, LANES), 1) < LANES // 2
    tot = tot_ref[...]
    for i, (early, late) in enumerate(halves):

        def own_state(p):
            j, k = where[p]
            return s_refs[j][:, lanes(k)]

        parts = r_ref[LANES:, lanes(early)].astype(F32)
        their_total = parts[0:1] + parts[1:2] + parts[2:3]
        my_total = jnp.where(side, column(tot, heads[late]), column(tot, heads[late] + 1))[0:1]
        at_first = jnp.exp2(their_total) * own_state(early) + received[:, lanes(early)]
        at_last = jnp.exp2(my_total) * received[:, lanes(late)] + own_state(late)
        both = jnp.where(later, at_last, at_first)
        fin_out[i * LANES : (i + 1) * LANES, :] = both.T.astype(fin_out.dtype)


def norm_kernel(places, ints, gain_ref, ka_ref, kb_ref, ra_ref, rb_ref, out_ref):
    step = pl.program_id(0)
    core = ints[3]
    rows = out_ref.shape[0]
    first = ints[2] + (core * pl.num_programs(0) + step) * rows
    ok = valid_rows(first, rows, ints[0], ints[1])
    blocks = []
    for who, refs in ((core, (ka_ref, kb_ref)), (1 - core, (ra_ref, rb_ref))):
        for ref, wheres in zip(refs, places, strict=True):
            for i, where in enumerate(wheres):
                at = pl.multiple_of((where + 5 * who) * LANES, LANES)
                blocks.append((at, ref, i))
    total = jnp.zeros((rows, LANES), F32)
    for _, ref, i in blocks:
        v = ref[:, lanes(i)]
        total = total + v * v
    mean = jnp.sum(total, axis=1, keepdims=True) * (1.0 / out_ref.shape[1])
    factor = lax.rsqrt(mean + EPS) * ok
    for at, ref, i in blocks:
        v = ref[:, lanes(i)]
        out_ref[:, pl.ds(at, LANES)] = (v * factor * gain_ref[0:1, pl.ds(at, LANES)]).astype(BF16)


def head_of(lane, core, share):
    return jnp.where(lane < 2 * share, lane + core * share + (lane // share) * share, -1)


def chosen_heads(core, heads, rows):
    row = lax.broadcasted_iota(jnp.int32, (rows, LANES), 0)
    lane = lax.broadcasted_iota(jnp.int32, (rows, LANES), 1)
    return jnp.where(row == head_of(lane, core, heads // 4), 1.0, 0.0)


def columns_of(source, core, inner):
    first = inner // 4 // LANES
    blocks = [inner // LANES + core]
    for i in range(first):
        blocks += [first * core + i, 2 * first + first * core + i]
    return [source[:, pl.ds(pl.multiple_of(at * LANES, LANES), LANES)] for at in blocks]


def sort_kernel(inner, ints, mix, step, kept_out, given_out):
    for out, core in ((kept_out, ints[1]), (given_out, 1 - ints[1])):
        parts = columns_of(mix, core, inner)
        out[:, lanes(0)] = parts[0]
        out[:, lanes(1)] = dot(step[...], chosen_heads(core, step.shape[1], step.shape[1]).astype(BF16)).astype(BF16)
        for i, part in enumerate(parts[1:]):
            out[:, lanes(2 + i)] = part


def stack_kernel(ints, kept, got, *outs):
    rows = kept.shape[0]
    core = ints[1]
    at = 0
    for out in outs:
        width = out.shape[1]
        out[pl.ds(pl.multiple_of(core * rows, rows), rows), :] = kept[:, at : at + width]
        out[pl.ds(pl.multiple_of((1 - core) * rows, rows), rows), :] = got[:, at : at + width]
        at += width


def settings_kernel(
    inner, place, deal, lengths, starts, small, ints_out, taps_out, rates_out, skip_out
):
    request, wanted, near = jnp.int32(0), jnp.int32(0), jnp.int32(0)
    req = place[4]
    for i in range(deal.shape[0]):
        request = jnp.where(req == i, deal[i], request)
        wanted = jnp.where(deal[i] == req, i, wanted)
        near = jnp.where(deal[i] == jnp.bitwise_xor(req, 1), i, near)
    start, length = jnp.int32(0), jnp.int32(0)
    for i in range(deal.shape[0]):
        start = jnp.where(request == i, starts[i], start)
        length = jnp.where(request == i, lengths[i], length)
    ints_out[0] = start
    ints_out[1] = start + length
    for i in range(4):
        ints_out[2 + i] = place[i]
    ints_out[6] = wanted
    ints_out[7] = near
    core = place[1]
    for i, part in enumerate(columns_of(small, core, inner)):
        row = lax.broadcasted_iota(jnp.int32, (8, LANES), 0)
        taps_out[:, lanes(i)] = jnp.where(row < 5, part[0:8], 0.0)
    heads = inner // LANES * 2
    exact = functools.partial(
        jnp.dot, precision=lax.Precision.HIGHEST, preferred_element_type=F32
    )
    own = exact(small[8:16, 0:LANES], chosen_heads(core, heads, LANES))
    rates_out[...] = own
    row = lax.broadcasted_iota(jnp.int32, (LANES, inner // 2), 0)
    lane = lax.broadcasted_iota(jnp.int32, (LANES, inner // 2), 1)
    pair, second = lane // LANES, (lane % LANES) // (LANES // 2)
    mine = (pair % 2) * (heads // 4) + 2 * (pair // 2) + second
    skip_out[...] = exact(own, jnp.where(row == mine, 1.0, 0.0))


def chosen(req, row, here, one, two):
    rel = jnp.bitwise_xor(row, req)
    far, near = (rel // 4) % 2 == 1, (rel // 2) % 2 == 1
    return jnp.where(
        near, jnp.where(far, two[1], two[0]), jnp.where(far, one[...], here[...])
    )


def pick_kernel(place, ints, here, one, two, out):
    out[...] = chosen(place[4], ints[7], here, one, two)


def last_kernel(place, ints, here, one, two, three, *refs):
    odd = jnp.bitwise_xor(ints[6], place[4]) % 2 == 1
    best = chosen(place[4], ints[6], here, one, two)
    out, base = refs[-1], 0
    for earlier in refs[:-1]:
        base = earlier.shape[0]
        out[0:base, :] = earlier[...]
    out[base:, :] = jnp.where(odd, three[...], best).astype(F32)


def swapped(x, masks):
    count = lax.axis_size("req") * lax.axis_size("seq")
    return lax.ppermute(x, AXES, [(i, i ^ masks[i % 2]) for i in range(count)])


def on_device(
    tokens, mix_weight, step_weight, conv_weight, conv_bias, step_bias, decay_rate, skip_gain,
    norm_gain, prompt_len, prompt_start, deal,
):
    seq_index = lax.axis_index("seq")
    req_index = lax.axis_index("req")
    core, along = seq_index % 2, seq_index // 2
    rows = tokens[0]
    span, depth = rows.shape
    inner = norm_gain.shape[0]
    heads = decay_rate.shape[0]
    head_dim = inner // heads
    nstate = (mix_weight.shape[1] - inner) // 2
    share = heads // 4
    quarter = inner // 4
    chip = req_index * 2 + along
    place = jnp.stack([along * 2 * span, core, along, chip, req_index])
    state = {}

    def after(*values):
        if "token" not in state:
            return values if len(values) > 1 else values[0]
        *out, state["token"] = lax.optimization_barrier((*values, state["token"]))
        return tuple(out) if len(out) > 1 else out[0]

    widths = [(len(held) + (2 if i == 0 else 0)) * LANES for i, held in enumerate(PAIRS)]
    total = sum(widths)
    portion = mix_weight.shape[0]
    kept, given = pl.pallas_call(
        functools.partial(sort_kernel, inner),
        in_specs=[SMEM, VMEM, VMEM],
        out_specs=[VMEM] * 2,
        out_shape=[jax.ShapeDtypeStruct((portion, total), BF16)] * 2,
        compiler_params=params(8),
        cost_estimate=LIGHT,
        name="sort",
    )(place, mix_weight, step_weight)
    got = swapped(given, (1, 1))
    blocks = pl.pallas_call(
        stack_kernel,
        in_specs=[SMEM, VMEM, VMEM],
        out_specs=[VMEM] * len(widths),
        out_shape=[jax.ShapeDtypeStruct((2 * portion, width), BF16) for width in widths],
        compiler_params=params(8),
        cost_estimate=LIGHT,
        name="stack",
    )(place, kept, got)
    blocks = list(blocks)
    arrived = [None] * len(widths)

    chip_rows = 2 * span
    groups = chip_rows // GROUP

    def scratch(width, spans):
        return [
            pltpu.VMEM((depth, width), BF16),
            pltpu.VMEM((spans, chip_rows + 8, LANES), F32),
        ]

    extra = len(PAIRS[0])

    def projected(ints, own, other, low, high, taps, rates):
        width = widths[0]
        return pl.pallas_call(
            first_kernel,
            in_specs=[SMEM] + [VMEM] * 6,
            out_specs=[VMEM] * 5,
            scratch_shapes=scratch(width, 1 + extra) + [pltpu.VMEM((chip_rows, LANES), F32)],
            out_shape=[
                jax.ShapeDtypeStruct((chip_rows, LANES), BF16),
                jax.ShapeDtypeStruct((chip_rows, extra * LANES), BF16),
                jax.ShapeDtypeStruct((chip_rows, LANES), F32),
                jax.ShapeDtypeStruct((groups, 32, GROUP), F32),
                jax.ShapeDtypeStruct((8, LANES), F32),
            ],
            compiler_params=params(28),
            cost_estimate=LIGHT,
            name="first",
        )(ints, own, other, low, high, taps, rates)

    def scanned(index, ints, own, other, low, high, taps, skip, x0, mine, theirs, table, kt, tot, *earlier):
        more = extra if index == 1 else 0
        held = (PAIRS[0] if more else ()) + PAIRS[index]
        pairs = len(held)
        new = pairs - more
        firsts = [first_head(p, share) for p in held]
        width = widths[index]
        return pl.pallas_call(
            functools.partial(scan_kernel, index, held, firsts, more),
            in_specs=[SMEM] + [VMEM] * (12 + len(earlier)),
            out_specs=[VMEM] * 3,
            scratch_shapes=scratch(width, new) + [pltpu.VMEM((LANES, pairs * LANES), F32)],
            out_shape=[
                jax.ShapeDtypeStruct((chip_rows, pairs * LANES), F32),
                jax.ShapeDtypeStruct((LANES, pairs * LANES), F32),
                jax.ShapeDtypeStruct(
                    (LANES + 16, pairs * LANES + sum(a.shape[1] for a in earlier)), BF16
                ),
            ],
            compiler_params=params(28),
            cost_estimate=LIGHT,
            name="scan",
        )(
            ints, own, other, low, high, taps,
            x0, mine, theirs, table, kt, tot, skip, *earlier,
        )

    def joined(held, ints, mine, theirs, table, tot, ys, ss, r):
        pairs = len(held)
        halves = [(i, i + 1) for i in range(0, pairs, 2)]
        sizes = [y.shape[1] // LANES for y in ys]
        return pl.pallas_call(
            functools.partial(join_kernel, [first_head(p, share) for p in held], sizes, halves),
            in_specs=[SMEM] + [VMEM] * (5 + 2 * len(ys)),
            out_specs=[VMEM] * 3,
            out_shape=[
                jax.ShapeDtypeStruct((span, pairs * LANES), F32),
                jax.ShapeDtypeStruct((span, pairs * LANES), F32),
                jax.ShapeDtypeStruct((len(halves) * LANES, nstate), BF16),
            ],
            compiler_params=params(28),
            cost_estimate=LIGHT,
            name="join",
        )(ints, mine, theirs, table, tot, r, *ys, *ss)

    early_pairs, late_pairs = sum(PAIRS[:CUT], ()), sum(PAIRS[CUT:], ())

    def normed(ints, keep_a, keep_b, got_a, got_b):
        places = [
            [(p % 2) * (2 * quarter // LANES) + p // 2 for p in held]
            for held in (early_pairs, late_pairs)
        ]
        block = span // 2
        return pl.pallas_call(
            functools.partial(norm_kernel, places),
            grid_spec=pltpu.PrefetchScalarGridSpec(
                num_scalar_prefetch=1,
                grid=(span // block,),
                in_specs=[pl.BlockSpec((1, inner), lambda i, ints: (0, 0))]
                + [
                    pl.BlockSpec((block, a.shape[1]), lambda i, ints: (i, 0))
                    for a in (keep_a, keep_b, got_a, got_b)
                ],
                out_specs=pl.BlockSpec((block, inner), lambda i, ints: (i, 0)),
            ),
            out_shape=jax.ShapeDtypeStruct((span, inner), BF16),
            compiler_params=params(28),
            cost_estimate=LIGHT,
            name="norm",
        )(ints, norm_gain[None], keep_a, keep_b, got_a, got_b)

    def picked(kernel, kind, *arrays, more=0):
        return pl.pallas_call(
            kernel,
            in_specs=[SMEM] * 2 + [VMEM] * len(arrays),
            out_specs=VMEM,
            out_shape=jax.ShapeDtypeStruct((arrays[0].shape[0] + more, nstate), kind),
            compiler_params=params(8),
            cost_estimate=LIGHT,
            name="pick",
        )(place, v["ints"], *arrays)

    v = state
    v["token"] = blocks[0]
    last = len(PAIRS) - 1
    for event in SCHEDULE:
        if event[0].isdigit():
            i, step = (int(part) for part in event.split("."))
            if step:
                blocks[i] = jnp.concatenate(after(blocks[i], arrived[i]), axis=0)
                v["token"] = blocks[i]
            route = ROUTES[i]
            arrived[i] = swapped(blocks[i], (FLIPS[route[0][step]], FLIPS[route[1][step]]))
        elif event == "tokens":
            given_rows, _ = lax.optimization_barrier((rows, blocks[0]))
            v["other"] = swapped(given_rows, (1, 1))
        elif event == "halo":
            other = after(v["other"])
            edge = jnp.where(core == 1, rows[span - HALO :], other[span - HALO :])
            count = lax.axis_size("req") * lax.axis_size("seq")
            route = [(i, i + 2) for i in range(count) if (i // 2) % 2 == 0]
            v["token"] = edge
            v["halo"] = lax.ppermute(edge, AXES, route)
        elif event == "settings":
            half = inner // 2

            conv_w, conv_b, step_b, rate, gain = after(
                conv_weight, conv_bias, step_bias, decay_rate, skip_gain
            )

            def row(values):
                return jnp.pad(values, (0, conv_weight.shape[1] - values.shape[0]))[None]

            small = jnp.concatenate(
                [conv_w, conv_b[None], jnp.zeros((3, conv_w.shape[1]), F32)]
                + [row(step_b), row(rate * (-LOG2E)), row(gain)]
                + [jnp.zeros((5, conv_weight.shape[1]), F32)],
                axis=0,
            )
            v["ints"], v["taps"], v["rates"], v["skip"] = pl.pallas_call(
                functools.partial(settings_kernel, inner),
                in_specs=[SMEM] * 4 + [VMEM],
                out_specs=[SMEM] + [VMEM] * 3,
                out_shape=[
                    jax.ShapeDtypeStruct((8,), jnp.int32),
                    jax.ShapeDtypeStruct((8, half + LANES), F32),
                    jax.ShapeDtypeStruct((8, LANES), F32),
                    jax.ShapeDtypeStruct((8, half), F32),
                ],
                compiler_params=params(8),
                cost_estimate=LIGHT,
                name="settings",
            )(after(place), deal, prompt_len, prompt_start, small)
            v["token"] = v["rates"]
        elif event == "own":
            v["own"] = jnp.concatenate([after(v["halo"]), rows], axis=0)
            v["token"] = v["own"]
        elif event == "K0":
            ints = after(v["ints"])
            bc, x0, table, kt, tot = projected(
                ints, v["own"], v["other"], blocks[0], arrived[0], v["taps"], v["rates"]
            )
            v["token"] = tot
            v["bc"] = swapped(bc, (1, 1))
        elif event[0] == "K":
            i = int(event[1:])
            if i == 1:
                theirs = after(v["bc"])
            ints = after(v["ints"])
            v["y", i], v["s", i], v["t", i] = scanned(
                i, ints, v["own"], v["other"], blocks[i], arrived[i], v["taps"], v["skip"],
                x0, bc, theirs, table, kt, tot, *([v["t", i - 1]] if i > 1 and i != CUT else []),
            )
            v["token"] = v["t", i]
        elif event in ("xA", "xB"):
            v["r", event[1]] = swapped(v["t", CUT - 1 if event == "xA" else last], (2, 2))
        elif event in ("JA", "JB"):
            which = range(1, CUT) if event == "JA" else range(CUT, last + 1)
            held = early_pairs if event == "JA" else late_pairs
            ints, r = after(v["ints"], v["r", event[1]])
            send, v["keep", event[1]], v["fin", event[1]] = joined(
                held, ints, bc, theirs, table, tot, [v["y", i] for i in which], [v["s", i] for i in which], r
            )
            v["token"] = v["fin", event[1]]
            v["got", event[1]] = swapped(send, (1, 1))
        elif event[0] == "f":
            key = event[1]
            if event[2] == "0":
                v["one", key] = swapped(v["fin", key], (16, 16))
            elif event[2] == "1":
                v["pair", key] = jnp.stack(after(v["fin", key], v["one", key]))
                v["token"] = v["pair", key]
                v["two", key] = swapped(v["pair", key], (8, 8))
            elif event[2] == "2":
                cand = (v["fin", key], v["one", key], after(v["two", key]))
                v["cand", key] = cand
                v["picked", key] = picked(pick_kernel, BF16, *cand)
                v["token"] = v["picked", key]
                v["three", key] = swapped(v["picked", key], (4, 4))
            else:
                three = after(v["three", key])
                earlier = [v["final", "A"]] if key == "B" else []
                more = sum(a.shape[0] for a in earlier)
                v["final", key] = picked(
                    last_kernel, F32, *v["cand", key], three, *earlier, more=more
                )
                v["token"] = v["final", key]
        else:
            ints = after(v["ints"])
            result = normed(ints, v["keep", "A"], v["keep", "B"], v["got", "A"], v["got", "B"])
            v["token"] = result
    return (result[None], v["final", "B"].reshape(1, share, head_dim, nstate))


def passed_along(block, axis, distance):
    devices = range(lax.axis_size(axis))
    route = [(i - distance, i) for i in devices if i - distance in devices]
    return lax.ppermute(block, axis, route)


def carried_in(part, axis, combine, identity):
    place = lax.axis_index(axis)
    gathered = jax.tree.map(lambda a: lax.all_gather(a, axis), part)
    state = jax.tree.map(lambda a, e: jnp.zeros_like(a) + jnp.asarray(e, a.dtype), part, identity)

    def one(step, state):
        return combine(
            state, jax.tree.map(lambda a: lax.dynamic_index_in_dim(a, step, 0, False), gathered)
        )

    return lax.fori_loop(0, place, one, state)


def broadcast(x, axis, root):
    mine = lax.axis_index(axis) == root
    return lax.psum(jnp.where(mine, x, jnp.zeros_like(x)), axis)


def on_device_general(
    tokens,
    mix_weight,
    step_weight,
    conv_weight,
    conv_bias,
    step_bias,
    decay_rate,
    skip_gain,
    norm_gain,
    prompt_len,
    prompt_start,
    deal,
):
    seq_count = lax.axis_size("seq")
    seq_index = lax.axis_index("seq")
    req_index = lax.axis_index("req")
    rows = tokens[0]
    span = rows.shape[0]
    total_reqs = deal.shape[0]
    slots = jnp.arange(total_reqs, dtype=jnp.int32)
    request = jnp.sum(jnp.where(slots == req_index, deal, 0))
    length = jnp.sum(jnp.where(slots == request, prompt_len, 0))
    start = jnp.sum(jnp.where(slots == request, prompt_start, 0))
    place = seq_index * span + jnp.arange(span, dtype=jnp.int32)
    valid = ((place >= start) & (place < start + length)).astype(jnp.float32)
    whole_mix, whole_step = (
        lax.all_gather(mix_weight, ("req", "seq"), axis=0, tiled=True),
        lax.all_gather(step_weight, ("req", "seq"), axis=0, tiled=True),
    )
    mixed = jnp.dot(rows, whole_mix, preferred_element_type=jnp.float32)
    raw_step = jnp.dot(rows, whole_step, preferred_element_type=jnp.float32)
    mixed = (mixed * valid[:, None]).astype(jnp.bfloat16)
    taps = conv_weight.shape[0]
    edge = passed_along(mixed[span - (taps - 1) :], "seq", 1)
    padded = jnp.concatenate([edge, mixed], axis=0)
    conv_sum = jnp.zeros(mixed.shape, jnp.float32) + conv_bias[None, :]
    for offset in range(taps):
        conv_sum = conv_sum + conv_weight[offset][None, :] * padded[offset : offset + span].astype(
            jnp.float32
        )
    convolved = jax.nn.silu(conv_sum).astype(jnp.bfloat16)
    heads = decay_rate.shape[0]
    inner = norm_gain.shape[0]
    head_dim = inner // heads
    nstate = (mixed.shape[1] - inner) // 2
    blocks = span // GROUP
    inputs = convolved[:, :inner].reshape(span, heads, head_dim)
    mixed_b = convolved[:, inner : inner + nstate]
    mixed_c = convolved[:, inner + nstate :]
    step_size = jax.nn.softplus(raw_step + step_bias[None, :]) * valid[:, None]
    pieces = (
        inputs.reshape(blocks, GROUP, heads, head_dim),
        mixed_b.reshape(blocks, GROUP, nstate),
        mixed_c.reshape(blocks, GROUP, nstate),
        step_size.reshape(blocks, GROUP, heads),
    )

    def local_group(block):
        part_in, part_b, part_c, part_step = block
        cum_decay = jnp.cumsum(-part_step * decay_rate[None, :], axis=0)
        places = jnp.arange(GROUP, dtype=jnp.int32)
        causal = places[:, None] >= places[None, :]
        spread = cum_decay[:, None, :] - cum_decay[None, :, :]
        spread = jnp.where(causal[:, :, None], spread, -1e30)
        scores = jnp.einsum("qn,kn->qk", part_c, part_b, preferred_element_type=jnp.float32)
        mixing = (jnp.exp(spread) * scores[:, :, None] * part_step[None, :, :]).astype(jnp.bfloat16)
        inner_out = jnp.einsum("qkh,khp->qhp", mixing, part_in, preferred_element_type=jnp.float32)
        to_end = jnp.exp(cum_decay[-1][None, :] - cum_decay) * part_step
        scaled = (to_end[:, :, None] * part_in.astype(jnp.float32)).astype(jnp.bfloat16)
        local = jnp.einsum("khp,kn->hpn", scaled, part_b, preferred_element_type=jnp.float32)
        return (inner_out, cum_decay, local)

    inner_out, cum_decay, group_state = lax.map(local_group, pieces)
    totals = cum_decay[:, -1, :]

    def advance(carry, item):
        group_total, group_local = item
        return (jnp.exp(group_total)[:, None, None] * carry + group_local, carry)

    dev_state, entry_zero = lax.scan(
        advance, jnp.zeros((heads, head_dim, nstate), jnp.float32), (totals, group_state)
    )
    before = jnp.cumsum(totals, axis=0) - totals
    dev_decay = jnp.exp(jnp.sum(totals, axis=0))

    def chain(earlier, later):
        return (earlier[0] * later[0], later[0][:, None, None] * earlier[1] + later[1])

    incoming_decay, incoming = carried_in(
        (dev_decay, dev_state), "seq", chain, (jnp.ones_like(dev_decay), jnp.zeros_like(dev_state))
    )
    entry = entry_zero + jnp.exp(before)[:, :, None, None] * incoming[None]
    carried = jnp.einsum(
        "cqn,chpn->cqhp", pieces[2].astype(jnp.float32), entry, precision=lax.Precision.HIGHEST
    )
    carried = carried * jnp.exp(cum_decay)[:, :, :, None]
    outputs = (inner_out + carried).reshape(span, heads, head_dim) + skip_gain[
        None, :, None
    ] * inputs.astype(jnp.float32)
    flat = outputs.reshape(span, inner)
    factor = lax.rsqrt(jnp.mean(flat * flat, axis=1, keepdims=True) + EPS)
    result = (flat * factor * norm_gain[None, :] * valid[:, None]).astype(jnp.bfloat16)[None]
    share = heads // seq_count
    leaving = dev_decay[:, None, None] * incoming + dev_state
    last_state = broadcast(leaving, "seq", seq_count - 1)
    own_state = lax.dynamic_slice_in_dim(last_state, seq_index * share, share, 0)[None]
    wanted = jnp.sum(jnp.where(deal == req_index, slots, 0))
    piece = lax.all_gather(own_state, "req", axis=0, tiled=True)
    count = piece.shape[0]
    chosen = jnp.arange(count, dtype=jnp.int32) == wanted
    final_state = jnp.zeros_like(own_state) + jnp.sum(
        jnp.where(chosen[:, None, None, None], piece, 0.0), axis=0, keepdims=True
    )
    return (result, final_state)


def solution(mesh):
    fits = mesh.shape["req"] == 8 and mesh.shape["seq"] == 4
    return jax.shard_map(
        on_device if fits else on_device_general,
        mesh=mesh,
        in_specs=(
            P("req", "seq", None),
            P(("req", "seq"), None),
            P(("req", "seq"), None),
        )
        + (P(),) * 9,
        out_specs=(P("req", "seq", None), P("req", "seq", None, None)),
        check_vma=False,
    )
```
